32 devices in a mesh: dp: 16 (over z, x, core), seq: 2 (over y).
Axes of the slice: x: 2, y: 2, z: 4, core: 2. Of those that a mesh axis runs over, the one named last changes fastest.
Arguments:
- grad_out: bfloat16 [16, 256, 6144], P('dp', 'seq'), may hold values from -6 to 6
- queries: bfloat16 [16, 256, 3072], P('dp', 'seq'), may hold values from -40 to 40
- keys: bfloat16 [16, 256, 3072], P('dp', 'seq'), may hold values from -12 to 12
- values: bfloat16 [16, 256, 3072], P('dp', 'seq'), may hold values from -6 to 6
- out_weight: bfloat16 [6144, 3072], P('dp', 'seq'), may hold values from -0.109375 to 0.109375
Outputs:
- query_grad: bfloat16 [16, 256, 3072], P('dp', 'seq')
- key_grad: bfloat16 [16, 256, 3072], P('dp', 'seq')
- value_grad: bfloat16 [16, 256, 3072], P('dp', 'seq')
- weight_grad: float32 [6144, 3072], P('dp', 'seq')
The draws below stay inside these ranges and needn't reach their ends.
All inputs are finite; a program needn't handle non-finite values.
Results may differ from the reference program's by a relative error of at most 0.03.
Values may be sent and summed in bfloat16 or wider, within the bound.
No kernel may reach another device: no remote copies, remote signals or barrier semaphores. Data moves between devices by JAX's collectives and lax.ppermute only.
A program may use at most 128 MiB of HBM per device.

```python
import math
import jax
import jax.numpy as jnp
from jax import lax

D = 6144
HEADS = 24
HEAD_DIM = 128
LEN = 256
BATCH = 16


def query_key_pair(key):
    base = jax.random.fold_in(key, 31)
    first, second = jax.random.split(base, 2)
    array_shape = (BATCH, LEN, HEADS * HEAD_DIM)
    key_rows = jax.random.truncated_normal(first, -4.0, 4.0, array_shape, jnp.float32)
    query_rows = 2.5 * jax.random.truncated_normal(second, -4.0, 4.0, array_shape, jnp.float32)
    return (query_rows, key_rows)


def draw_queries(key, part):
    return query_key_pair(key)[0].astype(jnp.bfloat16)


def draw_keys(key, part):
    return query_key_pair(key)[1].astype(jnp.bfloat16)


def spiked(array, key, source, target, shards_of, factor):
    def block_of(axis_at):
        return (jnp.arange(array.shape[axis_at]) // (array.shape[axis_at] // shards_of)).reshape((-1,) + (1,) * (array.ndim - 1 - axis_at))

    near = jax.random.permutation(key, shards_of)[block_of(target)]
    second = (block_of(target) + shards_of // 2) % shards_of
    return jnp.where((block_of(source) == near) | (block_of(source) == second), factor * array, array)


def shard_levels(own_key, shape, cuts, low, top_value):
    factor_of, own = 1.0, jax.random.fold_in(own_key, 6)
    for axis_at, parts in cuts:
        draws = jnp.exp(jax.random.uniform(jax.random.fold_in(own, axis_at), (parts,), jnp.float32, low / len(cuts), top_value / len(cuts)))
        factor_of = factor_of * jnp.repeat(draws, shape[axis_at] // parts).reshape([-1 if axis == axis_at else 1 for axis in range(len(shape))])
    return factor_of


def gaussian(own_key, dims, scale, bound, cuts=(), dtype=jnp.bfloat16):
    values = scale * jax.random.normal(own_key, dims, jnp.float32)
    if cuts:
        values = values * shard_levels(own_key, dims, cuts, -0.22, 0.18)
    return jnp.clip(values, -bound, bound).astype(dtype)


def bell_draw_with(own_key, shape, scale, limit, pieces, heavy, dtype=jnp.bfloat16):
    entries = scale * jax.random.normal(own_key, shape, jnp.float32)
    if pieces:
        entries = entries * shard_levels(own_key, shape, pieces, -0.22, 0.18)
    return jnp.clip(spiked(entries, jax.random.fold_in(own_key, 3), *heavy), -limit, limit).astype(dtype)


def setup_inputs(seed: int = 0) -> dict:
    arg_keys = jax.random.split(jax.random.key(seed), 6)
    return {
        "grad_out": bell_draw_with(arg_keys[0], (BATCH, LEN, D), 1.0, 6.0, ((0, 16), (1, 2)), (0, 2, 16, 2.0)),
        "queries": draw_queries(jax.random.fold_in(arg_keys[5], 71), 0),
        "keys": draw_keys(jax.random.fold_in(arg_keys[5], 71), 0),
        "values": gaussian(arg_keys[3], (BATCH, LEN, HEADS * HEAD_DIM), 1.0, 6.0, ((0, 16), (1, 2))),
        "out_weight": gaussian(arg_keys[4], (D, HEADS * HEAD_DIM), (HEADS * HEAD_DIM) ** -0.5, 0.109375, ((0, 16), (1, 2))),
    }


def sequence_grads(grad_rows, query_rows, key_rows, value_rows, out_weight):
    d_attn = jnp.dot(grad_rows, out_weight, preferred_element_type=jnp.float32).astype(jnp.bfloat16)
    head_shape = (LEN, HEADS, HEAD_DIM)
    query_heads = query_rows.reshape(head_shape).astype(jnp.float32)
    key_heads = key_rows.reshape(head_shape).astype(jnp.float32)
    value_heads = value_rows.reshape(head_shape).astype(jnp.float32)
    grad_heads = d_attn.reshape(head_shape).astype(jnp.float32)
    inverse_root = 1.0 / math.sqrt(HEAD_DIM)
    scores = jnp.einsum('qhd,khd->hqk', query_heads, key_heads) * inverse_root
    largest = lax.optimization_barrier(jnp.max(scores, axis=-1, keepdims=True))
    raised = jnp.exp(scores - largest)
    probabilities = raised / lax.optimization_barrier(jnp.sum(raised, axis=-1, keepdims=True))
    probs_low = probabilities.astype(jnp.bfloat16).astype(jnp.float32)
    attended = jnp.einsum('hqk,khd->qhd', probs_low, value_heads).astype(jnp.bfloat16)
    row_delta = lax.optimization_barrier(jnp.sum(grad_heads * attended.astype(jnp.float32), axis=-1))
    d_probs = jnp.einsum('qhd,khd->hqk', grad_heads, value_heads)
    d_scores = probabilities * (d_probs - jnp.transpose(row_delta)[:, :, None])
    scores_low = d_scores.astype(jnp.bfloat16).astype(jnp.float32)
    value_grad = jnp.einsum('hqk,qhd->khd', probs_low, grad_heads).astype(jnp.bfloat16)
    query_grad = (jnp.einsum('hqk,khd->qhd', scores_low, key_heads) * inverse_root).astype(jnp.bfloat16)
    key_grad = (jnp.einsum('hqk,qhd->khd', scores_low, query_heads) * inverse_root).astype(jnp.bfloat16)
    features = HEADS * HEAD_DIM
    return (query_grad.reshape(LEN, features), key_grad.reshape(LEN, features), value_grad.reshape(LEN, features), attended.reshape(LEN, features))

def reference(grad_out, queries, keys, values, out_weight):

    def per_sequence(inputs):
        return sequence_grads(inputs[0], inputs[1], inputs[2], inputs[3], out_weight)
    query_grad, key_grad, value_grad, attended = lax.map(per_sequence, (grad_out, queries, keys, values))
    flat_grad = grad_out.reshape(BATCH * LEN, D)
    flat_attended = attended.reshape(BATCH * LEN, HEADS * HEAD_DIM)
    weight_grad = jnp.dot(flat_grad.T, flat_attended, preferred_element_type=jnp.float32) / math.sqrt(BATCH * LEN)
    return (query_grad, key_grad, value_grad, weight_grad)
```

```python
import functools
import math

import jax
import jax.numpy as jnp
from jax import lax
from jax.experimental import pallas as pl
from jax.experimental.pallas import tpu as pltpu
from jax.sharding import PartitionSpec as P

HEAD_DIM = 128


def dot(a, b, contract):
    return lax.dot_general(a, b, (contract, ((), ())), preferred_element_type=jnp.float32)


def attention_kernel(
    heads,
    mine_ref,
    q_own,
    q_far,
    k_own,
    k_far,
    v_own,
    v_far,
    grad_ref,
    dq_own,
    dq_far,
    dk_own,
    dk_far,
    dv_own,
    dv_far,
    att_ref,
):
    inverse_root = 1.0 / math.sqrt(HEAD_DIM)
    tokens = q_own.shape[0]
    for head in range(heads):
        at = slice(head * HEAD_DIM, (head + 1) * HEAD_DIM)
        q = jnp.concatenate([q_own[:, at], q_far[:, at]], axis=0)
        k = jnp.concatenate([k_own[:, at], k_far[:, at]], axis=0)
        v = jnp.concatenate([v_own[:, at], v_far[:, at]], axis=0)
        g = grad_ref[:, at]
        scores = dot(q, k, ((1,), (1,))) * inverse_root
        raised = jnp.exp(scores - jnp.max(scores, axis=-1, keepdims=True))
        probs = raised * (1.0 / jnp.sum(raised, axis=-1, keepdims=True))
        low = probs.astype(jnp.bfloat16)
        att = dot(low, v, ((1,), (0,))).astype(jnp.bfloat16)
        att_ref[:, at] = att
        delta = jnp.sum(
            g.astype(jnp.float32) * att.astype(jnp.float32), axis=-1, keepdims=True
        )
        d_probs = dot(g, v, ((1,), (1,)))
        d_low = (probs * (d_probs - delta)).astype(jnp.bfloat16)
        dq = (dot(d_low, k, ((1,), (0,))) * inverse_root).astype(jnp.bfloat16)
        dk = (dot(d_low, q, ((0,), (0,))) * inverse_root).astype(jnp.bfloat16)
        dv = dot(low, g, ((0,), (0,))).astype(jnp.bfloat16)
        for own, far, value in ((dq_own, dq_far, dq), (dk_own, dk_far, dk), (dv_own, dv_far, dv)):
            own[:, at] = value[:tokens]
            far[:, at] = value[tokens:]


def attention(mine, own, far, grad):
    tokens, width = own[0].shape
    features = far[0].shape[1]
    heads = features // HEAD_DIM
    length = grad.shape[0]
    step = 2 if heads % 2 == 0 and length <= 512 else 1
    grid = heads // step
    block = step * HEAD_DIM
    own_spec = pl.BlockSpec((tokens, block), lambda h, mine: (0, mine[0] * grid + h))
    far_spec = pl.BlockSpec((length - tokens, block), lambda h, mine: (0, h))
    all_spec = pl.BlockSpec((length, block), lambda h, mine: (0, h))
    shape = lambda rows, columns: jax.ShapeDtypeStruct((rows, columns), jnp.bfloat16)
    outs = [shape(tokens, width), shape(length - tokens, features)] * 3 + [shape(length, features)]
    return pl.pallas_call(
        functools.partial(attention_kernel, step),
        grid_spec=pltpu.PrefetchScalarGridSpec(
            num_scalar_prefetch=1,
            grid=(grid,),
            in_specs=[own_spec, far_spec] * 3 + [all_spec],
            out_specs=[own_spec, far_spec] * 3 + [all_spec],
        ),
        out_shape=outs,
        compiler_params=pltpu.CompilerParams(vmem_limit_bytes=48 * 1024 * 1024),
        cost_estimate=pl.CostEstimate(
            flops=12 * heads * length * length * HEAD_DIM,
            bytes_accessed=16 * length * features,
            transcendentals=heads * length * length,
        ),
        name="attention",
    )(mine, own[0], far[0], own[1], far[1], own[2], far[2], grad)


def shards(grad_out, queries, keys, values, out_weight):
    dp = lax.axis_size("dp")
    seq = lax.axis_size("seq")
    mine = lax.axis_index("seq")
    tokens, width = grad_out.shape[1:]
    features = out_weight.shape[1]
    length = tokens * seq
    rows = out_weight.shape[0]
    token_scale = 1.0 / math.sqrt(dp * length)

    def shift(array, by):
        return lax.ppermute(array, "seq", [(i, (i + by) % seq) for i in range(seq)])

    whole_rows = lax.all_gather(out_weight, "dp", axis=0, tiled=True)

    own_grad = grad_out[0]
    own = (queries[0], keys[0], values[0])
    pieces = []
    for by in range(1, seq):
        start = ((mine + by) % seq) * features
        pieces.append(
            shift(
                jnp.stack([lax.dynamic_slice_in_dim(part, start, features, 1) for part in own]), by
            )
        )
    arrived = pieces[0] if seq == 2 else jnp.concatenate(pieces, axis=1)
    far = (arrived[0], arrived[1], arrived[2])
    all_grad = jnp.concatenate([own_grad] + [shift(own_grad, by) for by in range(1, seq)], axis=0)

    by_rows = jnp.transpose(own_grad.reshape(tokens, dp, rows), (1, 0, 2))
    by_rows = lax.all_to_all(by_rows, "dp", split_axis=0, concat_axis=0, tiled=True)
    row_grad = jnp.concatenate([by_rows] + [shift(by_rows, by) for by in range(1, seq)], axis=1)
    row_grad = row_grad.reshape(dp * length, rows)

    d_attn = jnp.dot(all_grad, whole_rows, preferred_element_type=jnp.float32).astype(jnp.bfloat16)
    dq, dq_far, dk, dk_far, dv, dv_far, attended = attention(
        mine.astype(jnp.int32).reshape(1), own, far, d_attn
    )
    every = lax.all_gather(attended, "dp", axis=0, tiled=True)
    weight_grad = dot(row_grad, every, ((0,), (0,))) * token_scale

    leaving = jnp.stack([dq_far, dk_far, dv_far])
    result = [dq, dk, dv]
    for by in range(1, seq):
        back = shift(leaving[:, (by - 1) * tokens : by * tokens], seq - by)
        start = ((mine + by) % seq) * features
        result = [
            lax.dynamic_update_slice_in_dim(whole, back[i], start, 1)
            for i, whole in enumerate(result)
        ]
    return (result[0][None], result[1][None], result[2][None], weight_grad)


def solution(mesh):
    in_specs = (
        P("dp", "seq", None),
        P("dp", "seq", None),
        P("dp", "seq", None),
        P("dp", "seq", None),
        P("dp", "seq"),
    )
    out_specs = (P("dp", "seq", None), P("dp", "seq", None), P("dp", "seq", None), P("dp", "seq"))
    return jax.shard_map(shards, mesh=mesh, in_specs=in_specs, out_specs=out_specs, check_vma=False)
```

```python
import functools
import math

import jax
import jax.numpy as jnp
from jax import lax
from jax.experimental import pallas as pl
from jax.experimental.pallas import tpu as pltpu
from jax.sharding import Mesh
from jax.sharding import PartitionSpec as P

HEAD_DIM = 128
INVERSE_ROOT = 1.0 / math.sqrt(HEAD_DIM)
DP = ("zh", "zl", "x", "core")


def dot(a, b, contract):
    return lax.dot_general(a, b, (contract, ((), ())), preferred_element_type=jnp.float32)


def shift(array, axis, by):
    count = lax.axis_size(axis)
    return lax.ppermute(array, axis, [(i, (i + by) % count) for i in range(count)])


def others(axis):
    return range(1, lax.axis_size(axis))


def part_of(array, axis, by, dim):
    count = lax.axis_size(axis)
    size = array.shape[dim] // count
    at = (lax.axis_index(axis) + by) % count
    return lax.dynamic_slice_in_dim(array, at * size, size, dim)


def softmax(q, k):
    scores = dot(q, k, ((1,), (1,))) * INVERSE_ROOT
    raised = jnp.exp(scores - jnp.max(scores, axis=-1, keepdims=True))
    return raised * (1.0 / jnp.sum(raised, axis=-1, keepdims=True))


def both(own, far, at):
    return jnp.concatenate([own[:, at], far[:, at]], axis=0)


def forward_kernel(heads, mine_ref, q_own, k_own, v_own, far, att_ref):
    for head in range(heads):
        at = slice(head * HEAD_DIM, (head + 1) * HEAD_DIM)
        q, k, v = (both(own, far.at[i], at) for i, own in enumerate((q_own, k_own, v_own)))
        low = softmax(q, k).astype(jnp.bfloat16)
        att_ref[:, at] = dot(low, v, ((1,), (0,))).astype(jnp.bfloat16)


def backward_kernel(heads, held, terms, mine_ref, q_own, k_own, v_own, far, *refs):
    grad_refs, refs = refs[:terms], refs[terms + held :]
    dq_own, dk_own, dv_own, leaving = refs
    tokens = q_own.shape[0]
    for head in range(heads):
        at = slice(head * HEAD_DIM, (head + 1) * HEAD_DIM)
        q, k, v = (both(own, far.at[i], at) for i, own in enumerate((q_own, k_own, v_own)))
        total = grad_refs[0][:, at].astype(jnp.float32)
        for ref in grad_refs[1:]:
            total = total + ref[:, at].astype(jnp.float32)
        g = total.astype(jnp.bfloat16)
        probs = softmax(q, k)
        low = probs.astype(jnp.bfloat16)
        att = dot(low, v, ((1,), (0,))).astype(jnp.bfloat16)
        delta = jnp.sum(
            g.astype(jnp.float32) * att.astype(jnp.float32), axis=-1, keepdims=True
        )
        d_probs = dot(g, v, ((1,), (1,)))
        d_low = (probs * (d_probs - delta)).astype(jnp.bfloat16)
        dq = (dot(d_low, k, ((1,), (0,))) * INVERSE_ROOT).astype(jnp.bfloat16)
        dk = (dot(d_low, q, ((0,), (0,))) * INVERSE_ROOT).astype(jnp.bfloat16)
        dv = dot(low, g, ((0,), (0,))).astype(jnp.bfloat16)
        for i, (own, value) in enumerate(((dq_own, dq), (dk_own, dk), (dv_own, dv))):
            own[:, at] = value[:tokens]
            leaving[i, :, at] = value[tokens:]


def heads_a_step(heads, length):
    return 2 if heads % 2 == 0 and length <= 512 else 1


def params():
    return pltpu.CompilerParams(vmem_limit_bytes=48 * 1024 * 1024)


def cost(dots, heads, length, arrays):
    return pl.CostEstimate(
        flops=2 * dots * heads * length * length * HEAD_DIM,
        bytes_accessed=2 * arrays * length * heads * HEAD_DIM,
        transcendentals=heads * length * length,
    )


def forward(mine, own, far):
    tokens = own[0].shape[0]
    _, rest, features = far.shape
    length = tokens + rest
    heads = features // HEAD_DIM
    step = heads_a_step(heads, length)
    grid = heads // step
    block = step * HEAD_DIM
    own_spec = pl.BlockSpec((tokens, block), lambda h, mine: (0, mine[0] * grid + h))
    far_spec = pl.BlockSpec((3, rest, block), lambda h, mine: (0, 0, h))
    return pl.pallas_call(
        functools.partial(forward_kernel, step),
        grid_spec=pltpu.PrefetchScalarGridSpec(
            num_scalar_prefetch=1,
            grid=(grid,),
            in_specs=[own_spec] * 3 + [far_spec],
            out_specs=pl.BlockSpec((length, block), lambda h, mine: (0, h)),
        ),
        out_shape=jax.ShapeDtypeStruct((length, features), jnp.bfloat16),
        compiler_params=params(),
        cost_estimate=cost(2, heads, length, 4),
        name="forward",
    )(mine, *own, far)


def backward(mine, own, far, grads, first_head, heads, held):
    tokens, width = own[0].shape
    _, rest, features = far.shape
    length = tokens + rest
    step = heads_a_step(heads, length)
    grid = heads // step
    block = step * HEAD_DIM
    every = features // block
    start = first_head // step
    own_spec = pl.BlockSpec((tokens, block), lambda h, mine: (0, mine[0] * every + start + h))
    far_spec = pl.BlockSpec((3, rest, block), lambda h, mine: (0, 0, start + h))
    grad_spec = pl.BlockSpec((length, block), lambda h, mine: (0, h))
    any_spec = pl.BlockSpec(memory_space=pl.ANY)
    before = 5 + len(grads)
    return pl.pallas_call(
        functools.partial(backward_kernel, step, len(held), len(grads)),
        grid_spec=pltpu.PrefetchScalarGridSpec(
            num_scalar_prefetch=1,
            grid=(grid,),
            in_specs=[own_spec] * 3
            + [far_spec]
            + [grad_spec] * len(grads)
            + [any_spec] * len(held),
            out_specs=[own_spec] * 3
            + [pl.BlockSpec((3, rest, block), lambda h, mine: (0, 0, h))],
        ),
        out_shape=[jax.ShapeDtypeStruct((tokens, width), jnp.bfloat16)] * 3
        + [jax.ShapeDtypeStruct((3, rest, heads * HEAD_DIM), jnp.bfloat16)],
        input_output_aliases={before + i: i for i in range(len(held))},
        compiler_params=params(),
        cost_estimate=cost(6, heads, length, 9),
        name="backward",
    )(mine, *own, far, *grads, *held)


def summed_rows(grads, attended, first, second):
    tokens, _, _, rows = grads.shape
    inner = lax.axis_size(second)

    def product(by):
        chosen = part_of(grads, first, by, 1).reshape(tokens, inner * rows)
        return dot(chosen, attended, ((0,), (0,)))

    sent = [shift(product(by).astype(jnp.bfloat16), first, by) for by in others(first)]
    total = product(0)
    for term in sent:
        total = total + term.astype(jnp.float32)
    sent = [
        shift(part_of(total, second, by, 0).astype(jnp.bfloat16), second, by)
        for by in others(second)
    ]
    final = part_of(total, second, 0, 0)
    for term in sent:
        final = final + term.astype(jnp.float32)
    return final


def shards(grad_out, queries, keys, values, out_weight):
    seq = lax.axis_size("seq")
    mine = lax.axis_index("seq")
    tokens = grad_out.shape[1]
    rows, features = out_weight.shape
    length = tokens * seq
    heads = features // HEAD_DIM
    clips = math.prod(lax.axis_size(axis) for axis in DP)
    token_scale = 1.0 / math.sqrt(clips * length)
    me = mine.astype(jnp.int32).reshape(1)

    weight = lax.all_gather(out_weight, ("zl", "x", "core"), axis=0, tiled=True)

    own_grad = grad_out[0]
    halves = [part_of(own_grad, "zh", 0, 1)]
    halves += [shift(part_of(own_grad, "zh", by, 1), "zh", by) for by in others("zh")]

    own = (queries[0], keys[0], values[0])
    pieces = [
        shift(jnp.stack([part_of(part, "seq", by, 1) for part in own]), "seq", by)
        for by in others("seq")
    ]
    far = pieces[0] if seq == 2 else jnp.concatenate(pieces, axis=1)

    grads = [
        jnp.concatenate([half] + [shift(half, "seq", by) for by in others("seq")], axis=0)
        for half in halves
    ]

    attended = forward(me, own, far)
    attends = [attended] + [shift(attended, "zh", by) for by in others("zh")]

    groups = 2 if heads % 4 == 0 else 1
    wide = features // groups
    partial = []
    for group in range(groups):
        chosen = weight[:, group * wide : (group + 1) * wide]
        terms = [
            shift(dot(grads[by], chosen, ((1,), (0,))).astype(jnp.bfloat16), "zh", -by)
            for by in others("zh")
        ]
        partial.append([dot(grads[0], chosen, ((1,), (0,)))] + terms)

    every_grad, every_attended = [], []
    cores = lax.axis_size("core")
    stacked = jnp.concatenate(grads, axis=0)
    count = stacked.shape[0]
    stacked = stacked.reshape(count, -1, cores, rows)
    attends = jnp.concatenate(attends, axis=0)
    for by in range(cores):
        chosen = part_of(stacked, "core", by, 2)[:, :, 0]
        every_grad.append(shift(chosen, "core", by) if by else chosen)
        every_attended.append(shift(attends, "core", by) if by else attends)
    every_grad = jnp.concatenate(every_grad, axis=0)
    every_attended = jnp.concatenate(every_attended, axis=0)
    every_grad = every_grad.reshape(
        every_grad.shape[0], lax.axis_size("zl"), lax.axis_size("x"), rows
    )
    middle = features // 2
    left = summed_rows(
        jnp.swapaxes(every_grad, 1, 2), every_attended[:, :middle], "x", "zl"
    )
    right = summed_rows(every_grad, every_attended[:, middle:], "zl", "x")
    weight_grad = jnp.concatenate([left, right], axis=1) * token_scale

    result, arrivals = [], []
    for group in range(groups):
        first = group * wide // HEAD_DIM
        *result, leaving = backward(
            me, own, far, partial[group], first, wide // HEAD_DIM, result
        )
        arrivals.append(
            [
                shift(leaving[:, (by - 1) * tokens : by * tokens], "seq", -by)
                for by in others("seq")
            ]
        )
    for group in range(groups):
        for by, back in zip(others("seq"), arrivals[group]):
            start = ((mine + by) % seq) * features + group * wide
            result = [
                lax.dynamic_update_slice_in_dim(whole, back[i], start, 1)
                for i, whole in enumerate(result)
            ]
    return (result[0][None], result[1][None], result[2][None], weight_grad)


def solution(mesh):
    dp, seq = mesh.devices.shape
    finer = Mesh(mesh.devices.reshape(2, dp // 8, 2, 2, seq), DP + ("seq",))
    tokens = P(DP, "seq", None)
    return jax.shard_map(
        shards,
        mesh=finer,
        in_specs=(tokens, tokens, tokens, tokens, P(DP, "seq")),
        out_specs=(tokens, tokens, tokens, P(DP, "seq")),
        check_vma=False,
    )
```

```python
import functools
import math

import jax
import jax.numpy as jnp
from jax import lax
from jax.experimental import pallas as pl
from jax.experimental.pallas import tpu as pltpu
from jax.sharding import Mesh
from jax.sharding import PartitionSpec as P

HEAD_DIM = 128
INVERSE_ROOT = 1.0 / math.sqrt(HEAD_DIM)
DP = ("zh", "zl", "x", "core")


def dot(a, b, contract):
    return lax.dot_general(a, b, (contract, ((), ())), preferred_element_type=jnp.float32)


def shift(array, axis, by):
    count = lax.axis_size(axis)
    return lax.ppermute(array, axis, [(i, (i + by) % count) for i in range(count)])


def others(axis):
    return range(1, lax.axis_size(axis))


def part_of(array, axis, by, dim):
    count = lax.axis_size(axis)
    size = array.shape[dim] // count
    at = (lax.axis_index(axis) + by) % count
    return lax.dynamic_slice_in_dim(array, at * size, size, dim)


def softmax(q, k):
    scores = dot(q, k, ((1,), (1,))) * INVERSE_ROOT
    raised = jnp.exp(scores - jnp.max(scores, axis=-1, keepdims=True))
    return raised * (1.0 / jnp.sum(raised, axis=-1, keepdims=True))


def both(own, far, at):
    return jnp.concatenate([own[:, at], far[:, at]], axis=0)


def forward_kernel(heads, mine_ref, q_own, k_own, v_own, far, att_ref):
    for head in range(heads):
        at = slice(head * HEAD_DIM, (head + 1) * HEAD_DIM)
        q, k, v = (both(own, far.at[i], at) for i, own in enumerate((q_own, k_own, v_own)))
        low = softmax(q, k).astype(jnp.bfloat16)
        att_ref[:, at] = dot(low, v, ((1,), (0,))).astype(jnp.bfloat16)


def backward_kernel(heads, held, terms, mine_ref, q_own, k_own, v_own, far, *refs):
    grad_refs, refs = refs[:terms], refs[terms + held :]
    dq_own, dk_own, dv_own, leaving = refs
    tokens = q_own.shape[0]
    for head in range(heads):
        at = slice(head * HEAD_DIM, (head + 1) * HEAD_DIM)
        q, k, v = (both(own, far.at[i], at) for i, own in enumerate((q_own, k_own, v_own)))
        total = grad_refs[0][:, at].astype(jnp.float32)
        for ref in grad_refs[1:]:
            total = total + ref[:, at].astype(jnp.float32)
        g = total.astype(jnp.bfloat16)
        probs = softmax(q, k)
        low = probs.astype(jnp.bfloat16)
        att = dot(low, v, ((1,), (0,))).astype(jnp.bfloat16)
        delta = jnp.sum(
            g.astype(jnp.float32) * att.astype(jnp.float32), axis=-1, keepdims=True
        )
        d_probs = dot(g, v, ((1,), (1,)))
        d_low = (probs * (d_probs - delta)).astype(jnp.bfloat16)
        dq = (dot(d_low, k, ((1,), (0,))) * INVERSE_ROOT).astype(jnp.bfloat16)
        dk = (dot(d_low, q, ((0,), (0,))) * INVERSE_ROOT).astype(jnp.bfloat16)
        dv = dot(low, g, ((0,), (0,))).astype(jnp.bfloat16)
        for i, (own, value) in enumerate(((dq_own, dq), (dk_own, dk), (dv_own, dv))):
            own[:, at] = value[:tokens]
            leaving[i, :, at] = value[tokens:]


def heads_a_step(heads, length):
    return 2 if heads % 2 == 0 and length <= 512 else 1


def params():
    return pltpu.CompilerParams(vmem_limit_bytes=48 * 1024 * 1024)


def cost(dots, heads, length, arrays):
    return pl.CostEstimate(
        flops=2 * dots * heads * length * length * HEAD_DIM,
        bytes_accessed=2 * arrays * length * heads * HEAD_DIM,
        transcendentals=heads * length * length,
    )


def forward(mine, own, far):
    tokens = own[0].shape[0]
    _, rest, features = far.shape
    length = tokens + rest
    heads = features // HEAD_DIM
    step = heads_a_step(heads, length)
    grid = heads // step
    block = step * HEAD_DIM
    own_spec = pl.BlockSpec((tokens, block), lambda h, mine: (0, mine[0] * grid + h))
    far_spec = pl.BlockSpec((3, rest, block), lambda h, mine: (0, 0, h))
    return pl.pallas_call(
        functools.partial(forward_kernel, step),
        grid_spec=pltpu.PrefetchScalarGridSpec(
            num_scalar_prefetch=1,
            grid=(grid,),
            in_specs=[own_spec] * 3 + [far_spec],
            out_specs=pl.BlockSpec((length, block), lambda h, mine: (0, h)),
        ),
        out_shape=jax.ShapeDtypeStruct((length, features), jnp.bfloat16),
        compiler_params=params(),
        cost_estimate=cost(2, heads, length, 4),
        name="forward",
    )(mine, *own, far)


def backward(mine, own, far, partial, terms, first_head, heads, held):
    tokens, width = own[0].shape
    _, rest, features = far.shape
    length = tokens + rest
    step = heads_a_step(heads, length)
    grid = heads // step
    block = step * HEAD_DIM
    every = features // block
    start = first_head // step
    own_spec = pl.BlockSpec((tokens, block), lambda h, mine: (0, mine[0] * every + start + h))
    far_spec = pl.BlockSpec((3, rest, block), lambda h, mine: (0, 0, start + h))
    grad_spec = pl.BlockSpec((length, block), lambda h, mine: (0, h))
    any_spec = pl.BlockSpec(memory_space=pl.ANY)
    before = 6 + len(terms)
    return pl.pallas_call(
        functools.partial(backward_kernel, step, len(held), 1 + len(terms)),
        grid_spec=pltpu.PrefetchScalarGridSpec(
            num_scalar_prefetch=1,
            grid=(grid,),
            in_specs=[own_spec] * 3
            + [far_spec]
            + [pl.BlockSpec((length, block), lambda h, mine: (0, start + h))]
            + [grad_spec] * len(terms)
            + [any_spec] * len(held),
            out_specs=[own_spec] * 3
            + [pl.BlockSpec((3, rest, block), lambda h, mine: (0, 0, h))],
        ),
        out_shape=[jax.ShapeDtypeStruct((tokens, width), jnp.bfloat16)] * 3
        + [jax.ShapeDtypeStruct((3, rest, heads * HEAD_DIM), jnp.bfloat16)],
        input_output_aliases={before + i: i for i in range(len(held))},
        compiler_params=params(),
        cost_estimate=cost(6, heads, length, 9),
        name="backward",
    )(mine, *own, far, partial, *terms, *held)


def partial_kernel(pieces, at_ref, own_ref, far_ref, *refs):
    weights, (out_ref, every_row, every_weight) = refs[:pieces], refs[pieces:]
    tokens = own_ref.shape[0]
    rows = weights[0].shape[0]

    @pl.when(pl.program_id(0) == 0)
    def _():
        every_row[:tokens] = own_ref[...]
        every_row[tokens:] = far_ref[...]

    for i, weight in enumerate(weights):
        every_weight[pl.ds(pl.multiple_of(at_ref[i] * rows, rows), rows), :] = weight[...]
    out_ref[...] = dot(every_row[...], every_weight[...], ((1,), (0,))).astype(out_ref.dtype)


def partial_product(at, own, far, weights, start, wide, dtype):
    tokens, depth = own.shape
    rest = far.shape[0]
    rows = weights[0].shape[0]
    block = 256 if wide % 256 == 0 else 128
    first = start // block
    return pl.pallas_call(
        functools.partial(partial_kernel, len(weights)),
        grid_spec=pltpu.PrefetchScalarGridSpec(
            num_scalar_prefetch=1,
            grid=(wide // block,),
            in_specs=[
                pl.BlockSpec((tokens, depth), lambda i, at: (0, 0)),
                pl.BlockSpec((rest, depth), lambda i, at: (0, 0)),
            ]
            + [pl.BlockSpec((rows, block), lambda i, at: (0, first + i))] * len(weights),
            out_specs=pl.BlockSpec((tokens + rest, block), lambda i, at: (0, i)),
            scratch_shapes=[
                pltpu.VMEM((tokens + rest, depth), jnp.bfloat16),
                pltpu.VMEM((depth, block), jnp.bfloat16),
            ],
        ),
        out_shape=jax.ShapeDtypeStruct((tokens + rest, wide), dtype),
        compiler_params=params(),
        cost_estimate=pl.CostEstimate(
            flops=2 * (tokens + rest) * depth * wide,
            bytes_accessed=2 * depth * (tokens + rest + wide),
            transcendentals=0,
        ),
        name="partial",
    )(at, own, far, *weights)


def rows_kernel(pieces, at_ref, *refs):
    inputs, (out_ref, every_grad, every_attended) = refs[: 3 * pieces], refs[3 * pieces :]
    tokens = inputs[0].shape[0]
    length = inputs[2].shape[0]

    @pl.when(pl.program_id(0) == 0)
    def _():
        for i in range(pieces):
            every_attended[i * length : (i + 1) * length] = inputs[3 * i + 2][...]

    for i in range(pieces):
        every_grad[i * length : i * length + tokens] = inputs[3 * i][...]
        every_grad[i * length + tokens : (i + 1) * length] = inputs[3 * i + 1][...]
    out_ref[...] = dot(every_grad[...], every_attended[...], ((0,), (0,))).astype(out_ref.dtype)


def rows_product(at, pieces, rows, group, groups, dtype):
    length, features = pieces[0][2].shape
    wide = features // groups
    operands, specs = [], []
    for own, far, attended in pieces:
        for grad in (own, far):
            tokens = grad.shape[0]
            if rows % 128 == 0:
                operands.append(grad)
                specs.append(pl.BlockSpec((tokens, rows), lambda i, at: (0, at[i])))
            else:
                operands.append(jnp.swapaxes(grad.reshape(tokens, -1, rows), 0, 1))
                specs.append(pl.BlockSpec((None, tokens, rows), lambda i, at: (at[i], 0, 0)))
        operands.append(attended)
        specs.append(pl.BlockSpec((length, wide), lambda i, at: (0, group)))
    depth = length * len(pieces)
    count = at.shape[0]
    return pl.pallas_call(
        functools.partial(rows_kernel, len(pieces)),
        grid_spec=pltpu.PrefetchScalarGridSpec(
            num_scalar_prefetch=1,
            grid=(count,),
            in_specs=specs,
            out_specs=pl.BlockSpec((None, rows, wide), lambda i, at: (i, 0, 0)),
            scratch_shapes=[
                pltpu.VMEM((depth, rows), jnp.bfloat16),
                pltpu.VMEM((depth, wide), jnp.bfloat16),
            ],
        ),
        out_shape=jax.ShapeDtypeStruct((count, rows, wide), dtype),
        compiler_params=params(),
        cost_estimate=pl.CostEstimate(
            flops=2 * depth * count * rows * wide,
            bytes_accessed=2 * depth * (count * rows + wide),
            transcendentals=0,
        ),
        name="rows",
    )(at, *operands)


def place(axis, by=0):
    return (lax.axis_index(axis) + by) % lax.axis_size(axis)


def block_at(zl, x, core):
    return ((zl * lax.axis_size("x") + x) * lax.axis_size("core") + core).astype(jnp.int32)


def blocks_along(axis, by):
    if axis == "x":
        zl = jnp.arange(lax.axis_size("zl"))
        return block_at(zl, place("x", by), place("core"))
    return block_at(place("zl", by), jnp.arange(lax.axis_size("x")), place("core"))


def gathered_weights(own):
    found = [((0, 0), own)]
    found += [((0, by), shift(own, "x", by)) for by in others("x")]
    for by in others("zl"):
        far = shift(own, "zl", by)
        found.append(((by, 0), far))
        found += [((by, bx), shift(far, "x", bx)) for bx in others("x")]
    every = [((zl, x, 0), block) for (zl, x), block in found]
    every += [
        ((zl, x, by), shift(block, "core", by)) for by in others("core") for (zl, x), block in found
    ]
    at = [block_at(place("zl", -zl), place("x", -x), place("core", -c)) for (zl, x, c), _ in every]
    return jnp.stack(at), [block for _, block in every]


def shards(grad_out, queries, keys, values, out_weight):
    seq = lax.axis_size("seq")
    mine = lax.axis_index("seq")
    tokens = grad_out.shape[1]
    rows, features = out_weight.shape
    length = tokens * seq
    heads = features // HEAD_DIM
    clips = math.prod(lax.axis_size(axis) for axis in DP)
    token_scale = 1.0 / math.sqrt(clips * length)
    me = mine.astype(jnp.int32).reshape(1)

    def along_seq(array, dim=0):
        arrived = [shift(array, "seq", by) for by in others("seq")]
        return arrived[0] if seq == 2 else jnp.concatenate(arrived, axis=dim)

    at, weights = gathered_weights(out_weight)

    own_grad = grad_out[0]
    halves = [shift(part_of(own_grad, "zh", by, 1), "zh", by) for by in others("zh")]

    own = (queries[0], keys[0], values[0])
    pieces = [
        shift(jnp.stack([part_of(part, "seq", by, 1) for part in own]), "seq", by)
        for by in others("seq")
    ]
    far = pieces[0] if seq == 2 else jnp.concatenate(pieces, axis=1)
    halves = [part_of(own_grad, "zh", 0, 1)] + halves

    grads = [(half, along_seq(half)) for half in halves]

    attended = forward(me, own, far)
    attends = [attended] + [shift(attended, "zh", by) for by in others("zh")]

    groups = 2 if heads % 4 == 0 else 1
    wide = features // groups
    sent = [
        [
            partial_product(at, *grads[by], weights, group * wide, wide, jnp.bfloat16)
            for by in others("zh")
        ]
        for group in range(groups)
    ]
    partial = partial_product(at, *grads[0], weights, 0, features, jnp.float32)
    terms = [
        [shift(term, "zh", -by) for by, term in zip(others("zh"), group)] for group in sent
    ]

    clip_pieces = [(*grad, attend) for grad, attend in zip(grads, attends)]
    clip_pieces += [
        tuple(shift(array, "core", by) for array in piece)
        for by in others("core")
        for piece in clip_pieces
    ]
    clip_pieces, sent = lax.optimization_barrier((clip_pieces, sent))
    splits = 2 if features % 256 == 0 else 1
    orders = [("x", "zl"), ("zl", "x")][:splits]

    def product(axis, by, split, dtype):
        return rows_product(blocks_along(axis, by), clip_pieces, rows, split, splits, dtype)

    first = [
        [shift(product(axis, by, split, jnp.bfloat16), axis, by) for by in others(axis)]
        for split, (axis, _) in enumerate(orders)
    ]
    kept = [product(axis, 0, split, jnp.float32) for split, (axis, _) in enumerate(orders)]
    columns = []
    for (_, axis), arrived, total in zip(orders, first, kept):
        for term in arrived:
            total = total + term.astype(jnp.float32)
        second = [
            shift(part_of(total, axis, by, 0).astype(jnp.bfloat16), axis, by)
            for by in others(axis)
        ]
        final = part_of(total, axis, 0, 0)
        for term in second:
            final = final + term.astype(jnp.float32)
        columns.append(final[0])
    weight_grad = jnp.concatenate(columns, axis=1) * token_scale

    result, arrivals = [], []
    for group in range(groups):
        start = group * wide // HEAD_DIM
        *result, leaving = backward(
            me, own, far, partial, terms[group], start, wide // HEAD_DIM, result
        )
        arrivals.append(
            [
                shift(leaving[:, (by - 1) * tokens : by * tokens], "seq", -by)
                for by in others("seq")
            ]
        )
    for group in range(groups):
        for by, back in zip(others("seq"), arrivals[group]):
            start = ((mine + by) % seq) * features + group * wide
            result = [
                lax.dynamic_update_slice_in_dim(whole, back[i], start, 1)
                for i, whole in enumerate(result)
            ]
    return (result[0][None], result[1][None], result[2][None], weight_grad)


def solution(mesh):
    dp, seq = mesh.devices.shape
    finer = Mesh(mesh.devices.reshape(2, dp // 8, 2, 2, seq), DP + ("seq",))
    tokens = P(DP, "seq", None)
    return jax.shard_map(
        shards,
        mesh=finer,
        in_specs=(tokens, tokens, tokens, tokens, P(DP, "seq")),
        out_specs=(tokens, tokens, tokens, P(DP, "seq")),
        check_vma=False,
    )
```

```python
import functools
import math

import jax
import jax.numpy as jnp
from jax import lax
from jax.experimental import pallas as pl
from jax.experimental.pallas import tpu as pltpu
from jax.sharding import Mesh
from jax.sharding import PartitionSpec as P

HEAD_DIM = 128
INVERSE_ROOT = 1.0 / math.sqrt(HEAD_DIM)
DP = ("zh", "zl", "x", "core")


def dot(a, b, contract):
    return lax.dot_general(a, b, (contract, ((), ())), preferred_element_type=jnp.float32)


def shift(array, axis, by):
    count = lax.axis_size(axis)
    return lax.ppermute(array, axis, [(i, (i + by) % count) for i in range(count)])


def others(axis):
    return range(1, lax.axis_size(axis))


def part_of(array, axis, by, dim):
    count = lax.axis_size(axis)
    size = array.shape[dim] // count
    at = (lax.axis_index(axis) + by) % count
    return lax.dynamic_slice_in_dim(array, at * size, size, dim)


def softmax(q, k):
    scores = dot(q, k, ((1,), (1,))) * INVERSE_ROOT
    raised = jnp.exp(scores - jnp.max(scores, axis=-1, keepdims=True))
    return raised * (1.0 / jnp.sum(raised, axis=-1, keepdims=True))


def both(own, far, at):
    return jnp.concatenate([own[:, at], far[:, at]], axis=0)


def forward_kernel(heads, mine_ref, q_own, k_own, v_own, far, att_ref):
    for head in range(heads):
        at = slice(head * HEAD_DIM, (head + 1) * HEAD_DIM)
        q, k, v = (both(own, far.at[i], at) for i, own in enumerate((q_own, k_own, v_own)))
        low = softmax(q, k).astype(jnp.bfloat16)
        att_ref[:, at] = dot(low, v, ((1,), (0,))).astype(jnp.bfloat16)


def backward_kernel(heads, held, terms, mine_ref, q_own, k_own, v_own, far, *refs):
    grad_refs, refs = refs[:terms], refs[terms + held :]
    dq_own, dk_own, dv_own, leaving = refs
    tokens = q_own.shape[0]
    for head in range(heads):
        at = slice(head * HEAD_DIM, (head + 1) * HEAD_DIM)
        q, k, v = (both(own, far.at[i], at) for i, own in enumerate((q_own, k_own, v_own)))
        total = grad_refs[0][:, at].astype(jnp.float32)
        for ref in grad_refs[1:]:
            total = total + ref[:, at].astype(jnp.float32)
        g = total.astype(jnp.bfloat16)
        probs = softmax(q, k)
        low = probs.astype(jnp.bfloat16)
        att = dot(low, v, ((1,), (0,))).astype(jnp.bfloat16)
        delta = jnp.sum(
            g.astype(jnp.float32) * att.astype(jnp.float32), axis=-1, keepdims=True
        )
        d_probs = dot(g, v, ((1,), (1,)))
        d_low = (probs * (d_probs - delta)).astype(jnp.bfloat16)
        dq = (dot(d_low, k, ((1,), (0,))) * INVERSE_ROOT).astype(jnp.bfloat16)
        dk = (dot(d_low, q, ((0,), (0,))) * INVERSE_ROOT).astype(jnp.bfloat16)
        dv = dot(low, g, ((0,), (0,))).astype(jnp.bfloat16)
        for i, (own, value) in enumerate(((dq_own, dq), (dk_own, dk), (dv_own, dv))):
            own[:, at] = value[:tokens]
            leaving[i, :, at] = value[tokens:]


def heads_a_step(heads, length):
    return 2 if heads % 2 == 0 and length <= 512 else 1


def params():
    return pltpu.CompilerParams(vmem_limit_bytes=48 * 1024 * 1024)


def small():
    return pl.CostEstimate(flops=1024, bytes_accessed=1024, transcendentals=0)


def after(value, *events):
    return lax.optimization_barrier((value, events))[0]


def forward(mine, own, far):
    tokens = own[0].shape[0]
    _, rest, features = far.shape
    length = tokens + rest
    heads = features // HEAD_DIM
    step = heads_a_step(heads, length)
    grid = heads // step
    block = step * HEAD_DIM
    own_spec = pl.BlockSpec((tokens, block), lambda h, mine: (0, mine[0] * grid + h))
    far_spec = pl.BlockSpec((3, rest, block), lambda h, mine: (0, 0, h))
    return pl.pallas_call(
        functools.partial(forward_kernel, step),
        grid_spec=pltpu.PrefetchScalarGridSpec(
            num_scalar_prefetch=1,
            grid=(grid,),
            in_specs=[own_spec] * 3 + [far_spec],
            out_specs=pl.BlockSpec((length, block), lambda h, mine: (0, h)),
        ),
        out_shape=jax.ShapeDtypeStruct((length, features), jnp.bfloat16),
        compiler_params=params(),
        cost_estimate=small(),
        name="forward",
    )(mine, *own, far)


def backward(mine, own, far, partial, terms, first_head, heads, held):
    tokens, width = own[0].shape
    _, rest, features = far.shape
    length = tokens + rest
    step = heads_a_step(heads, length)
    grid = heads // step
    block = step * HEAD_DIM
    every = features // block
    start = first_head // step
    own_spec = pl.BlockSpec((tokens, block), lambda h, mine: (0, mine[0] * every + start + h))
    far_spec = pl.BlockSpec((3, rest, block), lambda h, mine: (0, 0, start + h))
    grad_spec = pl.BlockSpec((length, block), lambda h, mine: (0, h))
    any_spec = pl.BlockSpec(memory_space=pl.ANY)
    before = 6 + len(terms)
    return pl.pallas_call(
        functools.partial(backward_kernel, step, len(held), 1 + len(terms)),
        grid_spec=pltpu.PrefetchScalarGridSpec(
            num_scalar_prefetch=1,
            grid=(grid,),
            in_specs=[own_spec] * 3
            + [far_spec]
            + [grad_spec] * (1 + len(terms))
            + [any_spec] * len(held),
            out_specs=[own_spec] * 3
            + [pl.BlockSpec((3, rest, block), lambda h, mine: (0, 0, h))],
        ),
        out_shape=[jax.ShapeDtypeStruct((tokens, width), jnp.bfloat16)] * 3
        + [jax.ShapeDtypeStruct((3, rest, heads * HEAD_DIM), jnp.bfloat16)],
        input_output_aliases={before + i: i for i in range(len(held))},
        compiler_params=params(),
        cost_estimate=small(),
        name="backward",
    )(mine, *own, far, partial, *terms, *held)


def partial_kernel(own_ref, far_ref, weight_ref, out_ref, every_row):
    tokens = own_ref.shape[0]

    @pl.when(pl.program_id(0) == 0)
    def _():
        every_row[:tokens] = own_ref[...]
        every_row[tokens:] = far_ref[...]

    out_ref[...] = dot(every_row[...], weight_ref[...], ((1,), (0,))).astype(out_ref.dtype)


def partial_product(own, far, weight, dtype):
    tokens, depth = own.shape
    rest = far.shape[0]
    wide = weight.shape[1]
    block = 256 if wide % 256 == 0 else 128
    return pl.pallas_call(
        partial_kernel,
        grid=(wide // block,),
        in_specs=[
            pl.BlockSpec((tokens, depth), lambda i: (0, 0)),
            pl.BlockSpec((rest, depth), lambda i: (0, 0)),
            pl.BlockSpec((depth, block), lambda i: (0, i)),
        ],
        out_specs=pl.BlockSpec((tokens + rest, block), lambda i: (0, i)),
        scratch_shapes=[pltpu.VMEM((tokens + rest, depth), jnp.bfloat16)],
        out_shape=jax.ShapeDtypeStruct((tokens + rest, wide), dtype),
        compiler_params=params(),
        cost_estimate=small(),
        name="partial",
    )(own, far, weight)


def turn_kernel(at_ref, *refs):
    *inputs, out_ref = refs
    column = 0
    for ref in inputs:
        tokens = ref.shape[0]
        out_ref[:, column : column + tokens] = ref[...].T
        column += tokens


def turned(at, grads, rows):
    operands, specs = [], []
    for grad in grads:
        tokens = grad.shape[0]
        if rows % 128 == 0:
            operands.append(grad)
            specs.append(pl.BlockSpec((tokens, rows), lambda i, at: (0, at[i])))
        else:
            operands.append(jnp.swapaxes(grad.reshape(tokens, -1, rows), 0, 1))
            specs.append(pl.BlockSpec((None, tokens, rows), lambda i, at: (at[i], 0, 0)))
    depth = sum(grad.shape[0] for grad in grads)
    return pl.pallas_call(
        turn_kernel,
        grid_spec=pltpu.PrefetchScalarGridSpec(
            num_scalar_prefetch=1,
            grid=(at.shape[0],),
            in_specs=specs,
            out_specs=pl.BlockSpec((None, rows, depth), lambda i, at: (i, 0, 0)),
        ),
        out_shape=jax.ShapeDtypeStruct((at.shape[0], rows, depth), jnp.bfloat16),
        compiler_params=params(),
        cost_estimate=small(),
        name="turn",
    )(at, *operands)


def rows_kernel(cores, at_ref, *refs):
    grads, (*attends, out_ref) = refs[:cores], refs[cores:]
    length = attends[0].shape[0]
    each = len(attends) // cores
    total = None
    for i, attended in enumerate(attends):
        start = (i % each) * length
        chosen = grads[i // each][:, start : start + length]
        term = dot(chosen, attended[...], ((1,), (0,)))
        total = term if total is None else total + term
    out_ref[...] = total.astype(out_ref.dtype)


def rows_product(at, grads, attends, group, groups, dtype):
    _, rows, depth = grads[0].shape
    flat = [array for arrays in attends for array in arrays]
    length, features = flat[0].shape
    wide = features // groups
    count = at.shape[0]
    return pl.pallas_call(
        functools.partial(rows_kernel, len(grads)),
        grid_spec=pltpu.PrefetchScalarGridSpec(
            num_scalar_prefetch=1,
            grid=(count,),
            in_specs=[pl.BlockSpec((None, rows, depth), lambda i, at: (at[i], 0, 0))] * len(grads)
            + [pl.BlockSpec((length, wide), lambda i, at: (0, group))] * len(flat),
            out_specs=pl.BlockSpec((None, rows, wide), lambda i, at: (i, 0, 0)),
        ),
        out_shape=jax.ShapeDtypeStruct((count, rows, wide), dtype),
        compiler_params=params(),
        cost_estimate=small(),
        name="rows",
    )(at, *grads, *flat)


def place(axis, by=0):
    return (lax.axis_index(axis) + by) % lax.axis_size(axis)


def blocks_along(axis, by):
    zl, x = jnp.arange(lax.axis_size("zl")), jnp.arange(lax.axis_size("x"))
    if axis == "x":
        x = place("x", by)
    else:
        zl = place("zl", by)
    return (zl * lax.axis_size("x") + x).astype(jnp.int32)


def shards(grad_out, queries, keys, values, out_weight):
    seq = lax.axis_size("seq")
    mine = lax.axis_index("seq")
    tokens = grad_out.shape[1]
    rows, features = out_weight.shape
    length = tokens * seq
    heads = features // HEAD_DIM
    clips = math.prod(lax.axis_size(axis) for axis in DP)
    token_scale = 1.0 / math.sqrt(clips * length)
    me = mine.astype(jnp.int32).reshape(1)

    def along_seq(array):
        arrived = [shift(array, "seq", by) for by in others("seq")]
        return arrived[0] if seq == 2 else jnp.concatenate(arrived, axis=0)

    groups = 2 if heads % 4 == 0 else 1
    wide = features // groups
    weights = [
        lax.all_gather(
            out_weight[:, group * wide : (group + 1) * wide], ("zl", "x", "core"), tiled=True
        )
        for group in range(groups)
    ]
    own_grad = grad_out[0]
    halves = [shift(part_of(own_grad, "zh", by, 1), "zh", by) for by in others("zh")]
    own = (queries[0], keys[0], values[0])
    pieces = [
        shift(jnp.stack([part_of(part, "seq", by, 1) for part in own]), "seq", by)
        for by in others("seq")
    ]
    far = pieces[0] if seq == 2 else jnp.concatenate(pieces, axis=1)

    attended = forward(me, own, far)
    attends = [shift(attended, "zh", by) for by in others("zh")]
    attended_across = [shift(attended, "core", by) for by in others("core")]

    halves = after(halves, attended)
    own_half = after(part_of(own_grad, "zh", 0, 1), halves)
    grads = [(half, along_seq(half)) for half in [own_half] + halves]

    def partials(group):
        return [partial_product(*grad, weights[group], jnp.bfloat16) for grad in grads[1:]]

    def returned(terms):
        return [shift(term, "zh", -by) for by, term in zip(others("zh"), terms)]

    def own_partial(group):
        return partial_product(*grads[0], weights[group], jnp.float32)

    sent = partials(0)
    partial = [own_partial(0)]
    mine_blocks = jnp.arange(lax.axis_size("zl") * lax.axis_size("x")) * lax.axis_size("core")
    flat = after([half for grad in grads for half in grad], sent, partial)

    def turned_for(by, arrays):
        return turned((mine_blocks + place("core", by)).astype(jnp.int32), arrays, rows)

    by_rows = [shift(turned_for(by, flat), "core", by) for by in others("core")]
    attends, sent = after((attends, sent), flat)
    terms = [returned(after(sent, attends))]
    attends_across = [[shift(array, "core", by) for array in attends] for by in others("core")]
    by_rows = [turned_for(0, after(flat, attends))] + by_rows
    attends = [[attended] + attends] + [
        [near] + more for near, more in zip(attended_across, attends_across)
    ]
    splits = 2 if features % 256 == 0 else 1
    orders = [("x", "zl"), ("zl", "x")][:splits]

    def product(axis, by, split, dtype):
        return rows_product(blocks_along(axis, by), by_rows, attends, split, splits, dtype)

    leave = [
        [product(axis, by, split, jnp.bfloat16) for by in others(axis)]
        for split, (axis, _) in enumerate(orders)
    ]
    arrive = [
        [shift(term, axis, by) for by, term in zip(others(axis), terms_of)]
        for (axis, _), terms_of in zip(orders, leave)
    ]
    result, arrivals = [], []

    def finish(group, *events):
        start = group * wide // HEAD_DIM
        *result[:], leaving = backward(
            me,
            own,
            far,
            partial[group],
            after(terms[group], *events),
            start,
            wide // HEAD_DIM,
            list(result),
        )
        arrivals.append(
            [
                shift(leaving[:, (by - 1) * tokens : by * tokens], "seq", -by)
                for by in others("seq")
            ]
        )

    for group in range(1, groups):
        weights[group] = after(weights[group], leave)
        terms.append(returned(partials(group)))
        finish(group - 1, weights[group])
        weights[group] = after(weights[group], result)
        partial.append(own_partial(group))
    by_rows = after(by_rows, partial, result)
    kept = [product(axis, 0, split, jnp.float32) for split, (axis, _) in enumerate(orders)]
    finish(groups - 1, kept)

    columns = []
    for (_, axis), arrived, total in zip(orders, after(arrive, result), kept):
        for term in arrived:
            total = total + term.astype(jnp.float32)
        second = [
            shift(part_of(total, axis, by, 0).astype(jnp.bfloat16), axis, by)
            for by in others(axis)
        ]
        final = part_of(total, axis, 0, 0)
        for term in second:
            final = final + term.astype(jnp.float32)
        columns.append(final[0])
    weight_grad = jnp.concatenate(columns, axis=1) * token_scale

    for group in range(groups):
        for by, back in zip(others("seq"), arrivals[group]):
            start = ((mine + by) % seq) * features + group * wide
            result = [
                lax.dynamic_update_slice_in_dim(whole, back[i], start, 1)
                for i, whole in enumerate(result)
            ]
    return (result[0][None], result[1][None], result[2][None], weight_grad)


def solution(mesh):
    dp, seq = mesh.devices.shape
    finer = Mesh(mesh.devices.reshape(2, dp // 8, 2, 2, seq), DP + ("seq",))
    tokens = P(DP, "seq", None)
    return jax.shard_map(
        shards,
        mesh=finer,
        in_specs=(tokens, tokens, tokens, tokens, P(DP, "seq")),
        out_specs=(tokens, tokens, tokens, P(DP, "seq")),
        check_vma=False,
    )
```

```python
import functools
import math

import jax
import jax.numpy as jnp
from jax import lax
from jax.experimental import pallas as pl
from jax.experimental.pallas import tpu as pltpu
from jax.sharding import Mesh
from jax.sharding import PartitionSpec as P

HEAD_DIM = 128
INVERSE_ROOT = 1.0 / math.sqrt(HEAD_DIM)
DP = ("zh", "zl", "x", "core")


def dot(a, b, contract):
    return lax.dot_general(a, b, (contract, ((), ())), preferred_element_type=jnp.float32)


def shift(array, axis, by):
    count = lax.axis_size(axis)
    return lax.ppermute(array, axis, [(i, (i + by) % count) for i in range(count)])


def others(axis):
    return range(1, lax.axis_size(axis))


def part_of(array, axis, by, dim):
    count = lax.axis_size(axis)
    size = array.shape[dim] // count
    at = (lax.axis_index(axis) + by) % count
    return lax.dynamic_slice_in_dim(array, at * size, size, dim)


def softmax(q, k):
    scores = dot(q, k, ((1,), (1,))) * INVERSE_ROOT
    raised = jnp.exp(scores - jnp.max(scores, axis=-1, keepdims=True))
    return raised * (1.0 / jnp.sum(raised, axis=-1, keepdims=True))


def both(own, far, at):
    return jnp.concatenate([own[:, at], far[:, at]], axis=0)


def forward_kernel(heads, mine_ref, q_own, k_own, v_own, far, att_ref):
    for head in range(heads):
        at = slice(head * HEAD_DIM, (head + 1) * HEAD_DIM)
        q, k, v = (both(own, far.at[i], at) for i, own in enumerate((q_own, k_own, v_own)))
        low = softmax(q, k).astype(jnp.bfloat16)
        att_ref[:, at] = dot(low, v, ((1,), (0,))).astype(jnp.bfloat16)


def backward_kernel(heads, held, terms, mine_ref, q_own, k_own, v_own, far, *refs):
    grad_refs, refs = refs[:terms], refs[terms + held :]
    dq_own, dk_own, dv_own, leaving = refs
    tokens = q_own.shape[0]
    for head in range(heads):
        at = slice(head * HEAD_DIM, (head + 1) * HEAD_DIM)
        q, k, v = (both(own, far.at[i], at) for i, own in enumerate((q_own, k_own, v_own)))
        total = grad_refs[0][:, at].astype(jnp.float32)
        for ref in grad_refs[1:]:
            total = total + ref[:, at].astype(jnp.float32)
        g = total.astype(jnp.bfloat16)
        probs = softmax(q, k)
        low = probs.astype(jnp.bfloat16)
        att = dot(low, v, ((1,), (0,))).astype(jnp.bfloat16)
        delta = jnp.sum(
            g.astype(jnp.float32) * att.astype(jnp.float32), axis=-1, keepdims=True
        )
        d_probs = dot(g, v, ((1,), (1,)))
        d_low = (probs * (d_probs - delta)).astype(jnp.bfloat16)
        dq = (dot(d_low, k, ((1,), (0,))) * INVERSE_ROOT).astype(jnp.bfloat16)
        dk = (dot(d_low, q, ((0,), (0,))) * INVERSE_ROOT).astype(jnp.bfloat16)
        dv = dot(low, g, ((0,), (0,))).astype(jnp.bfloat16)
        for i, (own, value) in enumerate(((dq_own, dq), (dk_own, dk), (dv_own, dv))):
            own[:, at] = value[:tokens]
            leaving[i, :, at] = value[tokens:]


def heads_a_step(heads, length):
    return 2 if heads % 2 == 0 and length <= 512 else 1


def params():
    return pltpu.CompilerParams(vmem_limit_bytes=56 * 1024 * 1024)


def small():
    return pl.CostEstimate(flops=1024, bytes_accessed=1024, transcendentals=0)


def after(value, *events):
    return lax.optimization_barrier((value, events))[0]


def within(start, end):
    return lambda step, *_: (0, jnp.clip(step - start, 0, end - start - 1))


def forward(mine, own, far):
    tokens = own[0].shape[0]
    _, rest, features = far.shape
    length = tokens + rest
    heads = features // HEAD_DIM
    step = heads_a_step(heads, length)
    grid = heads // step
    block = step * HEAD_DIM
    own_spec = pl.BlockSpec((tokens, block), lambda h, mine: (0, mine[0] * grid + h))
    far_spec = pl.BlockSpec((3, rest, block), lambda h, mine: (0, 0, h))
    return pl.pallas_call(
        functools.partial(forward_kernel, step),
        grid_spec=pltpu.PrefetchScalarGridSpec(
            num_scalar_prefetch=1,
            grid=(grid,),
            in_specs=[own_spec] * 3 + [far_spec],
            out_specs=pl.BlockSpec((length, block), lambda h, mine: (0, h)),
        ),
        out_shape=jax.ShapeDtypeStruct((length, features), jnp.bfloat16),
        compiler_params=params(),
        cost_estimate=small(),
        name="forward",
    )(mine, *own, far)


def backward(mine, own, far, partial, terms, first_head, heads, held):
    tokens, width = own[0].shape
    _, rest, features = far.shape
    length = tokens + rest
    step = heads_a_step(heads, length)
    grid = heads // step
    block = step * HEAD_DIM
    every = features // block
    start = first_head // step
    own_spec = pl.BlockSpec((tokens, block), lambda h, mine: (0, mine[0] * every + start + h))
    far_spec = pl.BlockSpec((3, rest, block), lambda h, mine: (0, 0, start + h))
    grad_spec = pl.BlockSpec((length, block), lambda h, mine: (0, h))
    any_spec = pl.BlockSpec(memory_space=pl.ANY)
    before = 6 + len(terms)
    return pl.pallas_call(
        functools.partial(backward_kernel, step, len(held), 1 + len(terms)),
        grid_spec=pltpu.PrefetchScalarGridSpec(
            num_scalar_prefetch=1,
            grid=(grid,),
            in_specs=[own_spec] * 3
            + [far_spec]
            + [grad_spec] * (1 + len(terms))
            + [any_spec] * len(held),
            out_specs=[own_spec] * 3
            + [pl.BlockSpec((3, rest, block), lambda h, mine: (0, 0, h))],
        ),
        out_shape=[jax.ShapeDtypeStruct((tokens, width), jnp.bfloat16)] * 3
        + [jax.ShapeDtypeStruct((3, rest, heads * HEAD_DIM), jnp.bfloat16)],
        input_output_aliases={before + i: i for i in range(len(held))},
        compiler_params=params(),
        cost_estimate=small(),
        name="backward",
    )(mine, *own, far, partial, *terms, *held)


def partial_kernel(clips, bounds, at_ref, *refs):
    owns, fars, refs = refs[:clips], refs[clips : 2 * clips], refs[2 * clips :]
    groups = len(bounds)
    *weights, every_row, every_weight = refs
    weights, outs = weights[: -clips * groups], weights[-clips * groups :]
    tokens = owns[0].shape[0]
    length = tokens + fars[0].shape[0]
    rows = weights[0].shape[0]
    step = pl.program_id(0)

    @pl.when(step == 0)
    def _():
        for i, (own, far) in enumerate(zip(owns, fars)):
            every_row[i * length : i * length + tokens] = own[...]
            every_row[i * length + tokens : (i + 1) * length] = far[...]

    for i, weight in enumerate(weights):
        every_weight[pl.ds(pl.multiple_of(at_ref[i] * rows, rows), rows), :] = weight[...]
    product = dot(every_row[...], every_weight[...], ((1,), (0,)))
    for i in range(clips):
        for (start, end), out_ref in zip(bounds, outs[i * groups : (i + 1) * groups]):

            @pl.when((step >= start) & (step < end))
            def _():
                out_ref[...] = product[i * length : (i + 1) * length].astype(out_ref.dtype)


def partial_products(at, owns, fars, weights, groups, dtype):
    tokens, depth = owns[0].shape
    clips, rest = len(owns), fars[0].shape[0]
    length = tokens + rest
    rows, features = weights[0].shape
    wide = features // groups
    block = 256 if wide % 256 == 0 else 128
    steps = wide // block
    bounds = [(group * steps, (group + 1) * steps) for group in range(groups)]
    once = pl.Buffered(1)
    found = pl.pallas_call(
        functools.partial(partial_kernel, clips, bounds),
        grid_spec=pltpu.PrefetchScalarGridSpec(
            num_scalar_prefetch=1,
            grid=(groups * steps,),
            in_specs=[
                pl.BlockSpec(array.shape, lambda i, at: (0, 0), pipeline_mode=once)
                for array in [*owns, *fars]
            ]
            + [pl.BlockSpec((rows, block), lambda i, at: (0, i))] * len(weights),
            out_specs=[pl.BlockSpec((length, block), within(*bound)) for bound in bounds] * clips,
            scratch_shapes=[
                pltpu.VMEM((clips * length, depth), jnp.bfloat16),
                pltpu.VMEM((depth, block), jnp.bfloat16),
            ],
        ),
        out_shape=[
            jax.ShapeDtypeStruct((length, wide), dtype) for _ in range(clips * groups)
        ],
        compiler_params=params(),
        cost_estimate=small(),
        name="partial",
    )(at, *owns, *fars, *weights)
    return [found[i * groups : (i + 1) * groups] for i in range(clips)]


def turn_kernel(clips, at_ref, *refs):
    out_ref = refs[-1]
    start = 0
    for i in range(clips):
        for ref in (refs[i], refs[clips + i]):
            tokens = ref.shape[0]
            out_ref[:, start : start + tokens] = ref[...].T
            start += tokens


def turned(at, owns, fars, rows):
    operands, specs = [], []
    for grad in [*owns, *fars]:
        tokens = grad.shape[0]
        if rows % 128 == 0:
            operands.append(grad)
            specs.append(pl.BlockSpec((tokens, rows), lambda i, at: (0, at[i])))
        else:
            operands.append(jnp.swapaxes(grad.reshape(tokens, -1, rows), 0, 1))
            specs.append(pl.BlockSpec((None, tokens, rows), lambda i, at: (at[i], 0, 0)))
    depth = sum(grad.shape[0] for grad in [*owns, *fars])
    return pl.pallas_call(
        functools.partial(turn_kernel, len(owns)),
        grid_spec=pltpu.PrefetchScalarGridSpec(
            num_scalar_prefetch=1,
            grid=(at.shape[0],),
            in_specs=specs,
            out_specs=pl.BlockSpec((None, rows, depth), lambda i, at: (i, 0, 0)),
        ),
        out_shape=jax.ShapeDtypeStruct((at.shape[0], rows, depth), jnp.bfloat16),
        compiler_params=params(),
        cost_estimate=small(),
        name="turn",
    )(at, *operands)


def rows_kernel(cores, at_ref, *refs):
    grads, attends, out_ref = refs[:cores], refs[cores : 2 * cores], refs[-1]
    total = None
    for grad, attended in zip(grads, attends):
        clips, length, wide = attended.shape
        term = dot(grad[...], attended[...].reshape(clips * length, wide), ((1,), (0,)))
        total = term if total is None else total + term
    out_ref[...] = total.astype(out_ref.dtype)


def rows_product(at, grads, attends, start, wide, dtype):
    _, rows, depth = grads[0].shape
    clips, length, _ = attends[0].shape
    column = start // wide
    count = at.shape[0]
    return pl.pallas_call(
        functools.partial(rows_kernel, len(grads)),
        grid_spec=pltpu.PrefetchScalarGridSpec(
            num_scalar_prefetch=1,
            grid=(count,),
            in_specs=[pl.BlockSpec((None, rows, depth), lambda i, at: (at[i], 0, 0))] * len(grads)
            + [pl.BlockSpec((clips, length, wide), lambda i, at: (0, 0, column))] * len(attends),
            out_specs=pl.BlockSpec((None, rows, wide), lambda i, at: (i, 0, 0)),
        ),
        out_shape=jax.ShapeDtypeStruct((count, rows, wide), dtype),
        compiler_params=params(),
        cost_estimate=small(),
        name="rows",
    )(at, *grads, *attends)


def place(axis, by=0):
    return (lax.axis_index(axis) + by) % lax.axis_size(axis)


def block_at(zl, x, core):
    return ((zl * lax.axis_size("x") + x) * lax.axis_size("core") + core).astype(jnp.int32)


def shift_both(array, zl, x):
    zls, xs = lax.axis_size("zl"), lax.axis_size("x")
    pairs = [
        (i * xs + j, ((i + zl) % zls) * xs + (j + x) % xs) for i in range(zls) for j in range(xs)
    ]
    return lax.ppermute(array, ("zl", "x"), pairs)


def blocks_along(axis, by):
    zl, x = jnp.arange(lax.axis_size("zl")), jnp.arange(lax.axis_size("x"))
    if axis == "x":
        x = place("x", by)
    else:
        zl = place("zl", by)
    return (zl * lax.axis_size("x") + x).astype(jnp.int32)


def shards(grad_out, queries, keys, values, out_weight):
    seq = lax.axis_size("seq")
    mine = lax.axis_index("seq")
    tokens = grad_out.shape[1]
    rows, features = out_weight.shape
    length = tokens * seq
    heads = features // HEAD_DIM
    clips = math.prod(lax.axis_size(axis) for axis in DP)
    token_scale = 1.0 / math.sqrt(clips * length)
    me = mine.astype(jnp.int32).reshape(1)

    def across(array):
        return [shift(array, "core", by) for by in others("core")]

    groups = 2 if heads % 4 == 0 else 1
    wide = features // groups
    unit = heads_a_step(heads, length)
    larger = (2 * heads // 3) // unit * unit
    widths = [count * HEAD_DIM for count in (larger, heads - larger) if count]
    orders = [("x", "zl"), ("zl", "x")][: len(widths)]

    own = (queries[0], keys[0], values[0])
    pieces = [
        shift(jnp.stack([part_of(part, "seq", by, 1) for part in own]), "seq", by)
        for by in others("seq")
    ]
    far = pieces[0] if seq == 2 else jnp.concatenate(pieces, axis=1)
    own_grad = grad_out[0]
    halves = [shift(part_of(own_grad, "zh", by, 1), "zh", by) for by in others("zh")]
    near_x = [shift(out_weight, "x", by) for by in others("x")]
    near_zl = [shift(out_weight, "zl", by) for by in others("zl")]
    own_across = across(out_weight)

    attended = forward(me, own, after(far, own_across))

    def along_seq(array):
        arrived = [shift(array, "seq", by) for by in others("seq")]
        return arrived[0] if seq == 2 else jnp.concatenate(arrived, axis=0)

    halves = after(halves, attended)
    attends = [shift(attended, "zh", by) for by in others("zh")]
    owns = [after(part_of(own_grad, "zh", 0, 1), halves)] + halves
    fars = [along_seq(half) for half in owns]
    near_zl = after(near_zl, halves)
    places = [(zl, x) for zl in others("zl") for x in others("x")]
    diagonal = [shift(block, "x", by) for block in near_zl for by in others("x")]

    near_x, near_zl, diagonal, attends, owns, fars = lax.optimization_barrier(
        (near_x, near_zl, diagonal, attends, owns, fars)
    )
    x_across = [across(block) for block in near_x]
    zl_across = [across(block) for block in near_zl]
    diagonal_across = [across(block) for block in diagonal]
    pair = jnp.stack([attended] + attends)
    attends = [pair] + across(pair)

    weights = [((0, 0), out_weight, own_across)]
    weights += [((0, by), *both_of) for by, *both_of in zip(others("x"), near_x, x_across)]
    weights += [((by, 0), *both_of) for by, *both_of in zip(others("zl"), near_zl, zl_across)]
    weights += zip(places, diagonal, diagonal_across)
    at, blocks = [], []
    for (zl, x), block, from_cores in weights:
        for core, array in enumerate([block] + from_cores):
            at.append(block_at(place("zl", -zl), place("x", -x), place("core", -core)))
            blocks.append(array)

    turns = jnp.arange(lax.axis_size("zl") * lax.axis_size("x")) * lax.axis_size("core")

    def turned_for(by):
        return turned((turns + place("core", by)).astype(jnp.int32), owns, fars, rows)

    others_rows = [turned_for(by) for by in others("core")]
    by_rows = [turned_for(0)] + [
        shift(array, "core", by) for by, array in zip(others("core"), others_rows)
    ]

    def product(axis, by, split, dtype):
        start = sum(widths[:split])
        return rows_product(blocks_along(axis, by), by_rows, attends, start, widths[split], dtype)

    leave = [
        [product(axis, by, split, jnp.bfloat16) for by in others(axis)]
        for split, (axis, _) in enumerate(orders)
    ]
    arrive = [
        [shift(term, axis, by) for by, term in zip(others(axis), terms_of)]
        for (axis, _), terms_of in zip(orders, leave)
    ]
    owns, fars = after((owns, fars), leave)
    sent = partial_products(jnp.stack(at), owns[1:], fars[1:], blocks, groups, jnp.bfloat16)
    terms = [
        [shift(clip[group], "zh", -by) for by, clip in zip(others("zh"), sent)]
        for group in range(groups)
    ]
    owns, fars = after((owns, fars), sent)
    (partial,) = partial_products(
        jnp.stack(at), owns[:1], fars[:1], blocks, groups, jnp.float32
    )
    by_rows = after(by_rows, partial)
    kept = [product(axis, 0, split, jnp.float32) for split, (axis, _) in enumerate(orders)]

    result, arrivals = [], []
    for group in range(groups):
        start = group * wide // HEAD_DIM
        *result, leaving = backward(
            me, own, far, partial[group], after(terms[group], kept), start, wide // HEAD_DIM, result
        )
        arrivals.append(
            [
                shift(leaving[:, (by - 1) * tokens : by * tokens], "seq", -by)
                for by in others("seq")
            ]
        )

    columns = []
    for (_, axis), arrived, total in zip(orders, after(arrive, result), kept):
        for term in arrived:
            total = total + term.astype(jnp.float32)
        second = [
            shift(part_of(total, axis, by, 0).astype(jnp.bfloat16), axis, by)
            for by in others(axis)
        ]
        final = part_of(total, axis, 0, 0)
        for term in second:
            final = final + term.astype(jnp.float32)
        columns.append(final[0])
    weight_grad = jnp.concatenate(columns, axis=1) * token_scale

    for group in range(groups):
        for by, back in zip(others("seq"), arrivals[group]):
            start = ((mine + by) % seq) * features + group * wide
            result = [
                lax.dynamic_update_slice_in_dim(whole, back[i], start, 1)
                for i, whole in enumerate(result)
            ]
    return (result[0][None], result[1][None], result[2][None], weight_grad)


def solution(mesh):
    dp, seq = mesh.devices.shape
    finer = Mesh(mesh.devices.reshape(2, dp // 8, 2, 2, seq), DP + ("seq",))
    tokens = P(DP, "seq", None)
    return jax.shard_map(
        shards,
        mesh=finer,
        in_specs=(tokens, tokens, tokens, tokens, P(DP, "seq")),
        out_specs=(tokens, tokens, tokens, P(DP, "seq")),
        check_vma=False,
    )
```

```python
import functools
import math

import jax
import jax.numpy as jnp
from jax import lax
from jax.experimental import pallas as pl
from jax.experimental.pallas import tpu as pltpu
from jax.sharding import Mesh
from jax.sharding import PartitionSpec as P

HEAD_DIM = 128
INVERSE_ROOT = 1.0 / math.sqrt(HEAD_DIM)
DP = ("zh", "zl", "x", "core")


def dot(a, b, contract):
    return lax.dot_general(a, b, (contract, ((), ())), preferred_element_type=jnp.float32)


def shift(array, axis, by):
    count = lax.axis_size(axis)
    return lax.ppermute(array, axis, [(i, (i + by) % count) for i in range(count)])


def others(axis):
    return range(1, lax.axis_size(axis))


def part_of(array, axis, by, dim):
    count = lax.axis_size(axis)
    size = array.shape[dim] // count
    at = (lax.axis_index(axis) + by) % count
    return lax.dynamic_slice_in_dim(array, at * size, size, dim)


def softmax(q, k):
    scores = dot(q, k, ((1,), (1,))) * INVERSE_ROOT
    raised = jnp.exp(scores - jnp.max(scores, axis=-1, keepdims=True))
    return raised * (1.0 / jnp.sum(raised, axis=-1, keepdims=True))


def all_tokens(own, far, at):
    return (jnp.concatenate([own[i, :, at], far[i, :, at]], axis=0) for i in range(3))


def forward_kernel(own, far, att_ref):
    for start in range(0, att_ref.shape[1], HEAD_DIM):
        at = slice(start, start + HEAD_DIM)
        q, k, v = all_tokens(own, far, at)
        low = softmax(q, k).astype(jnp.bfloat16)
        att_ref[:, at] = dot(low, v, ((1,), (0,))).astype(jnp.bfloat16)


def backward_kernel(first, own, far, *refs):
    *grad_refs, staying, leaving = refs
    tokens = own.shape[1]
    for start in range(0, staying.shape[2], HEAD_DIM):
        at = slice(start, start + HEAD_DIM)
        q, k, v = all_tokens(own, far, slice(first + start, first + start + HEAD_DIM))
        total = grad_refs[0][:, at].astype(jnp.float32)
        for ref in grad_refs[1:]:
            total = total + ref[:, at].astype(jnp.float32)
        g = total.astype(jnp.bfloat16)
        probs = softmax(q, k)
        low = probs.astype(jnp.bfloat16)
        att = dot(low, v, ((1,), (0,))).astype(jnp.bfloat16)
        delta = jnp.sum(
            g.astype(jnp.float32) * att.astype(jnp.float32), axis=-1, keepdims=True
        )
        d_probs = dot(g, v, ((1,), (1,)))
        d_low = (probs * (d_probs - delta)).astype(jnp.bfloat16)
        dq = (dot(d_low, k, ((1,), (0,))) * INVERSE_ROOT).astype(jnp.bfloat16)
        dk = (dot(d_low, q, ((0,), (0,))) * INVERSE_ROOT).astype(jnp.bfloat16)
        dv = dot(low, g, ((0,), (0,))).astype(jnp.bfloat16)
        for i, value in enumerate((dq, dk, dv)):
            staying[i, :, at] = value[:tokens]
            leaving[i, :, at] = value[tokens:]


def params(length):
    mebibytes = 32 if length <= 512 else 48
    return pltpu.CompilerParams(vmem_limit_bytes=mebibytes * 1024 * 1024)


def small():
    return pl.CostEstimate(flops=1024, bytes_accessed=1024, transcendentals=0)


def after(value, *events):
    return lax.optimization_barrier((value, events))[0]


def within(start, end):
    return lambda step, *_: (0, jnp.clip(step - start, 0, end - start - 1))


def whole_call(kernel, length, out_shape, operands, name, scalars=None, scratch_shapes=()):
    whole = pl.BlockSpec(memory_space=pltpu.VMEM)
    in_specs = [whole] * len(operands)
    if scalars is not None:
        operands = [scalars, *operands]
        in_specs = [pl.BlockSpec(memory_space=pltpu.SMEM)] + in_specs
    return pl.pallas_call(
        kernel,
        in_specs=in_specs,
        out_specs=jax.tree.map(lambda _: whole, out_shape),
        out_shape=out_shape,
        scratch_shapes=scratch_shapes,
        compiler_params=params(length),
        cost_estimate=small(),
        name=name,
    )(*operands)


def forward(own, far):
    _, tokens, features = own.shape
    length = tokens + far.shape[1]
    shape = jax.ShapeDtypeStruct((length, features), jnp.bfloat16)
    return whole_call(forward_kernel, length, shape, [own, far], "forward")


def backward(own, far, partial, terms, first):
    tokens, rest = own.shape[1], far.shape[1]
    wide = partial.shape[1]
    return whole_call(
        functools.partial(backward_kernel, first),
        tokens + rest,
        [jax.ShapeDtypeStruct((3, count, wide), jnp.bfloat16) for count in (tokens, rest)],
        [own, far, partial, *terms],
        "backward",
    )


def partial_kernel(pieces, at_ref, own, far, *refs):
    weights, outs, every = refs[:pieces], refs[pieces:-1], refs[-1]
    tokens = own.shape[0]
    rows = weights[0].shape[0]
    wide = outs[0].shape[1]
    block = 256 if wide % 256 == 0 else 128
    for i in range(pieces):
        columns = slice(i * rows, (i + 1) * rows)
        every[i, :tokens] = own[:, columns]
        every[i, tokens:] = far[:, columns]
    for group, out_ref in enumerate(outs):
        for start in range(0, wide, block):
            columns = slice(group * wide + start, group * wide + start + block)
            total = None
            for i, weight in enumerate(weights):
                term = dot(every[at_ref[i]], weight[:, columns], ((1,), (0,)))
                total = term if total is None else total + term
            out_ref[:, start : start + block] = total.astype(out_ref.dtype)


def partial_product(at, own, far, weights, groups, dtype):
    length = own.shape[0] + far.shape[0]
    rows, features = weights[0].shape
    return whole_call(
        functools.partial(partial_kernel, len(weights)),
        length,
        [jax.ShapeDtypeStruct((length, features // groups), dtype)] * groups,
        [own, far, *weights],
        "partial",
        at,
        [pltpu.VMEM((len(weights), length, rows), jnp.bfloat16)],
    )


def turn_kernel(clips, core_ref, *refs):
    grads, outs = refs[: 2 * clips], refs[2 * clips :]
    cores = len(outs)
    blocks, rows, _ = outs[0].shape
    for core in range(cores):

        @pl.when(core_ref[0] == core)
        def _():
            for by, out_ref in enumerate(outs):
                for i in range(blocks):
                    at = (i * cores + (core + by) % cores) * rows
                    start = 0
                    for grad in grads:
                        tokens = grad.shape[0]
                        out_ref[i, :, start : start + tokens] = grad[:, at : at + rows].T
                        start += tokens


def turned(core, owns, fars, rows, cores):
    grads = [grad for pair in zip(owns, fars) for grad in pair]
    depth = sum(grad.shape[0] for grad in grads)
    blocks = owns[0].shape[1] // (rows * cores)
    return whole_call(
        functools.partial(turn_kernel, len(owns)),
        depth,
        [jax.ShapeDtypeStruct((blocks, rows, depth), jnp.bfloat16)] * cores,
        grads,
        "turn",
        core,
    )


def rows_kernel(jobs, cores, at_ref, *refs):
    grads, attends, outs = refs[:cores], refs[cores : 2 * cores], refs[2 * cores :]
    clips, length, _ = attends[0].shape
    first = 0
    for (count, start, wide), out_ref in zip(jobs, outs):
        block = 256 if wide % 256 == 0 else 128
        for i in range(count):
            at = at_ref[first + i]
            for column in range(0, wide, block):
                columns = slice(start + column, start + column + block)
                total = None
                for grad, attended in zip(grads, attends):
                    chosen = attended[:, :, columns].reshape(clips * length, block)
                    term = dot(grad[at], chosen, ((1,), (0,)))
                    total = term if total is None else total + term
                out_ref[i, :, column : column + block] = total.astype(out_ref.dtype)
        first += count


def rows_products(jobs, grads, attends, dtype):
    rows = grads[0].shape[1]
    sizes = [(at.shape[0], start, wide) for at, start, wide in jobs]
    return whole_call(
        functools.partial(rows_kernel, sizes, len(grads)),
        grads[0].shape[2],
        [jax.ShapeDtypeStruct((count, rows, wide), dtype) for count, _, wide in sizes],
        [*grads, *attends],
        "rows",
        jnp.concatenate([at for at, _, _ in jobs]),
    )


def place(axis, by=0):
    return (lax.axis_index(axis) + by) % lax.axis_size(axis)


def block_at(zl, x, core):
    return ((zl * lax.axis_size("x") + x) * lax.axis_size("core") + core).astype(jnp.int32)


def shift_both(array, zl, x):
    zls, xs = lax.axis_size("zl"), lax.axis_size("x")
    pairs = [
        (i * xs + j, ((i + zl) % zls) * xs + (j + x) % xs) for i in range(zls) for j in range(xs)
    ]
    return lax.ppermute(array, ("zl", "x"), pairs)


def blocks_along(axis, by):
    zl, x = jnp.arange(lax.axis_size("zl")), jnp.arange(lax.axis_size("x"))
    if axis == "x":
        x = place("x", by)
    else:
        zl = place("zl", by)
    return (zl * lax.axis_size("x") + x).astype(jnp.int32)


def shards(grad_out, queries, keys, values, out_weight):
    seq = lax.axis_size("seq")
    mine = lax.axis_index("seq")
    tokens = grad_out.shape[1]
    rows, features = out_weight.shape
    length = tokens * seq
    heads = features // HEAD_DIM
    clips = math.prod(lax.axis_size(axis) for axis in DP)
    token_scale = 1.0 / math.sqrt(clips * length)

    def across(array):
        return [shift(array, "core", by) for by in others("core")]

    groups = 2 if heads % 4 == 0 else 1
    wide = features // groups
    larger = 2 * heads // 3
    widths = [count * HEAD_DIM for count in (larger, heads - larger) if count]
    orders = [("x", "zl"), ("zl", "x")][: len(widths)]

    def heads_of(by):
        return jnp.stack([part_of(part[0], "seq", by, 1) for part in (queries, keys, values)])

    pieces = [shift(heads_of(by), "seq", by) for by in others("seq")]
    far = pieces[0] if seq == 2 else jnp.concatenate(pieces, axis=1)
    own_grad = grad_out[0]
    halves = [shift(part_of(own_grad, "zh", by, 1), "zh", by) for by in others("zh")]
    near_x = [shift(out_weight, "x", by) for by in others("x")]
    near_zl = [shift(out_weight, "zl", by) for by in others("zl")]
    own_across = across(out_weight)

    own = heads_of(0)
    attended = forward(own, after(far, own_across))

    def along_seq(array):
        arrived = [shift(array, "seq", by) for by in others("seq")]
        return arrived[0] if seq == 2 else jnp.concatenate(arrived, axis=0)

    halves = after(halves, attended)
    attends = [shift(attended, "zh", by) for by in others("zh")]
    owns = [after(part_of(own_grad, "zh", 0, 1), halves)] + halves
    fars = [along_seq(half) for half in owns]
    near_zl = after(near_zl, halves)
    places = [(zl, x) for zl in others("zl") for x in others("x")]
    diagonal = [shift(block, "x", by) for block in near_zl for by in others("x")]

    near_x, near_zl, diagonal, attends, owns, fars = lax.optimization_barrier(
        (near_x, near_zl, diagonal, attends, owns, fars)
    )
    x_across = [across(block) for block in near_x]
    zl_across = [across(block) for block in near_zl]
    diagonal_across = [across(block) for block in diagonal]
    pair = jnp.stack([attended] + attends)
    attends = [pair] + across(pair)

    weights = [((0, 0), out_weight, own_across)]
    weights += [((0, by), *both_of) for by, *both_of in zip(others("x"), near_x, x_across)]
    weights += [((by, 0), *both_of) for by, *both_of in zip(others("zl"), near_zl, zl_across)]
    weights += zip(places, diagonal, diagonal_across)
    at, blocks = [], []
    for (zl, x), block, from_cores in weights:
        for core, array in enumerate([block] + from_cores):
            at.append(block_at(place("zl", -zl), place("x", -x), place("core", -core)))
            blocks.append(array)

    cores = lax.axis_size("core")
    core = place("core").astype(jnp.int32).reshape(1)
    by_rows = list(turned(core, owns, fars, rows, cores))
    by_rows = by_rows[:1] + [
        shift(array, "core", by) for by, array in zip(others("core"), by_rows[1:])
    ]

    starts = [sum(widths[:split]) for split in range(len(widths))]
    jobs = [
        (blocks_along(axis, by), start, size)
        for (axis, _), start, size in zip(orders, starts, widths)
        for by in others(axis)
    ]
    leave = rows_products(jobs, by_rows, attends, jnp.bfloat16)
    rest = iter(leave)
    arrive = [[shift(next(rest), axis, by) for by in others(axis)] for axis, _ in orders]

    owns, fars = after((owns, fars), leave)
    at = jnp.stack(at)
    sent = [
        partial_product(at, own_part, far_part, blocks, groups, jnp.bfloat16)
        for own_part, far_part in zip(owns[1:], fars[1:])
    ]
    terms = [
        [shift(clip[group], "zh", -by) for by, clip in zip(others("zh"), sent)]
        for group in range(groups)
    ]
    owns, fars = after((owns, fars), sent)
    partial = partial_product(at, owns[0], fars[0], blocks, groups, jnp.float32)
    jobs = [
        (blocks_along(axis, 0), start, size)
        for (axis, _), start, size in zip(orders, starts, widths)
    ]
    kept = rows_products(jobs, after(by_rows, partial), attends, jnp.float32)

    stays, arrivals = [], []
    for group in range(groups):
        start = group * wide
        staying, leaving = backward(own, far, partial[group], after(terms[group], kept), start)
        stays.append((mine * features + start, staying))
        for by in others("seq"):
            sent = leaving[:, (by - 1) * tokens : by * tokens]
            column = ((mine + by) % seq) * features + start
            arrivals.append((column, shift(sent, "seq", -by)))

    columns = []
    for (_, axis), arrived, total in zip(orders, after(arrive, [array for _, array in stays]), kept):
        for term in arrived:
            total = total + term.astype(jnp.float32)
        second = [
            shift(part_of(total, axis, by, 0).astype(jnp.bfloat16), axis, by)
            for by in others(axis)
        ]
        final = part_of(total, axis, 0, 0)
        for term in second:
            final = final + term.astype(jnp.float32)
        columns.append(final[0])
    weight_grad = jnp.concatenate(columns, axis=1) * token_scale

    result = jnp.zeros((3, tokens, queries.shape[2]), jnp.bfloat16)
    result = [result[0], result[1], result[2]]
    for column, arrays in stays + arrivals:
        result = [
            lax.dynamic_update_slice_in_dim(whole, array, column, 1)
            for whole, array in zip(result, arrays)
        ]
    return (result[0][None], result[1][None], result[2][None], weight_grad)


def solution(mesh):
    dp, seq = mesh.devices.shape
    finer = Mesh(mesh.devices.reshape(2, dp // 8, 2, 2, seq), DP + ("seq",))
    tokens = P(DP, "seq", None)
    return jax.shard_map(
        shards,
        mesh=finer,
        in_specs=(tokens, tokens, tokens, tokens, P(DP, "seq")),
        out_specs=(tokens, tokens, tokens, P(DP, "seq")),
        check_vma=False,
    )
```

```python
import functools
import math

import jax
import jax.numpy as jnp
from jax import lax
from jax.experimental import pallas as pl
from jax.experimental.pallas import tpu as pltpu
from jax.sharding import Mesh
from jax.sharding import PartitionSpec as P

HEAD_DIM = 128
INVERSE_ROOT = 1.0 / math.sqrt(HEAD_DIM)
DP = ("zh", "zl", "x", "core")


def dot(a, b, contract):
    return lax.dot_general(a, b, (contract, ((), ())), preferred_element_type=jnp.float32)


def shift(array, axis, by):
    count = lax.axis_size(axis)
    return lax.ppermute(array, axis, [(i, (i + by) % count) for i in range(count)])


def others(axis):
    return range(1, lax.axis_size(axis))


def part_of(array, axis, by, dim):
    count = lax.axis_size(axis)
    size = array.shape[dim] // count
    at = (lax.axis_index(axis) + by) % count
    return lax.dynamic_slice_in_dim(array, at * size, size, dim)


def softmax(q, k):
    scores = dot(q, k, ((1,), (1,))) * INVERSE_ROOT
    raised = jnp.exp(scores - jnp.max(scores, axis=-1, keepdims=True))
    return raised * (1.0 / jnp.sum(raised, axis=-1, keepdims=True))


def all_tokens(own, far, at):
    return (jnp.concatenate([own[i, :, at], far[i, :, at]], axis=0) for i in range(3))


def forward_kernel(own, far, att_ref):
    for start in range(0, att_ref.shape[1], HEAD_DIM):
        at = slice(start, start + HEAD_DIM)
        q, k, v = all_tokens(own, far, at)
        low = softmax(q, k).astype(jnp.bfloat16)
        att_ref[:, at] = dot(low, v, ((1,), (0,))).astype(jnp.bfloat16)


def backward_kernel(first, own, far, *refs):
    *grad_refs, staying, leaving = refs
    tokens = own.shape[1]
    for start in range(0, staying.shape[2], HEAD_DIM):
        at = slice(start, start + HEAD_DIM)
        q, k, v = all_tokens(own, far, slice(first + start, first + start + HEAD_DIM))
        total = grad_refs[0][:, at].astype(jnp.float32)
        for ref in grad_refs[1:]:
            total = total + ref[:, at].astype(jnp.float32)
        g = total.astype(jnp.bfloat16)
        probs = softmax(q, k)
        low = probs.astype(jnp.bfloat16)
        att = dot(low, v, ((1,), (0,))).astype(jnp.bfloat16)
        delta = jnp.sum(
            g.astype(jnp.float32) * att.astype(jnp.float32), axis=-1, keepdims=True
        )
        d_probs = dot(g, v, ((1,), (1,)))
        d_low = (probs * (d_probs - delta)).astype(jnp.bfloat16)
        dq = (dot(d_low, k, ((1,), (0,))) * INVERSE_ROOT).astype(jnp.bfloat16)
        dk = (dot(d_low, q, ((0,), (0,))) * INVERSE_ROOT).astype(jnp.bfloat16)
        dv = dot(low, g, ((0,), (0,))).astype(jnp.bfloat16)
        for i, value in enumerate((dq, dk, dv)):
            staying[i, :, at] = value[:tokens]
            leaving[i, :, at] = value[tokens:]


def params(length):
    mebibytes = 32 if length <= 512 else 48
    return pltpu.CompilerParams(vmem_limit_bytes=mebibytes * 1024 * 1024)


def small():
    return pl.CostEstimate(flops=1024, bytes_accessed=1024, transcendentals=0)


def after(value, *events):
    return lax.optimization_barrier((value, events))[0]


def within(start, end):
    return lambda step, *_: (0, jnp.clip(step - start, 0, end - start - 1))


def whole_call(kernel, length, out_shape, operands, name, scalars=None, scratch_shapes=()):
    whole = pl.BlockSpec(memory_space=pltpu.VMEM)
    in_specs = [whole] * len(operands)
    if scalars is not None:
        operands = [scalars, *operands]
        in_specs = [pl.BlockSpec(memory_space=pltpu.SMEM)] + in_specs
    return pl.pallas_call(
        kernel,
        in_specs=in_specs,
        out_specs=jax.tree.map(lambda _: whole, out_shape),
        out_shape=out_shape,
        scratch_shapes=scratch_shapes,
        compiler_params=params(length),
        cost_estimate=small(),
        name=name,
    )(*operands)


def forward(own, far):
    _, tokens, features = own.shape
    length = tokens + far.shape[1]
    shape = jax.ShapeDtypeStruct((length, features), jnp.bfloat16)
    return whole_call(forward_kernel, length, shape, [own, far], "forward")


def backward(own, far, partial, terms, first):
    tokens, rest = own.shape[1], far.shape[1]
    wide = partial.shape[1]
    return whole_call(
        functools.partial(backward_kernel, first),
        tokens + rest,
        [jax.ShapeDtypeStruct((3, count, wide), jnp.bfloat16) for count in (tokens, rest)],
        [own, far, partial, *terms],
        "backward",
    )


def partial_kernel(pieces, at_ref, own, far, *refs):
    weights, outs, every = refs[:pieces], refs[pieces:-1], refs[-1]
    tokens = own.shape[0]
    rows = weights[0].shape[0]
    wide = outs[0].shape[1]
    block = 256 if wide % 256 == 0 else 128
    for i in range(pieces):
        columns = slice(i * rows, (i + 1) * rows)
        every[i, :tokens] = own[:, columns]
        every[i, tokens:] = far[:, columns]
    for group, out_ref in enumerate(outs):
        for start in range(0, wide, block):
            columns = slice(group * wide + start, group * wide + start + block)
            grads = jnp.concatenate([every[at_ref[i]] for i in range(pieces)], axis=1)
            chosen = jnp.concatenate([weight[:, columns] for weight in weights], axis=0)
            product = dot(grads, chosen, ((1,), (0,)))
            out_ref[:, start : start + block] = product.astype(out_ref.dtype)


def partial_product(at, own, far, weights, groups, dtype):
    length = own.shape[0] + far.shape[0]
    rows, features = weights[0].shape
    return whole_call(
        functools.partial(partial_kernel, len(weights)),
        length,
        [jax.ShapeDtypeStruct((length, features // groups), dtype)] * groups,
        [own, far, *weights],
        "partial",
        at,
        [pltpu.VMEM((len(weights), length, rows), jnp.bfloat16)],
    )


def turn_kernel(clips, core_ref, *refs):
    grads, outs = refs[: 2 * clips], refs[2 * clips :]
    cores = len(outs)
    blocks, rows, _ = outs[0].shape
    for core in range(cores):

        @pl.when(core_ref[0] == core)
        def _():
            for by, out_ref in enumerate(outs):
                for i in range(blocks):
                    at = (i * cores + (core + by) % cores) * rows
                    start = 0
                    for grad in grads:
                        tokens = grad.shape[0]
                        out_ref[i, :, start : start + tokens] = grad[:, at : at + rows].T
                        start += tokens


def turned(core, owns, fars, rows, cores):
    grads = [grad for pair in zip(owns, fars) for grad in pair]
    depth = sum(grad.shape[0] for grad in grads)
    blocks = owns[0].shape[1] // (rows * cores)
    return whole_call(
        functools.partial(turn_kernel, len(owns)),
        depth,
        [jax.ShapeDtypeStruct((blocks, rows, depth), jnp.bfloat16)] * cores,
        grads,
        "turn",
        core,
    )


def rows_kernel(jobs, cores, at_ref, *refs):
    grads, attends, outs = refs[:cores], refs[cores : 2 * cores], refs[2 * cores :]
    clips, length, _ = attends[0].shape
    first = 0
    for (count, start, wide), out_ref in zip(jobs, outs):
        block = 256 if wide % 256 == 0 else 128
        for i in range(count):
            at = at_ref[first + i]
            for column in range(0, wide, block):
                columns = slice(start + column, start + column + block)
                chosen = [
                    attended[:, :, columns].reshape(clips * length, block) for attended in attends
                ]
                product = dot(
                    jnp.concatenate([grad[at] for grad in grads], axis=1),
                    jnp.concatenate(chosen, axis=0),
                    ((1,), (0,)),
                )
                out_ref[i, :, column : column + block] = product.astype(out_ref.dtype)
        first += count


def rows_products(jobs, grads, attends, dtype):
    rows = grads[0].shape[1]
    sizes = [(at.shape[0], start, wide) for at, start, wide in jobs]
    return whole_call(
        functools.partial(rows_kernel, sizes, len(grads)),
        grads[0].shape[2],
        [jax.ShapeDtypeStruct((count, rows, wide), dtype) for count, _, wide in sizes],
        [*grads, *attends],
        "rows",
        jnp.concatenate([at for at, _, _ in jobs]),
    )


def place(axis, by=0):
    return (lax.axis_index(axis) + by) % lax.axis_size(axis)


def block_at(zl, x, core):
    return ((zl * lax.axis_size("x") + x) * lax.axis_size("core") + core).astype(jnp.int32)


def shift_both(array, zl, x):
    zls, xs = lax.axis_size("zl"), lax.axis_size("x")
    pairs = [
        (i * xs + j, ((i + zl) % zls) * xs + (j + x) % xs) for i in range(zls) for j in range(xs)
    ]
    return lax.ppermute(array, ("zl", "x"), pairs)


def blocks_along(axis, by):
    zl, x = jnp.arange(lax.axis_size("zl")), jnp.arange(lax.axis_size("x"))
    if axis == "x":
        x = place("x", by)
    else:
        zl = place("zl", by)
    return (zl * lax.axis_size("x") + x).astype(jnp.int32)


def shards(grad_out, queries, keys, values, out_weight):
    seq = lax.axis_size("seq")
    mine = lax.axis_index("seq")
    tokens = grad_out.shape[1]
    rows, features = out_weight.shape
    length = tokens * seq
    heads = features // HEAD_DIM
    clips = math.prod(lax.axis_size(axis) for axis in DP)
    token_scale = 1.0 / math.sqrt(clips * length)

    def across(array):
        return [shift(array, "core", by) for by in others("core")]

    groups = 2 if heads % 4 == 0 else 1
    wide = features // groups
    larger = 2 * heads // 3
    widths = [count * HEAD_DIM for count in (larger, heads - larger) if count]
    orders = [("x", "zl"), ("zl", "x")][: len(widths)]

    def heads_of(by):
        return jnp.stack([part_of(part[0], "seq", by, 1) for part in (queries, keys, values)])

    pieces = [shift(heads_of(by), "seq", by) for by in others("seq")]
    far = pieces[0] if seq == 2 else jnp.concatenate(pieces, axis=1)
    own_grad = grad_out[0]
    halves = [shift(part_of(own_grad, "zh", by, 1), "zh", by) for by in others("zh")]
    near_x = [shift(out_weight, "x", by) for by in others("x")]
    near_zl = [shift(out_weight, "zl", by) for by in others("zl")]
    own_across = across(out_weight)

    own = heads_of(0)
    attended = forward(own, after(far, own_across))

    def along_seq(array):
        arrived = [shift(array, "seq", by) for by in others("seq")]
        return arrived[0] if seq == 2 else jnp.concatenate(arrived, axis=0)

    halves = after(halves, attended)
    attends = [shift(attended, "zh", by) for by in others("zh")]
    owns = [part_of(own_grad, "zh", 0, 1)] + halves
    fars = [along_seq(half) for half in owns]
    places = [(zl, x) for zl in others("zl") for x in others("x")]
    upper = rows // 2
    first = [[shift(block[:upper], "zl", by) for by in others("zl")] for block in near_x]
    last = [shift(block[upper:], "x", by) for block in near_zl for by in others("x")]
    diagonal = [(first[x - 1][zl - 1], low) for (zl, x), low in zip(places, last)]

    attends, fars[0] = lax.optimization_barrier((attends, fars[0]))
    pair = jnp.stack([attended] + attends)
    near_x, near_zl, diagonal, owns, fars, pair = lax.optimization_barrier(
        (near_x, near_zl, diagonal, owns, fars, pair)
    )
    diagonal = [jnp.concatenate(halves_of, axis=0) for halves_of in diagonal]
    x_across = [across(block) for block in near_x]
    zl_across = [across(block) for block in near_zl]
    diagonal_across = [across(block) for block in diagonal]
    attends = [pair] + across(pair)

    weights = [((0, 0), out_weight, own_across)]
    weights += [((0, by), *both_of) for by, *both_of in zip(others("x"), near_x, x_across)]
    weights += [((by, 0), *both_of) for by, *both_of in zip(others("zl"), near_zl, zl_across)]
    weights += zip(places, diagonal, diagonal_across)
    at, blocks = [], []
    for (zl, x), block, from_cores in weights:
        for core, array in enumerate([block] + from_cores):
            at.append(block_at(place("zl", -zl), place("x", -x), place("core", -core)))
            blocks.append(array)

    cores = lax.axis_size("core")
    core = place("core").astype(jnp.int32).reshape(1)
    by_rows = list(turned(core, owns, fars, rows, cores))
    by_rows = by_rows[:1] + [
        shift(array, "core", by) for by, array in zip(others("core"), by_rows[1:])
    ]

    at = jnp.stack(at)
    sent = [
        partial_product(at, own_part, far_part, blocks, groups, jnp.bfloat16)
        for own_part, far_part in zip(owns[1:], fars[1:])
    ]
    def returned(group, *events):
        parts = after([clip[group] for clip in sent], *events)
        return [shift(part, "zh", -by) for by, part in zip(others("zh"), parts)]

    terms = [returned(0)]

    by_rows[1:] = after(by_rows[1:], sent)
    starts = [sum(widths[:split]) for split in range(len(widths))]
    jobs = [
        (blocks_along(axis, by), start, size)
        for (axis, _), start, size in zip(orders, starts, widths)
        for by in others(axis)
    ]
    leave = rows_products(jobs, by_rows, attends, jnp.bfloat16)
    rest = iter(leave)
    arrive = [[shift(next(rest), axis, by) for by in others(axis)] for axis, _ in orders]
    owns, fars = after((owns, fars), leave)
    partial = partial_product(at, owns[0], fars[0], blocks, groups, jnp.float32)
    jobs = [
        (blocks_along(axis, 0), start, size)
        for (axis, _), start, size in zip(orders, starts, widths)
    ]
    kept = rows_products(jobs, after(by_rows, partial), attends, jnp.float32)
    for group in range(1, groups):
        terms.append(returned(group, terms[group - 1], kept))

    stays, arrivals = [], []
    for group in range(groups):
        start = group * wide
        staying, leaving = backward(own, far, partial[group], after(terms[group], kept), start)
        stays.append((mine * features + start, staying))
        for by in others("seq"):
            sent = leaving[:, (by - 1) * tokens : by * tokens]
            column = ((mine + by) % seq) * features + start
            arrivals.append((column, shift(sent, "seq", -by)))

    columns = []
    for (_, axis), arrived, total in zip(orders, after(arrive, [array for _, array in stays]), kept):
        for term in arrived:
            total = total + term.astype(jnp.float32)
        second = [
            shift(part_of(total, axis, by, 0).astype(jnp.bfloat16), axis, by)
            for by in others(axis)
        ]
        final = part_of(total, axis, 0, 0)
        for term in second:
            final = final + term.astype(jnp.float32)
        columns.append(final[0])
    weight_grad = jnp.concatenate(columns, axis=1) * token_scale

    result = jnp.zeros((3, tokens, queries.shape[2]), jnp.bfloat16)
    result = [result[0], result[1], result[2]]
    for column, arrays in stays + arrivals:
        result = [
            lax.dynamic_update_slice_in_dim(whole, array, column, 1)
            for whole, array in zip(result, arrays)
        ]
    return (result[0][None], result[1][None], result[2][None], weight_grad)


def solution(mesh):
    dp, seq = mesh.devices.shape
    finer = Mesh(mesh.devices.reshape(2, dp // 8, 2, 2, seq), DP + ("seq",))
    tokens = P(DP, "seq", None)
    return jax.shard_map(
        shards,
        mesh=finer,
        in_specs=(tokens, tokens, tokens, tokens, P(DP, "seq")),
        out_specs=(tokens, tokens, tokens, P(DP, "seq")),
        check_vma=False,
    )
```

```python
import functools
import math

import jax
import jax.numpy as jnp
from jax import lax
from jax.experimental import pallas as pl
from jax.experimental.pallas import tpu as pltpu
from jax.sharding import Mesh
from jax.sharding import PartitionSpec as P

HEAD_DIM = 128
INVERSE_ROOT = 1.0 / math.sqrt(HEAD_DIM)
DP = ("zh", "zl", "x", "core")


def dot(a, b, contract):
    return lax.dot_general(a, b, (contract, ((), ())), preferred_element_type=jnp.float32)


def shift(array, axis, by):
    count = lax.axis_size(axis)
    return lax.ppermute(array, axis, [(i, (i + by) % count) for i in range(count)])


def others(axis):
    return range(1, lax.axis_size(axis))


def part_of(array, axis, by, dim):
    count = lax.axis_size(axis)
    size = array.shape[dim] // count
    at = (lax.axis_index(axis) + by) % count
    return lax.dynamic_slice_in_dim(array, at * size, size, dim)


def softmax(q, k):
    scores = dot(q, k, ((1,), (1,))) * INVERSE_ROOT
    raised = jnp.exp(scores - jnp.max(scores, axis=-1, keepdims=True))
    return raised * (1.0 / jnp.sum(raised, axis=-1, keepdims=True))


def all_tokens(own, far, at):
    fars = (far[0][0, :, at], far[0][1, :, at], far[1][0, :, at])
    return (jnp.concatenate([own[i, :, at], arrived], axis=0) for i, arrived in enumerate(fars))


def forward_kernel(own, far_both, far_values, att_ref):
    far = (far_both, far_values)
    for start in range(0, att_ref.shape[1], HEAD_DIM):
        at = slice(start, start + HEAD_DIM)
        q, k, v = all_tokens(own, far, at)
        low = softmax(q, k).astype(jnp.bfloat16)
        att_ref[:, at] = dot(low, v, ((1,), (0,))).astype(jnp.bfloat16)


def backward_kernel(first, own, far_both, far_values, *refs):
    far = (far_both, far_values)
    *grad_refs, staying, leaving = refs
    tokens = own.shape[1]
    for start in range(0, staying.shape[2], HEAD_DIM):
        at = slice(start, start + HEAD_DIM)
        q, k, v = all_tokens(own, far, slice(first + start, first + start + HEAD_DIM))
        total = grad_refs[0][:, at].astype(jnp.float32)
        for ref in grad_refs[1:]:
            total = total + ref[:, at].astype(jnp.float32)
        g = total.astype(jnp.bfloat16)
        probs = softmax(q, k)
        low = probs.astype(jnp.bfloat16)
        att = dot(low, v, ((1,), (0,))).astype(jnp.bfloat16)
        delta = jnp.sum(
            g.astype(jnp.float32) * att.astype(jnp.float32), axis=-1, keepdims=True
        )
        d_probs = dot(g, v, ((1,), (1,)))
        d_low = (probs * (d_probs - delta)).astype(jnp.bfloat16)
        dq = (dot(d_low, k, ((1,), (0,))) * INVERSE_ROOT).astype(jnp.bfloat16)
        dk = (dot(d_low, q, ((0,), (0,))) * INVERSE_ROOT).astype(jnp.bfloat16)
        dv = dot(low, g, ((0,), (0,))).astype(jnp.bfloat16)
        for i, value in enumerate((dq, dk, dv)):
            staying[i, :, at] = value[:tokens]
            leaving[i, :, at] = value[tokens:]


def params(length):
    mebibytes = 32 if length <= 512 else 48
    return pltpu.CompilerParams(vmem_limit_bytes=mebibytes * 1024 * 1024)


def small():
    return pl.CostEstimate(flops=1024, bytes_accessed=1024, transcendentals=0)


def after(value, *events):
    return lax.optimization_barrier((value, events))[0]


def within(start, end):
    return lambda step, *_: (0, jnp.clip(step - start, 0, end - start - 1))


def whole_call(kernel, length, out_shape, operands, name, scalars=None, scratch_shapes=()):
    whole = pl.BlockSpec(memory_space=pltpu.VMEM)
    in_specs = [whole] * len(operands)
    if scalars is not None:
        operands = [scalars, *operands]
        in_specs = [pl.BlockSpec(memory_space=pltpu.SMEM)] + in_specs
    return pl.pallas_call(
        kernel,
        in_specs=in_specs,
        out_specs=jax.tree.map(lambda _: whole, out_shape),
        out_shape=out_shape,
        scratch_shapes=scratch_shapes,
        compiler_params=params(length),
        cost_estimate=small(),
        name=name,
    )(*operands)


def forward(own, far):
    _, tokens, features = own.shape
    length = tokens + far[0].shape[1]
    shape = jax.ShapeDtypeStruct((length, features), jnp.bfloat16)
    return whole_call(forward_kernel, length, shape, [own, *far], "forward")


def backward(own, far, partial, terms, first):
    tokens, rest = own.shape[1], far[0].shape[1]
    wide = partial.shape[1]
    return whole_call(
        functools.partial(backward_kernel, first),
        tokens + rest,
        [jax.ShapeDtypeStruct((3, count, wide), jnp.bfloat16) for count in (tokens, rest)],
        [own, *far, partial, *terms],
        "backward",
    )


def partial_kernel(count, which, at_ref, own, far, *refs):
    arrays, outs, every = refs[:count], refs[count:-1], refs[-1]
    tokens = own.shape[0]
    rows = every.shape[2]
    wide = outs[0].shape[1]
    block = 256 if wide % 256 == 0 else 128
    for i in range(len(which)):
        columns = slice(i * rows, (i + 1) * rows)
        every[i, :tokens] = own[:, columns]
        every[i, tokens:] = far[:, columns]
    for group, out_ref in enumerate(outs):
        for start in range(0, wide, block):
            columns = slice(group * wide + start, group * wide + start + block)
            grads = jnp.concatenate([every[at_ref[i]] for i in range(len(which))], axis=1)
            chosen = jnp.concatenate([arrays[j][i, :, columns] for j, i in which], axis=0)
            product = dot(grads, chosen, ((1,), (0,)))
            out_ref[:, start : start + block] = product.astype(out_ref.dtype)


def partial_product(at, own, far, weights, groups, dtype):
    length = own.shape[0] + far.shape[0]
    arrays = []
    for array, _ in weights:
        if all(array is not other for other in arrays):
            arrays.append(array)
    which = [
        (next(j for j, other in enumerate(arrays) if other is array), i) for array, i in weights
    ]
    rows, features = weights[0][0].shape[1:]
    return whole_call(
        functools.partial(partial_kernel, len(arrays), which),
        length,
        [jax.ShapeDtypeStruct((length, features // groups), dtype)] * groups,
        [own, far, *arrays],
        "partial",
        at,
        [pltpu.VMEM((len(which), length, rows), jnp.bfloat16)],
    )


def turn_kernel(clips, core_ref, *refs):
    grads, outs = refs[: 2 * clips], refs[2 * clips :]
    cores = len(outs)
    blocks, rows, _ = outs[0].shape
    for core in range(cores):

        @pl.when(core_ref[0] == core)
        def _():
            for by, out_ref in enumerate(outs):
                for i in range(blocks):
                    at = (i * cores + (core + by) % cores) * rows
                    start = 0
                    for grad in grads:
                        tokens = grad.shape[0]
                        out_ref[i, :, start : start + tokens] = grad[:, at : at + rows].T
                        start += tokens


def turned(core, owns, fars, rows, cores):
    grads = [grad for pair in zip(owns, fars) for grad in pair]
    depth = sum(grad.shape[0] for grad in grads)
    blocks = owns[0].shape[1] // (rows * cores)
    return whole_call(
        functools.partial(turn_kernel, len(owns)),
        depth,
        [jax.ShapeDtypeStruct((blocks, rows, depth), jnp.bfloat16)] * cores,
        grads,
        "turn",
        core,
    )


def rows_kernel(jobs, cores, at_ref, *refs):
    grads, attends, outs = refs[:cores], refs[cores : 2 * cores], refs[2 * cores :]
    clips, length, _ = attends[0].shape
    first = 0
    for (count, start, wide), out_ref in zip(jobs, outs):
        block = 256 if wide % 256 == 0 else 128
        for i in range(count):
            at = at_ref[first + i]
            for column in range(0, wide, block):
                columns = slice(start + column, start + column + block)
                chosen = [
                    attended[:, :, columns].reshape(clips * length, block) for attended in attends
                ]
                product = dot(
                    jnp.concatenate([grad[at] for grad in grads], axis=1),
                    jnp.concatenate(chosen, axis=0),
                    ((1,), (0,)),
                )
                out_ref[i, :, column : column + block] = product.astype(out_ref.dtype)
        first += count


def rows_products(jobs, grads, attends, dtype):
    rows = grads[0].shape[1]
    sizes = [(at.shape[0], start, wide) for at, start, wide in jobs]
    return whole_call(
        functools.partial(rows_kernel, sizes, len(grads)),
        grads[0].shape[2],
        [jax.ShapeDtypeStruct((count, rows, wide), dtype) for count, _, wide in sizes],
        [*grads, *attends],
        "rows",
        jnp.concatenate([at for at, _, _ in jobs]),
    )


def place(axis, by=0):
    return (lax.axis_index(axis) + by) % lax.axis_size(axis)


def block_at(zl, x, core):
    return ((zl * lax.axis_size("x") + x) * lax.axis_size("core") + core).astype(jnp.int32)


def shift_both(array, zl, x):
    zls, xs = lax.axis_size("zl"), lax.axis_size("x")
    pairs = [
        (i * xs + j, ((i + zl) % zls) * xs + (j + x) % xs) for i in range(zls) for j in range(xs)
    ]
    return lax.ppermute(array, ("zl", "x"), pairs)


def blocks_along(axis, by):
    zl, x = jnp.arange(lax.axis_size("zl")), jnp.arange(lax.axis_size("x"))
    if axis == "x":
        x = place("x", by)
    else:
        zl = place("zl", by)
    return (zl * lax.axis_size("x") + x).astype(jnp.int32)


def shards(grad_out, queries, keys, values, out_weight):
    seq = lax.axis_size("seq")
    mine = lax.axis_index("seq")
    tokens = grad_out.shape[1]
    rows, features = out_weight.shape
    length = tokens * seq
    heads = features // HEAD_DIM
    clips = math.prod(lax.axis_size(axis) for axis in DP)
    token_scale = 1.0 / math.sqrt(clips * length)

    def across(array):
        return [shift(array, "core", by) for by in others("core")]

    groups = 2 if heads % 4 == 0 else 1
    wide = features // groups
    larger = 2 * heads // 3
    widths = [count * HEAD_DIM for count in (larger, heads - larger) if count]
    orders = [("x", "zl"), ("zl", "x")][: len(widths)]

    def heads_of(by, *arrays):
        return jnp.stack([part_of(part[0], "seq", by, 1) for part in arrays])

    def far_heads(*arrays):
        pieces = [shift(heads_of(by, *arrays), "seq", by) for by in others("seq")]
        return pieces[0] if seq == 2 else jnp.concatenate(pieces, axis=1)

    far = [far_heads(queries, keys), far_heads(values)]
    own_grad = grad_out[0]
    halves = [shift(part_of(own_grad, "zh", by, 1), "zh", by) for by in others("zh")]
    near_x = [shift(out_weight, "x", by) for by in others("x")]
    near_zl = [shift(out_weight, "zl", by) for by in others("zl")]

    own = heads_of(0, queries, keys, values)
    attended = forward(own, far)

    def along_seq(array):
        arrived = [shift(array, "seq", by) for by in others("seq")]
        return arrived[0] if seq == 2 else jnp.concatenate(arrived, axis=0)

    halves = after(halves, attended)
    attends = [shift(attended, "zh", by) for by in others("zh")]
    owns = [part_of(own_grad, "zh", 0, 1)] + halves
    fars = [along_seq(half) for half in owns]

    places = [(zl, x) for zl in others("zl") for x in others("x")]
    upper = rows // 2
    first = [[shift(block[:upper], "zl", by) for by in others("zl")] for block in near_x]
    last = [shift(block[upper:], "x", by) for block in near_zl for by in others("x")]
    near = jnp.stack(near_x + near_zl)
    near_across = across(near)
    whole_weight = out_weight[None]
    cores = lax.axis_size("core")
    core = place("core").astype(jnp.int32).reshape(1)
    by_rows = by_rows_here = list(turned(core, owns, fars, rows, cores))
    by_rows = by_rows[:1] + [
        shift(array, "core", by) for by, array in zip(others("core"), by_rows[1:])
    ]

    pair = jnp.stack(after([attended] + attends, by_rows_here))
    attends = [pair] + across(pair)
    first, last = after((first, last), pair)
    diagonal = jnp.stack(
        [
            jnp.concatenate([first[x - 1][zl - 1], low], axis=0)
            for (zl, x), low in zip(places, last)
        ]
    )
    own_across, diagonal_across = across(whole_weight), across(diagonal)

    near_places = [(0, by) for by in others("x")] + [(by, 0) for by in others("zl")]
    weights = [((0, 0), [whole_weight] + own_across, 0)]
    weights += [(where, [near] + near_across, i) for i, where in enumerate(near_places)]
    weights += [(where, [diagonal] + diagonal_across, i) for i, where in enumerate(places)]
    at, blocks = [], []
    for (zl, x), arrays, i in weights:
        for core, array in enumerate(arrays):
            at.append(block_at(place("zl", -zl), place("x", -x), place("core", -core)))
            blocks.append((array, i))

    at = jnp.stack(at)
    sent = [
        partial_product(at, own_part, far_part, blocks, groups, jnp.bfloat16)
        for own_part, far_part in zip(owns[1:], fars[1:])
    ]
    def returned(group, *events):
        parts = after([clip[group] for clip in sent], *events)
        return [shift(part, "zh", -by) for by, part in zip(others("zh"), parts)]

    terms = [returned(0)]

    starts = [sum(widths[:split]) for split in range(len(widths))]
    jobs = [
        (blocks_along(axis, by), start, size)
        for (axis, _), start, size in zip(orders, starts, widths)
        for by in others(axis)
    ]
    leave = rows_products(jobs, by_rows, attends, jnp.bfloat16)
    rest = iter(leave)
    arrive = [[shift(next(rest), axis, by) for by in others(axis)] for axis, _ in orders]
    owns, fars = after((owns, fars), leave)
    partial = partial_product(at, owns[0], fars[0], blocks, groups, jnp.float32)
    jobs = [
        (blocks_along(axis, 0), start, size)
        for (axis, _), start, size in zip(orders, starts, widths)
    ]
    kept = rows_products(jobs, after(by_rows, partial), attends, jnp.float32)
    for group in range(1, groups):
        terms.append(returned(group, terms[group - 1], kept))

    stays, arrivals = [], []
    for group in range(groups):
        start = group * wide
        staying, leaving = backward(own, far, partial[group], after(terms[group], kept), start)
        stays.append((mine * features + start, staying))
        for by in others("seq"):
            sent = leaving[:, (by - 1) * tokens : by * tokens]
            column = ((mine + by) % seq) * features + start
            arrivals.append((column, shift(sent, "seq", -by)))

    columns = []
    for (_, axis), arrived, total in zip(orders, after(arrive, [array for _, array in stays]), kept):
        for term in arrived:
            total = total + term.astype(jnp.float32)
        second = [
            shift(part_of(total, axis, by, 0).astype(jnp.bfloat16), axis, by)
            for by in others(axis)
        ]
        final = part_of(total, axis, 0, 0)
        for term in second:
            final = final + term.astype(jnp.float32)
        columns.append(final[0])
    weight_grad = jnp.concatenate(columns, axis=1) * token_scale

    result = jnp.zeros((3, tokens, queries.shape[2]), jnp.bfloat16)
    result = [result[0], result[1], result[2]]
    for column, arrays in stays + arrivals:
        result = [
            lax.dynamic_update_slice_in_dim(whole, array, column, 1)
            for whole, array in zip(result, arrays)
        ]
    return (result[0][None], result[1][None], result[2][None], weight_grad)


def solution(mesh):
    dp, seq = mesh.devices.shape
    finer = Mesh(mesh.devices.reshape(2, dp // 8, 2, 2, seq), DP + ("seq",))
    tokens = P(DP, "seq", None)
    return jax.shard_map(
        shards,
        mesh=finer,
        in_specs=(tokens, tokens, tokens, tokens, P(DP, "seq")),
        out_specs=(tokens, tokens, tokens, P(DP, "seq")),
        check_vma=False,
    )
```

```python
import functools
import math

import jax
import jax.numpy as jnp
from jax import lax
from jax.experimental import pallas as pl
from jax.experimental.pallas import tpu as pltpu
from jax.sharding import Mesh
from jax.sharding import PartitionSpec as P

HEAD_DIM = 128
INVERSE_ROOT = 1.0 / math.sqrt(HEAD_DIM)
DP = ("zh", "zl", "x", "core")


def dot(a, b, contract):
    return lax.dot_general(a, b, (contract, ((), ())), preferred_element_type=jnp.float32)


def shift(array, axis, by):
    count = lax.axis_size(axis)
    return lax.ppermute(array, axis, [(i, (i + by) % count) for i in range(count)])


def others(axis):
    return range(1, lax.axis_size(axis))


def part_of(array, axis, by, dim):
    count = lax.axis_size(axis)
    size = array.shape[dim] // count
    at = (lax.axis_index(axis) + by) % count
    return lax.dynamic_slice_in_dim(array, at * size, size, dim)


def softmax(q, k):
    scores = dot(q, k, ((1,), (1,))) * INVERSE_ROOT
    raised = jnp.exp(scores - jnp.max(scores, axis=-1, keepdims=True))
    return raised * (1.0 / jnp.sum(raised, axis=-1, keepdims=True))


def all_tokens(own, far, at):
    fars = (far[0][0, :, at], far[0][1, :, at], far[1][0, :, at])
    return (jnp.concatenate([own[i, :, at], arrived], axis=0) for i, arrived in enumerate(fars))


def forward_kernel(own, far_both, far_values, att_ref):
    far = (far_both, far_values)
    for start in range(0, att_ref.shape[1], HEAD_DIM):
        at = slice(start, start + HEAD_DIM)
        q, k, v = all_tokens(own, far, at)
        low = softmax(q, k).astype(jnp.bfloat16)
        att_ref[:, at] = dot(low, v, ((1,), (0,))).astype(jnp.bfloat16)


def backward_kernel(first, own, far_both, far_values, *refs):
    far = (far_both, far_values)
    *grad_refs, staying, leaving = refs
    tokens = own.shape[1]
    for start in range(0, staying.shape[2], HEAD_DIM):
        at = slice(start, start + HEAD_DIM)
        q, k, v = all_tokens(own, far, slice(first + start, first + start + HEAD_DIM))
        total = grad_refs[0][:, at].astype(jnp.float32)
        for ref in grad_refs[1:]:
            total = total + ref[:, at].astype(jnp.float32)
        g = total.astype(jnp.bfloat16)
        probs = softmax(q, k)
        low = probs.astype(jnp.bfloat16)
        att = dot(low, v, ((1,), (0,))).astype(jnp.bfloat16)
        delta = jnp.sum(
            g.astype(jnp.float32) * att.astype(jnp.float32), axis=-1, keepdims=True
        )
        d_probs = dot(g, v, ((1,), (1,)))
        d_low = (probs * (d_probs - delta)).astype(jnp.bfloat16)
        dq = (dot(d_low, k, ((1,), (0,))) * INVERSE_ROOT).astype(jnp.bfloat16)
        dk = (dot(d_low, q, ((0,), (0,))) * INVERSE_ROOT).astype(jnp.bfloat16)
        dv = dot(low, g, ((0,), (0,))).astype(jnp.bfloat16)
        for i, value in enumerate((dq, dk, dv)):
            staying[i, :, at] = value[:tokens]
            leaving[i, :, at] = value[tokens:]


def params(length):
    mebibytes = 32 if length <= 512 else 48
    return pltpu.CompilerParams(vmem_limit_bytes=mebibytes * 1024 * 1024)


def small():
    return pl.CostEstimate(flops=1024, bytes_accessed=1024, transcendentals=0)


def after(value, *events):
    return lax.optimization_barrier((value, events))[0]


def within(start, end):
    return lambda step, *_: (0, jnp.clip(step - start, 0, end - start - 1))


def whole_call(kernel, length, out_shape, operands, name, scalars=None, scratch_shapes=()):
    whole = pl.BlockSpec(memory_space=pltpu.VMEM)
    in_specs = [whole] * len(operands)
    if scalars is not None:
        operands = [scalars, *operands]
        in_specs = [pl.BlockSpec(memory_space=pltpu.SMEM)] + in_specs
    return pl.pallas_call(
        kernel,
        in_specs=in_specs,
        out_specs=jax.tree.map(lambda _: whole, out_shape),
        out_shape=out_shape,
        scratch_shapes=scratch_shapes,
        compiler_params=params(length),
        cost_estimate=small(),
        name=name,
    )(*operands)


def forward(own, far):
    _, tokens, features = own.shape
    length = tokens + far[0].shape[1]
    shape = jax.ShapeDtypeStruct((length, features), jnp.bfloat16)
    return whole_call(forward_kernel, length, shape, [own, *far], "forward")


def backward(own, far, partial, terms, first):
    tokens, rest = own.shape[1], far[0].shape[1]
    wide = partial.shape[1]
    return whole_call(
        functools.partial(backward_kernel, first),
        tokens + rest,
        [jax.ShapeDtypeStruct((3, count, wide), jnp.bfloat16) for count in (tokens, rest)],
        [own, *far, partial, *terms],
        "backward",
    )


def partial_kernel(count, which, at_ref, own, far, *refs):
    arrays, outs, every = refs[:count], refs[count:-1], refs[-1]
    tokens = own.shape[0]
    rows = every.shape[2]
    wide = outs[0].shape[1]
    block = 256 if wide % 256 == 0 else 128
    for i in range(len(which)):
        columns = slice(i * rows, (i + 1) * rows)
        every[i, :tokens] = own[:, columns]
        every[i, tokens:] = far[:, columns]
    for group, out_ref in enumerate(outs):
        for start in range(0, wide, block):
            columns = slice(group * wide + start, group * wide + start + block)
            grads = jnp.concatenate([every[at_ref[i]] for i in range(len(which))], axis=1)
            chosen = jnp.concatenate([arrays[j][i, :, columns] for j, i in which], axis=0)
            product = dot(grads, chosen, ((1,), (0,)))
            out_ref[:, start : start + block] = product.astype(out_ref.dtype)


def partial_product(at, own, far, weights, groups, dtype):
    length = own.shape[0] + far.shape[0]
    arrays = []
    for array, _ in weights:
        if all(array is not other for other in arrays):
            arrays.append(array)
    which = [
        (next(j for j, other in enumerate(arrays) if other is array), i) for array, i in weights
    ]
    rows, features = weights[0][0].shape[1:]
    return whole_call(
        functools.partial(partial_kernel, len(arrays), which),
        length,
        [jax.ShapeDtypeStruct((length, features // groups), dtype)] * groups,
        [own, far, *arrays],
        "partial",
        at,
        [pltpu.VMEM((len(which), length, rows), jnp.bfloat16)],
    )


def turn_kernel(clips, core_ref, *refs):
    grads, outs = refs[: 2 * clips], refs[2 * clips :]
    cores = len(outs)
    blocks, rows, _ = outs[0].shape
    for core in range(cores):

        @pl.when(core_ref[0] == core)
        def _():
            for by, out_ref in enumerate(outs):
                for i in range(blocks):
                    at = (i * cores + (core + by) % cores) * rows
                    start = 0
                    for grad in grads:
                        tokens = grad.shape[0]
                        out_ref[i, :, start : start + tokens] = grad[:, at : at + rows].T
                        start += tokens


def turned(core, owns, fars, rows, cores):
    grads = [grad for pair in zip(owns, fars) for grad in pair]
    depth = sum(grad.shape[0] for grad in grads)
    blocks = owns[0].shape[1] // (rows * cores)
    return whole_call(
        functools.partial(turn_kernel, len(owns)),
        depth,
        [jax.ShapeDtypeStruct((blocks, rows, depth), jnp.bfloat16)] * cores,
        grads,
        "turn",
        core,
    )


def rows_kernel(jobs, cores, at_ref, *refs):
    grads, attends, outs = refs[:cores], refs[cores : 2 * cores], refs[2 * cores :]
    clips, length, _ = attends[0].shape
    first = 0
    for (count, start, wide), out_ref in zip(jobs, outs):
        block = 256 if wide % 256 == 0 else 128
        for i in range(count):
            at = at_ref[first + i]
            for column in range(0, wide, block):
                columns = slice(start + column, start + column + block)
                chosen = [
                    attended[:, :, columns].reshape(clips * length, block) for attended in attends
                ]
                product = dot(
                    jnp.concatenate([grad[at] for grad in grads], axis=1),
                    jnp.concatenate(chosen, axis=0),
                    ((1,), (0,)),
                )
                out_ref[i, :, column : column + block] = product.astype(out_ref.dtype)
        first += count


def rows_products(jobs, grads, attends, dtype):
    rows = grads[0].shape[1]
    sizes = [(at.shape[0], start, wide) for at, start, wide in jobs]
    return whole_call(
        functools.partial(rows_kernel, sizes, len(grads)),
        grads[0].shape[2],
        [jax.ShapeDtypeStruct((count, rows, wide), dtype) for count, _, wide in sizes],
        [*grads, *attends],
        "rows",
        jnp.concatenate([at for at, _, _ in jobs]),
    )


def place(axis, by=0):
    return (lax.axis_index(axis) + by) % lax.axis_size(axis)


def block_at(zl, x, core):
    return ((zl * lax.axis_size("x") + x) * lax.axis_size("core") + core).astype(jnp.int32)


def shift_both(array, zl, x):
    zls, xs = lax.axis_size("zl"), lax.axis_size("x")
    pairs = [
        (i * xs + j, ((i + zl) % zls) * xs + (j + x) % xs) for i in range(zls) for j in range(xs)
    ]
    return lax.ppermute(array, ("zl", "x"), pairs)


def blocks_along(axis, by):
    zl, x = jnp.arange(lax.axis_size("zl")), jnp.arange(lax.axis_size("x"))
    if axis == "x":
        x = place("x", by)
    else:
        zl = place("zl", by)
    return (zl * lax.axis_size("x") + x).astype(jnp.int32)


def shards(grad_out, queries, keys, values, out_weight):
    seq = lax.axis_size("seq")
    mine = lax.axis_index("seq")
    tokens = grad_out.shape[1]
    rows, features = out_weight.shape
    length = tokens * seq
    heads = features // HEAD_DIM
    clips = math.prod(lax.axis_size(axis) for axis in DP)
    token_scale = 1.0 / math.sqrt(clips * length)

    def across(array):
        return [shift(array, "core", by) for by in others("core")]

    groups = 2 if heads % 4 == 0 else 1
    wide = features // groups
    larger = 2 * heads // 3
    widths = [count * HEAD_DIM for count in (larger, heads - larger) if count]
    orders = [("x", "zl"), ("zl", "x")][: len(widths)]

    def heads_of(by, *arrays):
        return jnp.stack([part_of(part[0], "seq", by, 1) for part in arrays])

    def far_heads(*arrays):
        pieces = [shift(heads_of(by, *arrays), "seq", by) for by in others("seq")]
        return pieces[0] if seq == 2 else jnp.concatenate(pieces, axis=1)

    far = [far_heads(queries, keys), far_heads(values)]
    own_grad = grad_out[0]
    halves = [shift(part_of(own_grad, "zh", by, 1), "zh", by) for by in others("zh")]
    near_x = [shift(out_weight, "x", by) for by in others("x")]
    near_zl = [shift(out_weight, "zl", by) for by in others("zl")]

    own = heads_of(0, queries, keys, values)
    attended = forward(own, far)

    def along_seq(array):
        arrived = [shift(array, "seq", by) for by in others("seq")]
        return arrived[0] if seq == 2 else jnp.concatenate(arrived, axis=0)

    halves = after(halves, attended)
    attends = [shift(attended, "zh", by) for by in others("zh")]
    owns = [part_of(own_grad, "zh", 0, 1)] + halves
    fars = [along_seq(half) for half in owns]

    places = [(zl, x) for zl in others("zl") for x in others("x")]
    upper = rows // 2
    first = [[shift(block[:upper], "zl", by) for by in others("zl")] for block in near_x]
    last = [shift(block[upper:], "x", by) for block in near_zl for by in others("x")]
    near = jnp.stack(near_x + near_zl)
    near_across = across(near)
    whole_weight = out_weight[None]
    cores = lax.axis_size("core")
    core = place("core").astype(jnp.int32).reshape(1)
    by_rows = by_rows_here = list(turned(core, owns, fars, rows, cores))
    by_rows = by_rows[:1] + [
        shift(array, "core", by) for by, array in zip(others("core"), by_rows[1:])
    ]

    pair = jnp.stack(after([attended] + attends, by_rows_here))
    attends = [pair] + across(pair)
    first, last = after((first, last), pair)
    diagonal = jnp.stack(
        [
            jnp.concatenate([first[x - 1][zl - 1], low], axis=0)
            for (zl, x), low in zip(places, last)
        ]
    )
    own_across, diagonal_across = across(whole_weight), across(diagonal)

    near_places = [(0, by) for by in others("x")] + [(by, 0) for by in others("zl")]
    weights = [((0, 0), [whole_weight] + own_across, 0)]
    weights += [(where, [near] + near_across, i) for i, where in enumerate(near_places)]
    weights += [(where, [diagonal] + diagonal_across, i) for i, where in enumerate(places)]
    at, blocks = [], []
    for (zl, x), arrays, i in weights:
        for core, array in enumerate(arrays):
            at.append(block_at(place("zl", -zl), place("x", -x), place("core", -core)))
            blocks.append((array, i))

    at = jnp.stack(at)
    sent = [
        partial_product(at, own_part, far_part, blocks, groups, jnp.bfloat16)
        for own_part, far_part in zip(owns[1:], fars[1:])
    ]
    def returned(group, *events):
        parts = after([clip[group] for clip in sent], *events)
        return [shift(part, "zh", -by) for by, part in zip(others("zh"), parts)]

    terms = [returned(0)]

    starts = [sum(widths[:split]) for split in range(len(widths))]
    jobs = [
        (blocks_along(axis, by), start, size)
        for (axis, _), start, size in zip(orders, starts, widths)
        for by in others(axis)
    ]
    leave = rows_products(jobs, by_rows, attends, jnp.bfloat16)
    rest = iter(leave)
    arrive = [[shift(next(rest), axis, by) for by in others(axis)] for axis, _ in orders]
    owns, fars = after((owns, fars), leave)
    partial = partial_product(at, owns[0], fars[0], blocks, groups, jnp.float32)
    jobs = [
        (blocks_along(axis, 0), start, size)
        for (axis, _), start, size in zip(orders, starts, widths)
    ]
    kept = rows_products(jobs, after(by_rows, partial), attends, jnp.float32)
    for group in range(1, groups):
        terms.append(returned(group, terms[group - 1], kept))

    stays, arrivals = [], []
    second = []
    for group in range(groups):
        start = group * wide
        staying, leaving = backward(own, far, partial[group], after(terms[group], kept), start)
        stays.append((mine * features + start, staying))
        for by in others("seq"):
            sent = leaving[:, (by - 1) * tokens : by * tokens]
            column = ((mine + by) % seq) * features + start
            arrivals.append((column, shift(sent, "seq", -by)))
        if group == 0:
            for (_, axis), arrived, total in zip(orders, after(arrive, staying), kept):
                for term in arrived:
                    total = total + term.astype(jnp.float32)
                passed = [part_of(total, axis, by, 0).astype(jnp.bfloat16) for by in others(axis)]
                final = part_of(total, axis, 0, 0)
                second.append((final, passed))
            if groups > 1:
                terms[1] = after(terms[1], [passed for _, passed in second])

    columns = []
    for (_, axis), (final, passed) in zip(orders, second):
        for by, term in zip(others(axis), passed):
            final = final + shift(term, axis, by).astype(jnp.float32)
        columns.append(final[0])
    weight_grad = jnp.concatenate(columns, axis=1) * token_scale

    result = jnp.zeros((3, tokens, queries.shape[2]), jnp.bfloat16)
    result = [result[0], result[1], result[2]]
    for column, arrays in stays + arrivals:
        result = [
            lax.dynamic_update_slice_in_dim(whole, array, column, 1)
            for whole, array in zip(result, arrays)
        ]
    return (result[0][None], result[1][None], result[2][None], weight_grad)


def solution(mesh):
    dp, seq = mesh.devices.shape
    finer = Mesh(mesh.devices.reshape(2, dp // 8, 2, 2, seq), DP + ("seq",))
    tokens = P(DP, "seq", None)
    return jax.shard_map(
        shards,
        mesh=finer,
        in_specs=(tokens, tokens, tokens, tokens, P(DP, "seq")),
        out_specs=(tokens, tokens, tokens, P(DP, "seq")),
        check_vma=False,
    )
```

```python
import functools
import math

import jax
import jax.numpy as jnp
from jax import lax
from jax.experimental import pallas as pl
from jax.experimental.pallas import tpu as pltpu
from jax.sharding import Mesh
from jax.sharding import PartitionSpec as P

HEAD_DIM = 128
INVERSE_ROOT = 1.0 / math.sqrt(HEAD_DIM)
DP = ("zh", "zl", "x", "core")


def dot(a, b, contract):
    return lax.dot_general(a, b, (contract, ((), ())), preferred_element_type=jnp.float32)


def shift(array, axis, by):
    count = lax.axis_size(axis)
    return lax.ppermute(array, axis, [(i, (i + by) % count) for i in range(count)])


def others(axis):
    return range(1, lax.axis_size(axis))


def part_of(array, axis, by, dim):
    count = lax.axis_size(axis)
    size = array.shape[dim] // count
    at = (lax.axis_index(axis) + by) % count
    return lax.dynamic_slice_in_dim(array, at * size, size, dim)


def softmax(q, k):
    scores = dot(q, k, ((1,), (1,))) * INVERSE_ROOT
    raised = jnp.exp(scores - jnp.max(scores, axis=-1, keepdims=True))
    return raised * (1.0 / jnp.sum(raised, axis=-1, keepdims=True))


def all_tokens(own, far, at):
    fars = (far[0][0, :, at], far[0][1, :, at], far[1][0, :, at])
    return (jnp.concatenate([own[i, :, at], arrived], axis=0) for i, arrived in enumerate(fars))


def forward_kernel(own, far_both, far_values, att_ref):
    far = (far_both, far_values)
    for start in range(0, att_ref.shape[1], HEAD_DIM):
        at = slice(start, start + HEAD_DIM)
        q, k, v = all_tokens(own, far, at)
        low = softmax(q, k).astype(jnp.bfloat16)
        att_ref[:, at] = dot(low, v, ((1,), (0,))).astype(jnp.bfloat16)


def backward_kernel(first, own, far_both, far_values, *refs):
    far = (far_both, far_values)
    *grad_refs, staying, leaving = refs
    tokens = own.shape[1]
    for start in range(0, staying.shape[2], HEAD_DIM):
        at = slice(start, start + HEAD_DIM)
        q, k, v = all_tokens(own, far, slice(first + start, first + start + HEAD_DIM))
        total = grad_refs[0][:, at].astype(jnp.float32)
        for ref in grad_refs[1:]:
            total = total + ref[:, at].astype(jnp.float32)
        g = total.astype(jnp.bfloat16)
        probs = softmax(q, k)
        low = probs.astype(jnp.bfloat16)
        att = dot(low, v, ((1,), (0,))).astype(jnp.bfloat16)
        delta = jnp.sum(
            g.astype(jnp.float32) * att.astype(jnp.float32), axis=-1, keepdims=True
        )
        d_probs = dot(g, v, ((1,), (1,)))
        d_low = (probs * (d_probs - delta)).astype(jnp.bfloat16)
        dq = (dot(d_low, k, ((1,), (0,))) * INVERSE_ROOT).astype(jnp.bfloat16)
        dk = (dot(d_low, q, ((0,), (0,))) * INVERSE_ROOT).astype(jnp.bfloat16)
        dv = dot(low, g, ((0,), (0,))).astype(jnp.bfloat16)
        for i, value in enumerate((dq, dk, dv)):
            staying[i, :, at] = value[:tokens]
            leaving[i, :, at] = value[tokens:]


def params(length):
    mebibytes = 32 if length <= 512 else 48
    return pltpu.CompilerParams(vmem_limit_bytes=mebibytes * 1024 * 1024)


def small():
    return pl.CostEstimate(flops=1024, bytes_accessed=1024, transcendentals=0)


def after(value, *events):
    return lax.optimization_barrier((value, events))[0]


def within(start, end):
    return lambda step, *_: (0, jnp.clip(step - start, 0, end - start - 1))


def whole_call(kernel, length, out_shape, operands, name, scalars=None, scratch_shapes=()):
    whole = pl.BlockSpec(memory_space=pltpu.VMEM)
    in_specs = [whole] * len(operands)
    if scalars is not None:
        operands = [scalars, *operands]
        in_specs = [pl.BlockSpec(memory_space=pltpu.SMEM)] + in_specs
    return pl.pallas_call(
        kernel,
        in_specs=in_specs,
        out_specs=jax.tree.map(lambda _: whole, out_shape),
        out_shape=out_shape,
        scratch_shapes=scratch_shapes,
        compiler_params=params(length),
        cost_estimate=small(),
        name=name,
    )(*operands)


def forward(own, far):
    _, tokens, features = own.shape
    length = tokens + far[0].shape[1]
    shape = jax.ShapeDtypeStruct((length, features), jnp.bfloat16)
    return whole_call(forward_kernel, length, shape, [own, *far], "forward")


def backward(own, far, partial, terms, first):
    tokens, rest = own.shape[1], far[0].shape[1]
    wide = partial.shape[1]
    return whole_call(
        functools.partial(backward_kernel, first),
        tokens + rest,
        [jax.ShapeDtypeStruct((3, count, wide), jnp.bfloat16) for count in (tokens, rest)],
        [own, *far, partial, *terms],
        "backward",
    )


def partial_kernel(count, which, at_ref, own, far, *refs):
    arrays, outs, every = refs[:count], refs[count:-1], refs[-1]
    tokens = own.shape[0]
    rows = every.shape[2]
    wide = outs[0].shape[1]
    block = 256 if wide % 256 == 0 else 128
    for i in range(len(which)):
        columns = slice(i * rows, (i + 1) * rows)
        every[i, :tokens] = own[:, columns]
        every[i, tokens:] = far[:, columns]
    for group, out_ref in enumerate(outs):
        for start in range(0, wide, block):
            columns = slice(group * wide + start, group * wide + start + block)
            grads = jnp.concatenate([every[at_ref[i]] for i in range(len(which))], axis=1)
            chosen = jnp.concatenate([arrays[j][i, :, columns] for j, i in which], axis=0)
            product = dot(grads, chosen, ((1,), (0,)))
            out_ref[:, start : start + block] = product.astype(out_ref.dtype)


def partial_product(at, own, far, weights, groups, dtype):
    length = own.shape[0] + far.shape[0]
    arrays = []
    for array, _ in weights:
        if all(array is not other for other in arrays):
            arrays.append(array)
    which = [
        (next(j for j, other in enumerate(arrays) if other is array), i) for array, i in weights
    ]
    rows, features = weights[0][0].shape[1:]
    return whole_call(
        functools.partial(partial_kernel, len(arrays), which),
        length,
        [jax.ShapeDtypeStruct((length, features // groups), dtype)] * groups,
        [own, far, *arrays],
        "partial",
        at,
        [pltpu.VMEM((len(which), length, rows), jnp.bfloat16)],
    )


def turn_kernel(clips, core_ref, *refs):
    grads, outs = refs[: 2 * clips], refs[2 * clips :]
    cores = len(outs)
    blocks, rows, _ = outs[0].shape
    for core in range(cores):

        @pl.when(core_ref[0] == core)
        def _():
            for by, out_ref in enumerate(outs):
                for i in range(blocks):
                    at = (i * cores + (core + by) % cores) * rows
                    start = 0
                    for grad in grads:
                        tokens = grad.shape[0]
                        out_ref[i, :, start : start + tokens] = grad[:, at : at + rows].T
                        start += tokens


def turned(core, owns, fars, rows, cores):
    grads = [grad for pair in zip(owns, fars) for grad in pair]
    depth = sum(grad.shape[0] for grad in grads)
    blocks = owns[0].shape[1] // (rows * cores)
    return whole_call(
        functools.partial(turn_kernel, len(owns)),
        depth,
        [jax.ShapeDtypeStruct((blocks, rows, depth), jnp.bfloat16)] * cores,
        grads,
        "turn",
        core,
    )


def rows_kernel(jobs, cores, at_ref, *refs):
    grads, attends, outs = refs[:cores], refs[cores : 2 * cores], refs[2 * cores :]
    clips, length, _ = attends[0].shape
    first = 0
    for (count, start, wide), out_ref in zip(jobs, outs):
        block = 256 if wide % 256 == 0 else 128
        for i in range(count):
            at = at_ref[first + i]
            for column in range(0, wide, block):
                columns = slice(start + column, start + column + block)
                chosen = [
                    attended[:, :, columns].reshape(clips * length, block) for attended in attends
                ]
                product = dot(
                    jnp.concatenate([grad[at] for grad in grads], axis=1),
                    jnp.concatenate(chosen, axis=0),
                    ((1,), (0,)),
                )
                out_ref[i, :, column : column + block] = product.astype(out_ref.dtype)
        first += count


def rows_products(jobs, grads, attends, dtype):
    rows = grads[0].shape[1]
    sizes = [(at.shape[0], start, wide) for at, start, wide in jobs]
    return whole_call(
        functools.partial(rows_kernel, sizes, len(grads)),
        grads[0].shape[2],
        [jax.ShapeDtypeStruct((count, rows, wide), dtype) for count, _, wide in sizes],
        [*grads, *attends],
        "rows",
        jnp.concatenate([at for at, _, _ in jobs]),
    )


def place(axis, by=0):
    return (lax.axis_index(axis) + by) % lax.axis_size(axis)


def block_at(zl, x, core):
    return ((zl * lax.axis_size("x") + x) * lax.axis_size("core") + core).astype(jnp.int32)


def shift_both(array, zl, x):
    zls, xs = lax.axis_size("zl"), lax.axis_size("x")
    pairs = [
        (i * xs + j, ((i + zl) % zls) * xs + (j + x) % xs) for i in range(zls) for j in range(xs)
    ]
    return lax.ppermute(array, ("zl", "x"), pairs)


def blocks_along(axis, by):
    zl, x = jnp.arange(lax.axis_size("zl")), jnp.arange(lax.axis_size("x"))
    if axis == "x":
        x = place("x", by)
    else:
        zl = place("zl", by)
    return (zl * lax.axis_size("x") + x).astype(jnp.int32)


def shards(grad_out, queries, keys, values, out_weight):
    seq = lax.axis_size("seq")
    mine = lax.axis_index("seq")
    tokens = grad_out.shape[1]
    rows, features = out_weight.shape
    length = tokens * seq
    heads = features // HEAD_DIM
    clips = math.prod(lax.axis_size(axis) for axis in DP)
    token_scale = 1.0 / math.sqrt(clips * length)

    def across(array):
        return [shift(array, "core", by) for by in others("core")]

    groups = 2 if heads % 4 == 0 else 1
    wide = features // groups
    larger = 2 * heads // 3
    widths = [count * HEAD_DIM for count in (larger, heads - larger) if count]
    orders = [("x", "zl"), ("zl", "x")][: len(widths)]

    def heads_of(by, *arrays):
        return jnp.stack([part_of(part[0], "seq", by, 1) for part in arrays])

    def far_heads(*arrays):
        pieces = [shift(heads_of(by, *arrays), "seq", by) for by in others("seq")]
        return pieces[0] if seq == 2 else jnp.concatenate(pieces, axis=1)

    far = [far_heads(queries, keys), far_heads(values)]
    own_grad = grad_out[0]
    halves = [shift(part_of(own_grad, "zh", by, 1), "zh", by) for by in others("zh")]
    near_x = [shift(out_weight, "x", by) for by in others("x")]
    near_zl = [shift(out_weight, "zl", by) for by in others("zl")]

    own = heads_of(0, queries, keys, values)
    attended = forward(own, far)

    def along_seq(array):
        arrived = [shift(array, "seq", by) for by in others("seq")]
        return arrived[0] if seq == 2 else jnp.concatenate(arrived, axis=0)

    halves = after(halves, attended)
    attends = [shift(attended, "zh", by) for by in others("zh")]
    owns = [part_of(own_grad, "zh", 0, 1)] + halves
    fars = [along_seq(half) for half in owns]

    places = [(zl, x) for zl in others("zl") for x in others("x")]
    upper = rows // 2
    first = [[shift(block[:upper], "zl", by) for by in others("zl")] for block in near_x]
    last = [shift(block[upper:], "x", by) for block in near_zl for by in others("x")]
    near = jnp.stack(near_x + near_zl)
    near_across = across(near)
    whole_weight = out_weight[None]
    cores = lax.axis_size("core")
    core = place("core").astype(jnp.int32).reshape(1)
    by_rows = by_rows_here = list(turned(core, owns, fars, rows, cores))
    by_rows = by_rows[:1] + [
        shift(array, "core", by) for by, array in zip(others("core"), by_rows[1:])
    ]

    pair = jnp.stack(after([attended] + attends, by_rows_here, first, last))
    attends = [pair] + across(pair)
    first, last = after((first, last), pair)
    diagonal = jnp.stack(
        [
            jnp.concatenate([first[x - 1][zl - 1], low], axis=0)
            for (zl, x), low in zip(places, last)
        ]
    )
    own_across, diagonal_across = across(whole_weight), across(diagonal)

    near_places = [(0, by) for by in others("x")] + [(by, 0) for by in others("zl")]
    weights = [((0, 0), [whole_weight] + own_across, 0)]
    weights += [(where, [near] + near_across, i) for i, where in enumerate(near_places)]
    weights += [(where, [diagonal] + diagonal_across, i) for i, where in enumerate(places)]
    at, blocks = [], []
    for (zl, x), arrays, i in weights:
        for core, array in enumerate(arrays):
            at.append(block_at(place("zl", -zl), place("x", -x), place("core", -core)))
            blocks.append((array, i))

    at = jnp.stack(at)
    sent = [
        partial_product(at, own_part, far_part, blocks, groups, jnp.bfloat16)
        for own_part, far_part in zip(owns[1:], fars[1:])
    ]
    def returned(group, *events):
        parts = after([clip[group] for clip in sent], *events)
        return [shift(part, "zh", -by) for by, part in zip(others("zh"), parts)]

    terms = [returned(0)]

    starts = [sum(widths[:split]) for split in range(len(widths))]
    jobs = [
        (blocks_along(axis, by), start, size)
        for (axis, _), start, size in zip(orders, starts, widths)
        for by in others(axis)
    ]
    leave = rows_products(jobs, by_rows, attends, jnp.bfloat16)
    rest = iter(leave)
    arrive = [[shift(next(rest), axis, by) for by in others(axis)] for axis, _ in orders]
    owns, fars = after((owns, fars), leave)
    partial = partial_product(at, owns[0], fars[0], blocks, groups, jnp.float32)
    jobs = [
        (blocks_along(axis, 0), start, size)
        for (axis, _), start, size in zip(orders, starts, widths)
    ]
    kept = rows_products(jobs, after(by_rows, partial), attends, jnp.float32)
    for group in range(1, groups):
        terms.append(returned(group, terms[group - 1], kept))

    stays, arrivals = [], []
    second = []
    for group in range(groups):
        start = group * wide
        staying, leaving = backward(own, far, partial[group], after(terms[group], kept), start)
        stays.append((mine * features + start, staying))
        for by in others("seq"):
            sent = leaving[:, (by - 1) * tokens : by * tokens]
            column = ((mine + by) % seq) * features + start
            arrivals.append((column, shift(sent, "seq", -by)))
        if group == 0:
            for (_, axis), arrived, total in zip(orders, after(arrive, staying), kept):
                for term in arrived:
                    total = total + term.astype(jnp.float32)
                passed = [part_of(total, axis, by, 0).astype(jnp.bfloat16) for by in others(axis)]
                final = part_of(total, axis, 0, 0)
                second.append((final, passed))
            if groups > 1:
                terms[1] = after(terms[1], [passed for _, passed in second])

    columns = []
    for (_, axis), (final, passed) in zip(orders, second):
        for by, term in zip(others(axis), passed):
            final = final + shift(term, axis, by).astype(jnp.float32)
        columns.append(final[0])
    weight_grad = jnp.concatenate(columns, axis=1) * token_scale

    result = jnp.zeros((3, tokens, queries.shape[2]), jnp.bfloat16)
    result = [result[0], result[1], result[2]]
    for column, arrays in stays + arrivals:
        result = [
            lax.dynamic_update_slice_in_dim(whole, array, column, 1)
            for whole, array in zip(result, arrays)
        ]
    return (result[0][None], result[1][None], result[2][None], weight_grad)


def solution(mesh):
    dp, seq = mesh.devices.shape
    finer = Mesh(mesh.devices.reshape(2, dp // 8, 2, 2, seq), DP + ("seq",))
    tokens = P(DP, "seq", None)
    return jax.shard_map(
        shards,
        mesh=finer,
        in_specs=(tokens, tokens, tokens, tokens, P(DP, "seq")),
        out_specs=(tokens, tokens, tokens, P(DP, "seq")),
        check_vma=False,
    )
```

```python
import functools
import math

import jax
import jax.numpy as jnp
from jax import lax
from jax.experimental import pallas as pl
from jax.experimental.pallas import tpu as pltpu
from jax.sharding import Mesh
from jax.sharding import PartitionSpec as P

HEAD_DIM = 128
INVERSE_ROOT = 1.0 / math.sqrt(HEAD_DIM)
DP = ("zh", "zl", "x", "core")


def dot(a, b, contract):
    return lax.dot_general(a, b, (contract, ((), ())), preferred_element_type=jnp.float32)


def shift(array, axis, by):
    count = lax.axis_size(axis)
    return lax.ppermute(array, axis, [(i, (i + by) % count) for i in range(count)])


def others(axis):
    return range(1, lax.axis_size(axis))


def part_of(array, axis, by, dim):
    count = lax.axis_size(axis)
    size = array.shape[dim] // count
    at = (lax.axis_index(axis) + by) % count
    return lax.dynamic_slice_in_dim(array, at * size, size, dim)


def softmax(q, k):
    scores = dot(q, k, ((1,), (1,))) * INVERSE_ROOT
    raised = jnp.exp(scores - jnp.max(scores, axis=-1, keepdims=True))
    return raised * (1.0 / jnp.sum(raised, axis=-1, keepdims=True))


def all_tokens(own, far, at):
    fars = (far[0][0, :, at], far[0][1, :, at], far[1][0, :, at])
    return (jnp.concatenate([own[i, :, at], arrived], axis=0) for i, arrived in enumerate(fars))


def forward_kernel(own, far_both, far_values, att_ref):
    far = (far_both, far_values)
    for start in range(0, att_ref.shape[1], HEAD_DIM):
        at = slice(start, start + HEAD_DIM)
        q, k, v = all_tokens(own, far, at)
        low = softmax(q, k).astype(jnp.bfloat16)
        att_ref[:, at] = dot(low, v, ((1,), (0,))).astype(jnp.bfloat16)


def backward_kernel(first, own, far_both, far_values, *refs):
    far = (far_both, far_values)
    *grad_refs, staying, leaving = refs
    tokens = own.shape[1]
    for start in range(0, staying.shape[2], HEAD_DIM):
        at = slice(start, start + HEAD_DIM)
        q, k, v = all_tokens(own, far, slice(first + start, first + start + HEAD_DIM))
        total = grad_refs[0][:, at].astype(jnp.float32)
        for ref in grad_refs[1:]:
            total = total + ref[:, at].astype(jnp.float32)
        g = total.astype(jnp.bfloat16)
        probs = softmax(q, k)
        low = probs.astype(jnp.bfloat16)
        att = dot(low, v, ((1,), (0,))).astype(jnp.bfloat16)
        delta = jnp.sum(
            g.astype(jnp.float32) * att.astype(jnp.float32), axis=-1, keepdims=True
        )
        d_probs = dot(g, v, ((1,), (1,)))
        d_low = (probs * (d_probs - delta)).astype(jnp.bfloat16)
        dq = (dot(d_low, k, ((1,), (0,))) * INVERSE_ROOT).astype(jnp.bfloat16)
        dk = (dot(d_low, q, ((0,), (0,))) * INVERSE_ROOT).astype(jnp.bfloat16)
        dv = dot(low, g, ((0,), (0,))).astype(jnp.bfloat16)
        for i, value in enumerate((dq, dk, dv)):
            staying[i, :, at] = value[:tokens]
            leaving[i, :, at] = value[tokens:]


def params(length):
    mebibytes = 32 if length <= 512 else 48
    return pltpu.CompilerParams(vmem_limit_bytes=mebibytes * 1024 * 1024)


def small():
    return pl.CostEstimate(flops=1024, bytes_accessed=1024, transcendentals=0)


def after(value, *events):
    return lax.optimization_barrier((value, events))[0]


def within(start, end):
    return lambda step, *_: (0, jnp.clip(step - start, 0, end - start - 1))


def whole_call(kernel, length, out_shape, operands, name, scalars=None, scratch_shapes=()):
    whole = pl.BlockSpec(memory_space=pltpu.VMEM)
    in_specs = [whole] * len(operands)
    if scalars is not None:
        operands = [scalars, *operands]
        in_specs = [pl.BlockSpec(memory_space=pltpu.SMEM)] + in_specs
    return pl.pallas_call(
        kernel,
        in_specs=in_specs,
        out_specs=jax.tree.map(lambda _: whole, out_shape),
        out_shape=out_shape,
        scratch_shapes=scratch_shapes,
        compiler_params=params(length),
        cost_estimate=small(),
        name=name,
    )(*operands)


def forward(own, far):
    _, tokens, features = own.shape
    length = tokens + far[0].shape[1]
    shape = jax.ShapeDtypeStruct((length, features), jnp.bfloat16)
    return whole_call(forward_kernel, length, shape, [own, *far], "forward")


def backward(own, far, partial, terms, first):
    tokens, rest = own.shape[1], far[0].shape[1]
    wide = partial.shape[1]
    return whole_call(
        functools.partial(backward_kernel, first),
        tokens + rest,
        [jax.ShapeDtypeStruct((3, count, wide), jnp.bfloat16) for count in (tokens, rest)],
        [own, *far, partial, *terms],
        "backward",
    )


def partial_kernel(count, which, at_ref, own, far, *refs):
    arrays, outs, every = refs[:count], refs[count:-1], refs[-1]
    tokens = own.shape[0]
    rows = every.shape[2]
    wide = outs[0].shape[1]
    block = 256 if wide % 256 == 0 else 128
    for i in range(len(which)):
        columns = slice(i * rows, (i + 1) * rows)
        every[i, :tokens] = own[:, columns]
        every[i, tokens:] = far[:, columns]
    for group, out_ref in enumerate(outs):
        for start in range(0, wide, block):
            columns = slice(group * wide + start, group * wide + start + block)
            grads = jnp.concatenate([every[at_ref[i]] for i in range(len(which))], axis=1)
            chosen = jnp.concatenate([arrays[j][i, :, columns] for j, i in which], axis=0)
            product = dot(grads, chosen, ((1,), (0,)))
            out_ref[:, start : start + block] = product.astype(out_ref.dtype)


def partial_product(at, own, far, weights, groups, dtype):
    length = own.shape[0] + far.shape[0]
    arrays = []
    for array, _ in weights:
        if all(array is not other for other in arrays):
            arrays.append(array)
    which = [
        (next(j for j, other in enumerate(arrays) if other is array), i) for array, i in weights
    ]
    rows, features = weights[0][0].shape[1:]
    return whole_call(
        functools.partial(partial_kernel, len(arrays), which),
        length,
        [jax.ShapeDtypeStruct((length, features // groups), dtype)] * groups,
        [own, far, *arrays],
        "partial",
        at,
        [pltpu.VMEM((len(which), length, rows), jnp.bfloat16)],
    )


def turn_kernel(clips, core_ref, *refs):
    grads, outs = refs[: 2 * clips], refs[2 * clips :]
    cores = len(outs)
    blocks, rows, _ = outs[0].shape
    for core in range(cores):

        @pl.when(core_ref[0] == core)
        def _():
            for by, out_ref in enumerate(outs):
                for i in range(blocks):
                    at = (i * cores + (core + by) % cores) * rows
                    start = 0
                    for grad in grads:
                        tokens = grad.shape[0]
                        out_ref[i, :, start : start + tokens] = grad[:, at : at + rows].T
                        start += tokens


def turned(core, owns, fars, rows, cores):
    grads = [grad for pair in zip(owns, fars) for grad in pair]
    depth = sum(grad.shape[0] for grad in grads)
    blocks = owns[0].shape[1] // (rows * cores)
    return whole_call(
        functools.partial(turn_kernel, len(owns)),
        depth,
        [jax.ShapeDtypeStruct((blocks, rows, depth), jnp.bfloat16)] * cores,
        grads,
        "turn",
        core,
    )


def rows_kernel(jobs, cores, at_ref, *refs):
    grads, attends, outs = refs[:cores], refs[cores : 2 * cores], refs[2 * cores :]
    clips, length, _ = attends[0].shape
    first = 0
    for (count, start, wide), out_ref in zip(jobs, outs):
        block = 256 if wide % 256 == 0 else 128
        for i in range(count):
            at = at_ref[first + i]
            for column in range(0, wide, block):
                columns = slice(start + column, start + column + block)
                chosen = [
                    attended[:, :, columns].reshape(clips * length, block) for attended in attends
                ]
                product = dot(
                    jnp.concatenate([grad[at] for grad in grads], axis=1),
                    jnp.concatenate(chosen, axis=0),
                    ((1,), (0,)),
                )
                out_ref[i, :, column : column + block] = product.astype(out_ref.dtype)
        first += count


def rows_products(jobs, grads, attends, dtype):
    rows = grads[0].shape[1]
    sizes = [(at.shape[0], start, wide) for at, start, wide in jobs]
    return whole_call(
        functools.partial(rows_kernel, sizes, len(grads)),
        grads[0].shape[2],
        [jax.ShapeDtypeStruct((count, rows, wide), dtype) for count, _, wide in sizes],
        [*grads, *attends],
        "rows",
        jnp.concatenate([at for at, _, _ in jobs]),
    )


def place(axis, by=0):
    return (lax.axis_index(axis) + by) % lax.axis_size(axis)


def block_at(zl, x, core):
    return ((zl * lax.axis_size("x") + x) * lax.axis_size("core") + core).astype(jnp.int32)


def shift_both(array, zl, x):
    zls, xs = lax.axis_size("zl"), lax.axis_size("x")
    pairs = [
        (i * xs + j, ((i + zl) % zls) * xs + (j + x) % xs) for i in range(zls) for j in range(xs)
    ]
    return lax.ppermute(array, ("zl", "x"), pairs)


def blocks_along(axis, by):
    zl, x = jnp.arange(lax.axis_size("zl")), jnp.arange(lax.axis_size("x"))
    if axis == "x":
        x = place("x", by)
    else:
        zl = place("zl", by)
    return (zl * lax.axis_size("x") + x).astype(jnp.int32)


def shards(grad_out, queries, keys, values, out_weight):
    seq = lax.axis_size("seq")
    mine = lax.axis_index("seq")
    tokens = grad_out.shape[1]
    rows, features = out_weight.shape
    length = tokens * seq
    heads = features // HEAD_DIM
    clips = math.prod(lax.axis_size(axis) for axis in DP)
    token_scale = 1.0 / math.sqrt(clips * length)

    def across(array):
        return [shift(array, "core", by) for by in others("core")]

    groups = 3 if heads % 3 == 0 else 1
    wide = features // groups
    larger = 2 * heads // 3
    widths = [count * HEAD_DIM for count in (larger, heads - larger) if count]
    orders = [("x", "zl"), ("zl", "x")][: len(widths)]

    def heads_of(by, *arrays):
        return jnp.stack([part_of(part[0], "seq", by, 1) for part in arrays])

    def far_heads(*arrays):
        pieces = [shift(heads_of(by, *arrays), "seq", by) for by in others("seq")]
        return pieces[0] if seq == 2 else jnp.concatenate(pieces, axis=1)

    far = [far_heads(queries, keys), far_heads(values)]
    own_grad = grad_out[0]
    halves = [shift(part_of(own_grad, "zh", by, 1), "zh", by) for by in others("zh")]
    near_x = [shift(out_weight, "x", by) for by in others("x")]
    near_zl = [shift(out_weight, "zl", by) for by in others("zl")]

    own = heads_of(0, queries, keys, values)
    attended = forward(own, far)

    def along_seq(array):
        arrived = [shift(array, "seq", by) for by in others("seq")]
        return arrived[0] if seq == 2 else jnp.concatenate(arrived, axis=0)

    halves = after(halves, attended)
    attends = [shift(attended, "zh", by) for by in others("zh")]
    owns = [part_of(own_grad, "zh", 0, 1)] + halves
    fars = [along_seq(half) for half in owns]

    places = [(zl, x) for zl in others("zl") for x in others("x")]
    upper = rows // 2
    first = [[shift(block[:upper], "zl", by) for by in others("zl")] for block in near_x]
    last = [shift(block[upper:], "x", by) for block in near_zl for by in others("x")]
    near = jnp.stack(near_x + near_zl)
    near_across = across(near)
    whole_weight = out_weight[None]
    cores = lax.axis_size("core")
    core = place("core").astype(jnp.int32).reshape(1)
    by_rows = by_rows_here = list(turned(core, owns, fars, rows, cores))
    by_rows = by_rows[:1] + [
        shift(array, "core", by) for by, array in zip(others("core"), by_rows[1:])
    ]

    pair = jnp.stack(after([attended] + attends, by_rows_here, first, last))
    attends = [pair] + across(pair)
    first, last = after((first, last), pair)
    diagonal = jnp.stack(
        [
            jnp.concatenate([first[x - 1][zl - 1], low], axis=0)
            for (zl, x), low in zip(places, last)
        ]
    )
    own_across, diagonal_across = across(whole_weight), across(diagonal)

    near_places = [(0, by) for by in others("x")] + [(by, 0) for by in others("zl")]
    weights = [((0, 0), [whole_weight] + own_across, 0)]
    weights += [(where, [near] + near_across, i) for i, where in enumerate(near_places)]
    weights += [(where, [diagonal] + diagonal_across, i) for i, where in enumerate(places)]
    at, blocks = [], []
    for (zl, x), arrays, i in weights:
        for core, array in enumerate(arrays):
            at.append(block_at(place("zl", -zl), place("x", -x), place("core", -core)))
            blocks.append((array, i))

    at = jnp.stack(at)
    sent = [
        partial_product(at, own_part, far_part, blocks, groups, jnp.bfloat16)
        for own_part, far_part in zip(owns[1:], fars[1:])
    ]
    def returned(group, *events):
        parts = after([clip[group] for clip in sent], *events)
        return [shift(part, "zh", -by) for by, part in zip(others("zh"), parts)]

    terms = [returned(0)]

    starts = [sum(widths[:split]) for split in range(len(widths))]
    jobs = [
        (blocks_along(axis, by), start, size)
        for (axis, _), start, size in zip(orders, starts, widths)
        for by in others(axis)
    ]
    leave = rows_products(jobs, by_rows, attends, jnp.bfloat16)
    rest = iter(leave)
    arrive = [[shift(next(rest), axis, by) for by in others(axis)] for axis, _ in orders]
    owns, fars = after((owns, fars), leave)
    partial = partial_product(at, owns[0], fars[0], blocks, groups, jnp.float32)
    jobs = [
        (blocks_along(axis, 0), start, size)
        for (axis, _), start, size in zip(orders, starts, widths)
    ]
    kept = rows_products(jobs, after(by_rows, partial), attends, jnp.float32)
    for group in range(1, groups):
        terms.append(returned(group, terms[group - 1], kept))

    stays, arrivals = [], []
    second = []
    for group in range(groups):
        start = group * wide
        staying, leaving = backward(own, far, partial[group], after(terms[group], kept), start)
        stays.append((mine * features + start, staying))
        for by in others("seq"):
            sent = leaving[:, (by - 1) * tokens : by * tokens]
            column = ((mine + by) % seq) * features + start
            arrivals.append((column, shift(sent, "seq", -by)))
        if group == max(groups - 2, 0):
            for (_, axis), arrived, total in zip(orders, after(arrive, staying), kept):
                for term in arrived:
                    total = total + term.astype(jnp.float32)
                passed = [part_of(total, axis, by, 0).astype(jnp.bfloat16) for by in others(axis)]
                final = part_of(total, axis, 0, 0)
                second.append((final, passed))
            if groups > 1:
                terms[-1] = after(terms[-1], [passed for _, passed in second])

    columns = []
    for (_, axis), (final, passed) in zip(orders, second):
        for by, term in zip(others(axis), passed):
            final = final + shift(term, axis, by).astype(jnp.float32)
        columns.append(final[0])
    weight_grad = jnp.concatenate(columns, axis=1) * token_scale

    result = jnp.zeros((3, tokens, queries.shape[2]), jnp.bfloat16)
    result = [result[0], result[1], result[2]]
    for column, arrays in stays + arrivals:
        result = [
            lax.dynamic_update_slice_in_dim(whole, array, column, 1)
            for whole, array in zip(result, arrays)
        ]
    return (result[0][None], result[1][None], result[2][None], weight_grad)


def solution(mesh):
    dp, seq = mesh.devices.shape
    finer = Mesh(mesh.devices.reshape(2, dp // 8, 2, 2, seq), DP + ("seq",))
    tokens = P(DP, "seq", None)
    return jax.shard_map(
        shards,
        mesh=finer,
        in_specs=(tokens, tokens, tokens, tokens, P(DP, "seq")),
        out_specs=(tokens, tokens, tokens, P(DP, "seq")),
        check_vma=False,
    )
```

```python
import functools
import math

import jax
import jax.numpy as jnp
from jax import lax
from jax.experimental import pallas as pl
from jax.experimental.pallas import tpu as pltpu
from jax.sharding import Mesh
from jax.sharding import PartitionSpec as P

HEAD_DIM = 128
INVERSE_ROOT = 1.0 / math.sqrt(HEAD_DIM)
DP = ("zh", "zl", "x", "core")


def dot(a, b, contract):
    return lax.dot_general(a, b, (contract, ((), ())), preferred_element_type=jnp.float32)


def shift(array, axis, by):
    count = lax.axis_size(axis)
    return lax.ppermute(array, axis, [(i, (i + by) % count) for i in range(count)])


def others(axis):
    return range(1, lax.axis_size(axis))


def part_of(array, axis, by, dim):
    count = lax.axis_size(axis)
    size = array.shape[dim] // count
    at = (lax.axis_index(axis) + by) % count
    return lax.dynamic_slice_in_dim(array, at * size, size, dim)


def softmax(q, k):
    scores = dot(q, k, ((1,), (1,))) * INVERSE_ROOT
    raised = jnp.exp(scores - jnp.max(scores, axis=-1, keepdims=True))
    return raised * (1.0 / jnp.sum(raised, axis=-1, keepdims=True))


def all_tokens(own, far, at):
    fars = (far[0][0, :, at], far[0][1, :, at], far[1][0, :, at])
    return (jnp.concatenate([own[i, :, at], arrived], axis=0) for i, arrived in enumerate(fars))


def forward_kernel(own, far_both, far_values, att_ref):
    far = (far_both, far_values)
    for start in range(0, att_ref.shape[1], HEAD_DIM):
        at = slice(start, start + HEAD_DIM)
        q, k, v = all_tokens(own, far, at)
        low = softmax(q, k).astype(jnp.bfloat16)
        att_ref[:, at] = dot(low, v, ((1,), (0,))).astype(jnp.bfloat16)


def backward_kernel(first, own, far_both, far_values, *refs):
    far = (far_both, far_values)
    *grad_refs, staying, leaving = refs
    tokens = own.shape[1]
    for start in range(0, staying.shape[2], HEAD_DIM):
        at = slice(start, start + HEAD_DIM)
        q, k, v = all_tokens(own, far, slice(first + start, first + start + HEAD_DIM))
        total = grad_refs[0][:, at].astype(jnp.float32)
        for ref in grad_refs[1:]:
            total = total + ref[:, at].astype(jnp.float32)
        g = total.astype(jnp.bfloat16)
        probs = softmax(q, k)
        low = probs.astype(jnp.bfloat16)
        att = dot(low, v, ((1,), (0,))).astype(jnp.bfloat16)
        delta = jnp.sum(
            g.astype(jnp.float32) * att.astype(jnp.float32), axis=-1, keepdims=True
        )
        d_probs = dot(g, v, ((1,), (1,)))
        d_low = (probs * (d_probs - delta)).astype(jnp.bfloat16)
        dq = (dot(d_low, k, ((1,), (0,))) * INVERSE_ROOT).astype(jnp.bfloat16)
        dk = (dot(d_low, q, ((0,), (0,))) * INVERSE_ROOT).astype(jnp.bfloat16)
        dv = dot(low, g, ((0,), (0,))).astype(jnp.bfloat16)
        for i, value in enumerate((dq, dk, dv)):
            staying[i, :, at] = value[:tokens]
            leaving[i, :, at] = value[tokens:]


def params(length):
    mebibytes = 32 if length <= 512 else 48
    return pltpu.CompilerParams(vmem_limit_bytes=mebibytes * 1024 * 1024)


def small():
    return pl.CostEstimate(flops=1024, bytes_accessed=1024, transcendentals=0)


def after(value, *events):
    return lax.optimization_barrier((value, events))[0]


def within(start, end):
    return lambda step, *_: (0, jnp.clip(step - start, 0, end - start - 1))


def whole_call(kernel, length, out_shape, operands, name, scalars=None, scratch_shapes=()):
    whole = pl.BlockSpec(memory_space=pltpu.VMEM)
    in_specs = [whole] * len(operands)
    if scalars is not None:
        operands = [scalars, *operands]
        in_specs = [pl.BlockSpec(memory_space=pltpu.SMEM)] + in_specs
    return pl.pallas_call(
        kernel,
        in_specs=in_specs,
        out_specs=jax.tree.map(lambda _: whole, out_shape),
        out_shape=out_shape,
        scratch_shapes=scratch_shapes,
        compiler_params=params(length),
        cost_estimate=small(),
        name=name,
    )(*operands)


def forward(own, far):
    _, tokens, features = own.shape
    length = tokens + far[0].shape[1]
    shape = jax.ShapeDtypeStruct((length, features), jnp.bfloat16)
    return whole_call(forward_kernel, length, shape, [own, *far], "forward")


def backward(own, far, partial, terms, first):
    tokens, rest = own.shape[1], far[0].shape[1]
    wide = partial.shape[1]
    return whole_call(
        functools.partial(backward_kernel, first),
        tokens + rest,
        [jax.ShapeDtypeStruct((3, count, wide), jnp.bfloat16) for count in (tokens, rest)],
        [own, *far, partial, *terms],
        "backward",
    )


def partial_kernel(count, which, at_ref, own, far, *refs):
    arrays, outs, every = refs[:count], refs[count:-1], refs[-1]
    tokens = own.shape[0]
    rows = every.shape[2]
    wide = outs[0].shape[1]
    block = 256 if wide % 256 == 0 else 128
    for i in range(len(which)):
        columns = slice(i * rows, (i + 1) * rows)
        every[i, :tokens] = own[:, columns]
        every[i, tokens:] = far[:, columns]
    for group, out_ref in enumerate(outs):
        for start in range(0, wide, block):
            columns = slice(group * wide + start, group * wide + start + block)
            grads = jnp.concatenate([every[at_ref[i]] for i in range(len(which))], axis=1)
            chosen = jnp.concatenate([arrays[j][i, :, columns] for j, i in which], axis=0)
            product = dot(grads, chosen, ((1,), (0,)))
            out_ref[:, start : start + block] = product.astype(out_ref.dtype)


def partial_product(at, own, far, weights, groups, dtype):
    length = own.shape[0] + far.shape[0]
    arrays = []
    for array, _ in weights:
        if all(array is not other for other in arrays):
            arrays.append(array)
    which = [
        (next(j for j, other in enumerate(arrays) if other is array), i) for array, i in weights
    ]
    rows, features = weights[0][0].shape[1:]
    return whole_call(
        functools.partial(partial_kernel, len(arrays), which),
        length,
        [jax.ShapeDtypeStruct((length, features // groups), dtype)] * groups,
        [own, far, *arrays],
        "partial",
        at,
        [pltpu.VMEM((len(which), length, rows), jnp.bfloat16)],
    )


def turn_kernel(clips, core_ref, *refs):
    grads, outs = refs[: 2 * clips], refs[2 * clips :]
    cores = len(outs)
    blocks, rows, _ = outs[0].shape
    for core in range(cores):

        @pl.when(core_ref[0] == core)
        def _():
            for by, out_ref in enumerate(outs):
                for i in range(blocks):
                    at = (i * cores + (core + by) % cores) * rows
                    start = 0
                    for grad in grads:
                        tokens = grad.shape[0]
                        out_ref[i, :, start : start + tokens] = grad[:, at : at + rows].T
                        start += tokens


def turned(core, owns, fars, rows, cores):
    grads = [grad for pair in zip(owns, fars) for grad in pair]
    depth = sum(grad.shape[0] for grad in grads)
    blocks = owns[0].shape[1] // (rows * cores)
    return whole_call(
        functools.partial(turn_kernel, len(owns)),
        depth,
        [jax.ShapeDtypeStruct((blocks, rows, depth), jnp.bfloat16)] * cores,
        grads,
        "turn",
        core,
    )


def rows_kernel(jobs, cores, at_ref, *refs):
    grads, attends, outs = refs[:cores], refs[cores : 2 * cores], refs[2 * cores :]
    clips, length, _ = attends[0].shape
    first = 0
    for (count, start, wide), out_ref in zip(jobs, outs):
        block = 256 if wide % 256 == 0 else 128
        for i in range(count):
            at = at_ref[first + i]
            for column in range(0, wide, block):
                columns = slice(start + column, start + column + block)
                chosen = [
                    attended[:, :, columns].reshape(clips * length, block) for attended in attends
                ]
                product = dot(
                    jnp.concatenate([grad[at] for grad in grads], axis=1),
                    jnp.concatenate(chosen, axis=0),
                    ((1,), (0,)),
                )
                out_ref[i, :, column : column + block] = product.astype(out_ref.dtype)
        first += count


def rows_products(jobs, grads, attends, dtype):
    rows = grads[0].shape[1]
    sizes = [(at.shape[0], start, wide) for at, start, wide in jobs]
    return whole_call(
        functools.partial(rows_kernel, sizes, len(grads)),
        grads[0].shape[2],
        [jax.ShapeDtypeStruct((count, rows, wide), dtype) for count, _, wide in sizes],
        [*grads, *attends],
        "rows",
        jnp.concatenate([at for at, _, _ in jobs]),
    )


def place(axis, by=0):
    return (lax.axis_index(axis) + by) % lax.axis_size(axis)


def block_at(zl, x, core):
    return ((zl * lax.axis_size("x") + x) * lax.axis_size("core") + core).astype(jnp.int32)


def shift_both(array, zl, x):
    zls, xs = lax.axis_size("zl"), lax.axis_size("x")
    pairs = [
        (i * xs + j, ((i + zl) % zls) * xs + (j + x) % xs) for i in range(zls) for j in range(xs)
    ]
    return lax.ppermute(array, ("zl", "x"), pairs)


def blocks_along(axis, by):
    zl, x = jnp.arange(lax.axis_size("zl")), jnp.arange(lax.axis_size("x"))
    if axis == "x":
        x = place("x", by)
    else:
        zl = place("zl", by)
    return (zl * lax.axis_size("x") + x).astype(jnp.int32)


def shards(grad_out, queries, keys, values, out_weight):
    seq = lax.axis_size("seq")
    mine = lax.axis_index("seq")
    tokens = grad_out.shape[1]
    rows, features = out_weight.shape
    length = tokens * seq
    heads = features // HEAD_DIM
    clips = math.prod(lax.axis_size(axis) for axis in DP)
    token_scale = 1.0 / math.sqrt(clips * length)

    def across(array):
        return [shift(array, "core", by) for by in others("core")]

    groups = 3 if heads % 3 == 0 else 1
    wide = features // groups
    larger = 2 * heads // 3
    widths = [count * HEAD_DIM for count in (larger, heads - larger) if count]
    orders = [("x", "zl"), ("zl", "x")][: len(widths)]

    def heads_of(by, *arrays):
        return jnp.stack([part_of(part[0], "seq", by, 1) for part in arrays])

    def far_heads(*arrays):
        pieces = [shift(heads_of(by, *arrays), "seq", by) for by in others("seq")]
        return pieces[0] if seq == 2 else jnp.concatenate(pieces, axis=1)

    far = [far_heads(queries, keys), far_heads(values)]
    own_grad = grad_out[0]
    halves = [shift(part_of(own_grad, "zh", by, 1), "zh", by) for by in others("zh")]
    near_x = [shift(out_weight, "x", by) for by in others("x")]
    near_zl = [shift(out_weight, "zl", by) for by in others("zl")]

    own = heads_of(0, queries, keys, values)
    attended = forward(own, far)

    def along_seq(array):
        arrived = [shift(array, "seq", by) for by in others("seq")]
        return arrived[0] if seq == 2 else jnp.concatenate(arrived, axis=0)

    halves = after(halves, attended)
    attends = [shift(attended, "zh", by) for by in others("zh")]
    owns = [part_of(own_grad, "zh", 0, 1)] + halves
    fars = [along_seq(half) for half in owns]

    places = [(zl, x) for zl in others("zl") for x in others("x")]
    upper = rows // 2
    first = [[shift(block[:upper], "zl", by) for by in others("zl")] for block in near_x]
    last = [shift(block[upper:], "x", by) for block in near_zl for by in others("x")]
    near = jnp.stack(near_x + near_zl)
    near_across = across(near)
    whole_weight = out_weight[None]
    cores = lax.axis_size("core")
    core = place("core").astype(jnp.int32).reshape(1)
    by_rows = by_rows_here = list(turned(core, owns, fars, rows, cores))
    by_rows = by_rows[:1] + [
        shift(array, "core", by) for by, array in zip(others("core"), by_rows[1:])
    ]

    pair = jnp.stack(after([attended] + attends, by_rows_here, first, last))
    attends = [pair] + across(pair)
    first, last = after((first, last), pair)
    diagonal = jnp.stack(
        [
            jnp.concatenate([first[x - 1][zl - 1], low], axis=0)
            for (zl, x), low in zip(places, last)
        ]
    )
    own_across, diagonal_across = across(whole_weight), across(diagonal)

    near_places = [(0, by) for by in others("x")] + [(by, 0) for by in others("zl")]
    weights = [((0, 0), [whole_weight] + own_across, 0)]
    weights += [(where, [near] + near_across, i) for i, where in enumerate(near_places)]
    weights += [(where, [diagonal] + diagonal_across, i) for i, where in enumerate(places)]
    at, blocks = [], []
    for (zl, x), arrays, i in weights:
        for core, array in enumerate(arrays):
            at.append(block_at(place("zl", -zl), place("x", -x), place("core", -core)))
            blocks.append((array, i))

    at = jnp.stack(at)
    sent = [
        partial_product(at, own_part, far_part, blocks, groups, jnp.bfloat16)
        for own_part, far_part in zip(owns[1:], fars[1:])
    ]
    def returned(group, *events):
        parts = after([clip[group] for clip in sent], *events)
        return [shift(part, "zh", -by) for by, part in zip(others("zh"), parts)]

    terms = [returned(0)]

    starts = [sum(widths[:split]) for split in range(len(widths))]
    jobs = [
        (blocks_along(axis, by), start, size)
        for (axis, _), start, size in zip(orders, starts, widths)
        for by in others(axis)
    ]
    leave = rows_products(jobs, by_rows, attends, jnp.bfloat16)
    rest = iter(leave)
    arrive = [[shift(next(rest), axis, by) for by in others(axis)] for axis, _ in orders]
    owns, fars = after((owns, fars), leave)
    partial = partial_product(at, owns[0], fars[0], blocks, groups, jnp.float32)
    jobs = [
        (blocks_along(axis, 0), start, size)
        for (axis, _), start, size in zip(orders, starts, widths)
    ]
    kept = rows_products(jobs, after(by_rows, partial), attends, jnp.float32)
    for group in range(1, groups):
        terms.append(returned(group, terms[group - 1], partial))

    stays, arrivals = [], []
    second = []
    for group in range(groups):
        start = group * wide
        staying, leaving = backward(own, far, partial[group], after(terms[group], kept), start)
        stays.append((mine * features + start, staying))
        for by in others("seq"):
            sent = leaving[:, (by - 1) * tokens : by * tokens]
            column = ((mine + by) % seq) * features + start
            arrivals.append((column, shift(sent, "seq", -by)))
        last = len(orders) if group == groups - 1 else group + 1
        for split in range(len(second), min(last, len(orders))):
            axis = orders[split][1]
            arrived, total = after(arrive[split], staying), kept[split]
            for term in arrived:
                total = total + term.astype(jnp.float32)
            passed = [part_of(total, axis, by, 0).astype(jnp.bfloat16) for by in others(axis)]
            second.append((part_of(total, axis, 0, 0), passed))
            if group + 1 < groups:
                terms[group + 1] = after(terms[group + 1], passed)
        if group > 0 and group + 1 < groups:
            terms[group + 1] = after(terms[group + 1], [array for _, array in arrivals])

    columns = []
    for (_, axis), (final, passed) in zip(orders, second):
        for by, term in zip(others(axis), passed):
            final = final + shift(term, axis, by).astype(jnp.float32)
        columns.append(final[0])
    weight_grad = jnp.concatenate(columns, axis=1) * token_scale

    result = jnp.zeros((3, tokens, queries.shape[2]), jnp.bfloat16)
    result = [result[0], result[1], result[2]]
    for column, arrays in stays + arrivals:
        result = [
            lax.dynamic_update_slice_in_dim(whole, array, column, 1)
            for whole, array in zip(result, arrays)
        ]
    return (result[0][None], result[1][None], result[2][None], weight_grad)


def solution(mesh):
    dp, seq = mesh.devices.shape
    finer = Mesh(mesh.devices.reshape(2, dp // 8, 2, 2, seq), DP + ("seq",))
    tokens = P(DP, "seq", None)
    return jax.shard_map(
        shards,
        mesh=finer,
        in_specs=(tokens, tokens, tokens, tokens, P(DP, "seq")),
        out_specs=(tokens, tokens, tokens, P(DP, "seq")),
        check_vma=False,
    )
```

```python
import functools
import math

import jax
import jax.numpy as jnp
from jax import lax
from jax.experimental import pallas as pl
from jax.experimental.pallas import tpu as pltpu
from jax.sharding import Mesh
from jax.sharding import PartitionSpec as P

HEAD_DIM = 128
INVERSE_ROOT = 1.0 / math.sqrt(HEAD_DIM)
DP = ("zh", "zl", "x", "core")


def dot(a, b, contract):
    return lax.dot_general(a, b, (contract, ((), ())), preferred_element_type=jnp.float32)


def shift(array, axis, by):
    count = lax.axis_size(axis)
    return lax.ppermute(array, axis, [(i, (i + by) % count) for i in range(count)])


def others(axis):
    return range(1, lax.axis_size(axis))


def part_of(array, axis, by, dim):
    count = lax.axis_size(axis)
    size = array.shape[dim] // count
    at = (lax.axis_index(axis) + by) % count
    return lax.dynamic_slice_in_dim(array, at * size, size, dim)


def softmax(q, k):
    scores = dot(q, k, ((1,), (1,))) * INVERSE_ROOT
    raised = jnp.exp(scores - jnp.max(scores, axis=-1, keepdims=True))
    return raised * (1.0 / jnp.sum(raised, axis=-1, keepdims=True))


def all_tokens(own, far, at):
    fars = (far[0][0, :, at], far[0][1, :, at], far[1][0, :, at])
    return (jnp.concatenate([own[i, :, at], arrived], axis=0) for i, arrived in enumerate(fars))


def forward_kernel(own, far_both, far_values, att_ref):
    far = (far_both, far_values)
    for start in range(0, att_ref.shape[1], HEAD_DIM):
        at = slice(start, start + HEAD_DIM)
        q, k, v = all_tokens(own, far, at)
        low = softmax(q, k).astype(jnp.bfloat16)
        att_ref[:, at] = dot(low, v, ((1,), (0,))).astype(jnp.bfloat16)


def backward_kernel(first, own, far_both, far_values, *refs):
    far = (far_both, far_values)
    *grad_refs, staying, leaving = refs
    tokens = own.shape[1]
    for start in range(0, staying.shape[2], HEAD_DIM):
        at = slice(start, start + HEAD_DIM)
        q, k, v = all_tokens(own, far, slice(first + start, first + start + HEAD_DIM))
        total = grad_refs[0][:, at].astype(jnp.float32)
        for ref in grad_refs[1:]:
            total = total + ref[:, at].astype(jnp.float32)
        g = total.astype(jnp.bfloat16)
        probs = softmax(q, k)
        low = probs.astype(jnp.bfloat16)
        att = dot(low, v, ((1,), (0,))).astype(jnp.bfloat16)
        delta = jnp.sum(
            g.astype(jnp.float32) * att.astype(jnp.float32), axis=-1, keepdims=True
        )
        d_probs = dot(g, v, ((1,), (1,)))
        d_low = (probs * (d_probs - delta)).astype(jnp.bfloat16)
        dq = (dot(d_low, k, ((1,), (0,))) * INVERSE_ROOT).astype(jnp.bfloat16)
        dk = (dot(d_low, q, ((0,), (0,))) * INVERSE_ROOT).astype(jnp.bfloat16)
        dv = dot(low, g, ((0,), (0,))).astype(jnp.bfloat16)
        for i, value in enumerate((dq, dk, dv)):
            staying[i, :, at] = value[:tokens]
            leaving[i, :, at] = value[tokens:]


def params(length):
    mebibytes = 16 if length <= 512 else 48
    return pltpu.CompilerParams(vmem_limit_bytes=mebibytes * 1024 * 1024)


def small():
    return pl.CostEstimate(flops=1024, bytes_accessed=1024, transcendentals=0)


def after(value, *events):
    return lax.optimization_barrier((value, events))[0]


def within(start, end):
    return lambda step, *_: (0, jnp.clip(step - start, 0, end - start - 1))


def whole_call(kernel, length, out_shape, operands, name, scalars=None, scratch_shapes=()):
    whole = pl.BlockSpec(memory_space=pltpu.VMEM)
    in_specs = [whole] * len(operands)
    if scalars is not None:
        operands = [scalars, *operands]
        in_specs = [pl.BlockSpec(memory_space=pltpu.SMEM)] + in_specs
    return pl.pallas_call(
        kernel,
        in_specs=in_specs,
        out_specs=jax.tree.map(lambda _: whole, out_shape),
        out_shape=out_shape,
        scratch_shapes=scratch_shapes,
        compiler_params=params(length),
        cost_estimate=small(),
        name=name,
    )(*operands)


def forward(own, far):
    _, tokens, features = own.shape
    length = tokens + far[0].shape[1]
    shape = jax.ShapeDtypeStruct((length, features), jnp.bfloat16)
    return whole_call(forward_kernel, length, shape, [own, *far], "forward")


def backward(own, far, partial, terms, first):
    tokens, rest = own.shape[1], far[0].shape[1]
    wide = partial.shape[1]
    return whole_call(
        functools.partial(backward_kernel, first),
        tokens + rest,
        [jax.ShapeDtypeStruct((3, count, wide), jnp.bfloat16) for count in (tokens, rest)],
        [own, *far, partial, *terms],
        "backward",
    )


def partial_kernel(count, which, at_ref, own, far, *refs):
    arrays, outs, every = refs[:count], refs[count:-1], refs[-1]
    tokens = own.shape[0]
    rows = every.shape[2]
    wide = outs[0].shape[1]
    block = 256 if wide % 256 == 0 else 128
    for i in range(len(which)):
        columns = slice(i * rows, (i + 1) * rows)
        every[i, :tokens] = own[:, columns]
        every[i, tokens:] = far[:, columns]
    for group, out_ref in enumerate(outs):
        for start in range(0, wide, block):
            columns = slice(group * wide + start, group * wide + start + block)
            grads = jnp.concatenate([every[at_ref[i]] for i in range(len(which))], axis=1)
            chosen = jnp.concatenate([arrays[j][i, :, columns] for j, i in which], axis=0)
            product = dot(grads, chosen, ((1,), (0,)))
            out_ref[:, start : start + block] = product.astype(out_ref.dtype)


def partial_product(at, own, far, weights, groups, dtype):
    length = own.shape[0] + far.shape[0]
    arrays = []
    for array, _ in weights:
        if all(array is not other for other in arrays):
            arrays.append(array)
    which = [
        (next(j for j, other in enumerate(arrays) if other is array), i) for array, i in weights
    ]
    rows, features = weights[0][0].shape[1:]
    return whole_call(
        functools.partial(partial_kernel, len(arrays), which),
        length,
        [jax.ShapeDtypeStruct((length, features // groups), dtype)] * groups,
        [own, far, *arrays],
        "partial",
        at,
        [pltpu.VMEM((len(which), length, rows), jnp.bfloat16)],
    )


def turn_kernel(clips, core_ref, *refs):
    grads, outs = refs[: 2 * clips], refs[2 * clips :]
    cores = len(outs)
    blocks, rows, _ = outs[0].shape
    for core in range(cores):

        @pl.when(core_ref[0] == core)
        def _():
            for by, out_ref in enumerate(outs):
                for i in range(blocks):
                    at = (i * cores + (core + by) % cores) * rows
                    start = 0
                    for grad in grads:
                        tokens = grad.shape[0]
                        out_ref[i, :, start : start + tokens] = grad[:, at : at + rows].T
                        start += tokens


def turned(core, owns, fars, rows, cores):
    grads = [grad for pair in zip(owns, fars) for grad in pair]
    depth = sum(grad.shape[0] for grad in grads)
    blocks = owns[0].shape[1] // (rows * cores)
    return whole_call(
        functools.partial(turn_kernel, len(owns)),
        depth,
        [jax.ShapeDtypeStruct((blocks, rows, depth), jnp.bfloat16)] * cores,
        grads,
        "turn",
        core,
    )


def rows_kernel(jobs, cores, at_ref, *refs):
    grads, attends, outs = refs[:cores], refs[cores : 2 * cores], refs[2 * cores :]
    clips, length, _ = attends[0].shape
    first = 0
    for (count, start, wide), out_ref in zip(jobs, outs):
        block = 256 if wide % 256 == 0 else 128
        for i in range(count):
            at = at_ref[first + i]
            for column in range(0, wide, block):
                columns = slice(start + column, start + column + block)
                chosen = [
                    attended[:, :, columns].reshape(clips * length, block) for attended in attends
                ]
                product = dot(
                    jnp.concatenate([grad[at] for grad in grads], axis=1),
                    jnp.concatenate(chosen, axis=0),
                    ((1,), (0,)),
                )
                out_ref[i, :, column : column + block] = product.astype(out_ref.dtype)
        first += count


def rows_products(jobs, grads, attends, dtype):
    rows = grads[0].shape[1]
    sizes = [(at.shape[0], start, wide) for at, start, wide in jobs]
    return whole_call(
        functools.partial(rows_kernel, sizes, len(grads)),
        grads[0].shape[2],
        [jax.ShapeDtypeStruct((count, rows, wide), dtype) for count, _, wide in sizes],
        [*grads, *attends],
        "rows",
        jnp.concatenate([at for at, _, _ in jobs]),
    )


def place(axis, by=0):
    return (lax.axis_index(axis) + by) % lax.axis_size(axis)


def block_at(zl, x, core):
    return ((zl * lax.axis_size("x") + x) * lax.axis_size("core") + core).astype(jnp.int32)


def shift_both(array, zl, x):
    zls, xs = lax.axis_size("zl"), lax.axis_size("x")
    pairs = [
        (i * xs + j, ((i + zl) % zls) * xs + (j + x) % xs) for i in range(zls) for j in range(xs)
    ]
    return lax.ppermute(array, ("zl", "x"), pairs)


def blocks_along(axis, by):
    zl, x = jnp.arange(lax.axis_size("zl")), jnp.arange(lax.axis_size("x"))
    if axis == "x":
        x = place("x", by)
    else:
        zl = place("zl", by)
    return (zl * lax.axis_size("x") + x).astype(jnp.int32)


def shards(grad_out, queries, keys, values, out_weight):
    seq = lax.axis_size("seq")
    mine = lax.axis_index("seq")
    tokens = grad_out.shape[1]
    rows, features = out_weight.shape
    length = tokens * seq
    heads = features // HEAD_DIM
    clips = math.prod(lax.axis_size(axis) for axis in DP)
    token_scale = 1.0 / math.sqrt(clips * length)

    def across(array):
        return [shift(array, "core", by) for by in others("core")]

    groups = 3 if heads % 3 == 0 else 1
    wide = features // groups
    larger = 2 * heads // 3
    widths = [count * HEAD_DIM for count in (larger, heads - larger) if count]
    orders = [("x", "zl"), ("zl", "x")][: len(widths)]

    def heads_of(by, *arrays):
        return jnp.stack([part_of(part[0], "seq", by, 1) for part in arrays])

    def far_heads(*arrays):
        pieces = [shift(heads_of(by, *arrays), "seq", by) for by in others("seq")]
        return pieces[0] if seq == 2 else jnp.concatenate(pieces, axis=1)

    far = [far_heads(queries, keys), far_heads(values)]
    own_grad = grad_out[0]
    halves = [shift(part_of(own_grad, "zh", by, 1), "zh", by) for by in others("zh")]
    near_x = [shift(out_weight, "x", by) for by in others("x")]
    near_zl = [shift(out_weight, "zl", by) for by in others("zl")]

    own = heads_of(0, queries, keys, values)
    attended = forward(own, far)

    def along_seq(array):
        arrived = [shift(array, "seq", by) for by in others("seq")]
        return arrived[0] if seq == 2 else jnp.concatenate(arrived, axis=0)

    halves = after(halves, attended)
    attends = [shift(attended, "zh", by) for by in others("zh")]
    owns = [part_of(own_grad, "zh", 0, 1)] + halves
    fars = [along_seq(half) for half in owns]

    places = [(zl, x) for zl in others("zl") for x in others("x")]
    upper = rows // 2
    first = [[shift(block[:upper], "zl", by) for by in others("zl")] for block in near_x]
    last = [shift(block[upper:], "x", by) for block in near_zl for by in others("x")]
    near = jnp.stack(near_x + near_zl)
    near_across = across(near)
    whole_weight = out_weight[None]
    cores = lax.axis_size("core")
    core = place("core").astype(jnp.int32).reshape(1)
    by_rows = by_rows_here = list(turned(core, owns, fars, rows, cores))
    by_rows = by_rows[:1] + [
        shift(array, "core", by) for by, array in zip(others("core"), by_rows[1:])
    ]

    pair = jnp.stack(after([attended] + attends, by_rows_here, first, last))
    attends = [pair] + across(pair)
    first, last = after((first, last), pair)
    diagonal = jnp.stack(
        [
            jnp.concatenate([first[x - 1][zl - 1], low], axis=0)
            for (zl, x), low in zip(places, last)
        ]
    )
    own_across, diagonal_across = across(whole_weight), across(diagonal)

    near_places = [(0, by) for by in others("x")] + [(by, 0) for by in others("zl")]
    weights = [((0, 0), [whole_weight] + own_across, 0)]
    weights += [(where, [near] + near_across, i) for i, where in enumerate(near_places)]
    weights += [(where, [diagonal] + diagonal_across, i) for i, where in enumerate(places)]
    at, blocks = [], []
    for (zl, x), arrays, i in weights:
        for core, array in enumerate(arrays):
            at.append(block_at(place("zl", -zl), place("x", -x), place("core", -core)))
            blocks.append((array, i))

    at = jnp.stack(at)
    sent = [
        partial_product(at, own_part, far_part, blocks, groups, jnp.bfloat16)
        for own_part, far_part in zip(owns[1:], fars[1:])
    ]
    def returned(group, *events):
        parts = after([clip[group] for clip in sent], *events)
        return [shift(part, "zh", -by) for by, part in zip(others("zh"), parts)]

    terms = [returned(0)]

    starts = [sum(widths[:split]) for split in range(len(widths))]
    jobs = [
        (blocks_along(axis, by), start, size)
        for (axis, _), start, size in zip(orders, starts, widths)
        for by in others(axis)
    ]
    leave = rows_products(jobs, by_rows, attends, jnp.bfloat16)
    rest = iter(leave)
    arrive = [[shift(next(rest), axis, by) for by in others(axis)] for axis, _ in orders]
    owns, fars = after((owns, fars), leave)
    partial = partial_product(at, owns[0], fars[0], blocks, groups, jnp.float32)
    jobs = [
        (blocks_along(axis, 0), start, size)
        for (axis, _), start, size in zip(orders, starts, widths)
    ]
    kept = rows_products(jobs, after(by_rows, partial), attends, jnp.float32)
    for group in range(1, groups):
        terms.append(returned(group, terms[group - 1], partial))

    stays, arrivals = [], []
    second = []
    for group in range(groups):
        start = group * wide
        staying, leaving = backward(own, far, partial[group], after(terms[group], kept), start)
        stays.append((mine * features + start, staying))
        for by in others("seq"):
            sent = leaving[:, (by - 1) * tokens : by * tokens]
            column = ((mine + by) % seq) * features + start
            arrivals.append((column, shift(sent, "seq", -by)))
        last = len(orders) if group == groups - 1 else group + 1
        for split in range(len(second), min(last, len(orders))):
            axis = orders[split][1]
            arrived, total = after(arrive[split], staying), kept[split]
            for term in arrived:
                total = total + term.astype(jnp.float32)
            passed = [part_of(total, axis, by, 0).astype(jnp.bfloat16) for by in others(axis)]
            second.append((part_of(total, axis, 0, 0), passed))
            if group + 1 < groups:
                terms[group + 1] = after(terms[group + 1], passed)
        if group > 0 and group + 1 < groups:
            terms[group + 1] = after(terms[group + 1], [array for _, array in arrivals])

    columns = []
    for (_, axis), (final, passed) in zip(orders, second):
        for by, term in zip(others(axis), passed):
            final = final + shift(term, axis, by).astype(jnp.float32)
        columns.append(final[0])
    weight_grad = jnp.concatenate(columns, axis=1) * token_scale

    result = jnp.zeros((3, tokens, queries.shape[2]), jnp.bfloat16)
    result = [result[0], result[1], result[2]]
    for column, arrays in stays + arrivals:
        result = [
            lax.dynamic_update_slice_in_dim(whole, array, column, 1)
            for whole, array in zip(result, arrays)
        ]
    return (result[0][None], result[1][None], result[2][None], weight_grad)


def solution(mesh):
    dp, seq = mesh.devices.shape
    finer = Mesh(mesh.devices.reshape(2, dp // 8, 2, 2, seq), DP + ("seq",))
    tokens = P(DP, "seq", None)
    return jax.shard_map(
        shards,
        mesh=finer,
        in_specs=(tokens, tokens, tokens, tokens, P(DP, "seq")),
        out_specs=(tokens, tokens, tokens, P(DP, "seq")),
        check_vma=False,
    )
```
